32 devices in a mesh: tm: 4 (over y, core), clip: 8 (over z, x).
Axes of the slice: x: 2, y: 2, z: 4, core: 2. Of those that a mesh axis runs over, the one named last changes fastest.
Arguments:
- tokens: bfloat16 [16, 8, 256, 1024], P('tm', 'clip'), may hold values from -6 to 6
- actions: int32 [16, 8], P('tm', 'clip'), may hold values from 0 to 7
- sides: int32 [8], P('clip'), may hold values from 8 to 16, as said below
- action_table: bfloat16 [8, 1024], P(None, ('tm', 'clip')), may hold values from -5 to 5
- norm_gains: bfloat16 [3, 1024], P(None, ('tm', 'clip')), may hold values from 0.099609375 to 1.8984375
- norm_shifts: bfloat16 [3, 1024], P(None, ('tm', 'clip')), may hold values from -1.5 to 1.5
- s_qkv: bfloat16 [1024, 3072], P(('tm', 'clip')), may hold values from -0.1875 to 0.1875
- s_out: bfloat16 [1024, 1024], P(('tm', 'clip')), may hold values from -0.75 to 0.75
- t_qkv: bfloat16 [1024, 3072], P(('tm', 'clip')), may hold values from -0.1875 to 0.1875
- t_out: bfloat16 [1024, 1024], P(('tm', 'clip')), may hold values from -0.375 to 0.375
- w_up: bfloat16 [1024, 4096], P(('tm', 'clip')), may hold values from -0.1875 to 0.1875
- b_up: bfloat16 [4096], P(('tm', 'clip')), may hold values from -2.5 to 2.5
- w_down: bfloat16 [4096, 1024], P(('tm', 'clip')), may hold values from -0.09375 to 0.09375
- b_down: bfloat16 [1024], P(('tm', 'clip')), may hold values from -1.5 to 1.5
- grad_out: bfloat16 [16, 8, 256, 1024], P('tm', 'clip'), may hold values from -6 to 6
Outputs:
- mixed: bfloat16 [16, 8, 256, 1024], P('tm', 'clip')
- input_grad: float32 [16, 8, 256, 1024], P('tm', 'clip')
- grad_actions: float32 [8, 1024], P(None, ('tm', 'clip'))
- grad_gains: float32 [3, 1024], P(None, ('tm', 'clip'))
- grad_shifts: float32 [3, 1024], P(None, ('tm', 'clip'))
- grad_s_qkv: float32 [1024, 3072], P(('tm', 'clip'))
- grad_s_out: float32 [1024, 1024], P(('tm', 'clip'))
- grad_t_qkv: float32 [1024, 3072], P(('tm', 'clip'))
- grad_t_out: float32 [1024, 1024], P(('tm', 'clip'))
- grad_w_up: float32 [1024, 4096], P(('tm', 'clip'))
- grad_b_up: float32 [4096], P(('tm', 'clip'))
- grad_w_down: float32 [4096, 1024], P(('tm', 'clip'))
- grad_b_down: float32 [1024], P(('tm', 'clip'))
The draws below stay inside these ranges and needn't reach their ends.
Inputs may be any that keep to these rules, and one draw needn't show every extreme that they name: `sides`: each clip's frames are grids of 16 x 16 or of half that side; a smaller grid uses the first slots of each frame. Exactly 2 clips have the smaller side.
All inputs are finite; a program needn't handle non-finite values.
Results may differ from the reference program's by a relative error of at most 0.013.
Values may be sent and summed in bfloat16 or wider, within the bound.
No kernel may reach another device: no remote copies, remote signals or barrier semaphores. Data moves between devices by JAX's collectives and lax.ppermute only.
A program may use at most 448 MiB of HBM per device.

```python
import math
import jax
import jax.numpy as jnp
from jax import lax

D = 1024
FF = 4096
H = 16
E = 64
ACTIONS = 8
GRID = 16
FRAMES = 16
P_SIZE = 256
CLIPS = 8


def draw_sides(key, part):
    key = jax.random.fold_in(key, 7)
    order = jax.random.permutation(key, CLIPS)
    return jnp.where(order < CLIPS // 4, GRID // 2, GRID).astype(jnp.int32)


def with_ends(result, rng, least, top_value):
    shape = result.shape
    index_at = [jax.random.randint(jax.random.fold_in(rng, axis), (), 0, shape[axis]) for axis in range(len(shape))]
    result = result.at[tuple(index_at)].set(least)
    longest = shape.index(max(shape))
    index_at[longest] = (index_at[longest] + 1) % shape[longest]
    return result.at[tuple(index_at)].set(top_value)


def levels(rng, extent, pieces, least, high):
    loudness, own = 1.0, jax.random.fold_in(rng, 6)
    for dim, parts in pieces:
        steps = jnp.exp(jax.random.uniform(jax.random.fold_in(own, dim), (parts,), jnp.float32, least / len(pieces), high / len(pieces)))
        loudness = loudness * jnp.repeat(steps, extent[dim] // parts).reshape([-1 if axis == dim else 1 for axis in range(len(extent))])
    return loudness


def centred(key, extent, deviation, bound, cuts=(), kind=jnp.bfloat16):
    entries = jax.random.normal(key, extent, jnp.float32) * deviation
    if len(cuts) > 0:
        entries = levels(key, extent, cuts, -0.22, 0.18) * entries
    return jnp.clip(entries, min=-bound, max=bound).astype(kind)


def setup_inputs(seed: int = 0) -> dict:
    streams_of = jax.random.split(jax.random.key(seed), 16)
    return {
        "tokens": centred(streams_of[0], (FRAMES, CLIPS, P_SIZE, D), 1.0, 6.0, ((0, 4), (1, 8))),
        "actions": with_ends(jax.random.randint(streams_of[1], (FRAMES, CLIPS), 0, ACTIONS), jax.random.fold_in(streams_of[1], 1), 0, ACTIONS - 1).astype(jnp.int32),
        "sides": draw_sides(jax.random.fold_in(streams_of[15], 71), 0),
        "action_table": centred(streams_of[3], (ACTIONS, D), 1.0, 5.0, ((1, 32),)),
        "norm_gains": jnp.clip(1.0 + 0.18 * jax.random.normal(streams_of[4], (3, D), jnp.float32), 0.099609375, 1.8984375).astype(jnp.bfloat16),
        "norm_shifts": centred(streams_of[5], (3, D), 0.3, 1.5, ((1, 32),)),
        "s_qkv": centred(streams_of[6], (D, 3 * D), D ** -0.5, 0.1875, ((0, 32),)),
        "s_out": centred(streams_of[7], (D, D), (D // 16) ** -0.5, 0.75, ((0, 32),)),
        "t_qkv": centred(streams_of[8], (D, 3 * D), D ** -0.5, 0.1875, ((0, 32),)),
        "t_out": centred(streams_of[9], (D, D), (D // 4) ** -0.5, 0.375, ((0, 32),)),
        "w_up": centred(streams_of[10], (D, FF), D ** -0.5, 0.1875, ((0, 32),)),
        "b_up": centred(streams_of[11], (FF,), 0.5, 2.5, ((0, 32),)),
        "w_down": centred(streams_of[12], (FF, D), FF ** -0.5, 0.09375, ((0, 32),)),
        "b_down": centred(streams_of[13], (D,), 0.3, 1.5, ((0, 32),)),
        "grad_out": centred(streams_of[14], (FRAMES, CLIPS, P_SIZE, D), 1.0, 6.0, ((0, 4), (1, 8))),
    }


@jax.custom_vjp
def low(v):
    return lax.optimization_barrier(v.astype(jnp.bfloat16)).astype(jnp.float32)

@jax.custom_vjp
def low_back(v):
    return v

def low_keep(v):
    return (low(v), None)

def low_pass(kept, grad):
    return (grad,)

def back_keep(v):
    return (v, None)

def back_low(kept, grad):
    return (low(grad),)
low.defvjp(low_keep, low_pass)
low_back.defvjp(back_keep, back_low)
highest = lax.Precision.HIGHEST
negative = -1e+30

def layer_norm(inputs, gain, shift):
    average = lax.optimization_barrier(jnp.mean(inputs, axis=-1, keepdims=True))
    centered = inputs - average
    variance = lax.optimization_barrier(jnp.mean(centered * centered, axis=-1, keepdims=True))
    return centered * lax.rsqrt(variance + 1e-05) * gain + shift

def matrix(inputs, weight):
    return jnp.dot(inputs, weight, precision=highest, preferred_element_type=jnp.float32)

def clip_forward(params, clip_tokens, clip_actions, clip_side):
    action_rows, gain_rows, shift_rows, sq_full, so_full, tq_full, to_full, up_full, upb_full, down_full, downb_full = params
    row_count = FRAMES * P_SIZE
    factor = 1.0 / math.sqrt(E)
    onehot = (clip_actions[:, None] == jnp.arange(ACTIONS)[None, :]).astype(jnp.float32)
    hidden0 = clip_tokens + matrix(onehot, action_rows)[:, None, :]
    visible = jnp.arange(P_SIZE) < clip_side * clip_side
    normed = low(layer_norm(hidden0, gain_rows[0], shift_rows[0])).reshape(row_count, D)
    packed = low_back(low(matrix(normed, sq_full))).reshape(FRAMES, P_SIZE, 3, H, E)
    scores = low_back(jnp.einsum('fphe,fqhe->fhpq', packed[:, :, 0], packed[:, :, 1], precision=highest) * factor)
    scores = jnp.where(visible[None, None, None, :], scores, negative)
    probs = jax.nn.softmax(scores, axis=-1)
    attended = jnp.einsum('fhpq,fqhe->fphe', low(probs), packed[:, :, 2], precision=highest)
    attended = low_back(low(attended)).reshape(row_count, D)
    hidden1 = hidden0 + low_back(matrix(attended, so_full)).reshape(FRAMES, P_SIZE, D)
    normed = low(layer_norm(hidden1, gain_rows[1], shift_rows[1])).reshape(row_count, D)
    packed = low_back(low(matrix(normed, tq_full))).reshape(FRAMES, P_SIZE, 3, H, E)
    scores = jnp.einsum('fphe,gphe->phfg', packed[:, :, 0], packed[:, :, 1], precision=highest) * factor
    causal = jnp.arange(FRAMES)[:, None] >= jnp.arange(FRAMES)[None, :]
    scores = jnp.where(causal, scores, negative)
    probs = jax.nn.softmax(scores, axis=-1)
    attended = low(jnp.einsum('phfg,gphe->fphe', probs, packed[:, :, 2], precision=highest)).reshape(row_count, D)
    hidden2 = hidden1 + low_back(matrix(attended, to_full)).reshape(FRAMES, P_SIZE, D)
    normed = low(layer_norm(hidden2, gain_rows[2], shift_rows[2])).reshape(row_count, D)
    inner = low_back(matrix(normed, up_full) + upb_full)
    active = low(jax.nn.gelu(inner, approximate=False))
    hidden3 = hidden2 + low_back(matrix(active, down_full) + downb_full).reshape(FRAMES, P_SIZE, D)
    return hidden3 * visible[None, :, None].astype(jnp.float32)

def reference(tokens, actions, sides, action_table, norm_gains, norm_shifts, s_qkv, s_out, t_qkv, t_out, w_up, b_up, w_down, b_down, grad_out):
    params = tuple((array_in.astype(jnp.float32) for array_in in (action_table, norm_gains, norm_shifts, s_qkv, s_out, t_qkv, t_out, w_up, b_up, w_down, b_down)))
    clip_inputs = jnp.moveaxis(tokens.astype(jnp.float32), 1, 0)
    clip_actions = jnp.moveaxis(actions, 1, 0)
    per_clip = jax.checkpoint(clip_forward)

    def forward(inputs, weights):
        return lax.map(lambda bundle: per_clip(weights, bundle[0], bundle[1], bundle[2]), (inputs, clip_actions, sides))
    outputs, pullback = jax.vjp(forward, clip_inputs, params)
    input_grad, grads = pullback(jnp.moveaxis(grad_out.astype(jnp.float32), 1, 0))
    mixed = jnp.moveaxis(outputs, 0, 1).astype(jnp.bfloat16)
    return (mixed, jnp.moveaxis(input_grad, 0, 1), grads[0], grads[1], grads[2], grads[3], grads[4], grads[5], grads[6], grads[7], grads[8], grads[9], grads[10])
```

```python
from functools import partial

import jax
import jax.numpy as jnp
from jax import lax
from jax.experimental import pallas as pl
from jax.experimental.pallas import tpu as pltpu
from jax.sharding import PartitionSpec as P

H = 16
E = 64
ACTIONS = 8
FRAMES = 16
AXES = ("tm", "clip")
LANES = 128
GROUP = 16

negative = -1e30
highest = lax.Precision.HIGHEST
VMEM = 48 * 1024 * 1024


def flip(value, bit, total):
    return lax.ppermute(value, AXES, [(i, i ^ bit) for i in range(total)])


def unscramble(parts, me):
    bit = 1
    while bit < len(parts):
        swap = (me & bit) != 0
        parts = [jnp.where(swap, parts[p ^ bit], parts[p]) for p in range(len(parts))]
        bit *= 2
    return parts


def gather_small(value, me, total):
    blocks = value[None]
    bit = 1
    while bit < total:
        blocks = jnp.concatenate([blocks, flip(blocks, bit, total)], axis=0)
        bit *= 2
    bit = 1
    while bit < total:
        view = blocks.reshape(total // (2 * bit), 2, bit, *value.shape)
        view = jnp.where((me & bit) != 0, view[:, ::-1], view)
        blocks = view.reshape(total, *value.shape)
        bit *= 2
    return blocks


def scatter_small(value, me, total):
    bit = total // 2
    while bit:
        low_half, high_half = value[:bit], value[bit:]
        mine = (me & bit) != 0
        keep = jnp.where(mine, high_half, low_half)
        send = jnp.where(mine, low_half, high_half)
        value = keep + flip(send, bit, total)
        bit //= 2
    return value[0]


def scatter(value, order, me, total):
    _, rows, cols = value.shape
    left = [1 << i for i in reversed(range(total.bit_length() - 1))]
    for bit in order:
        at = left.index(bit)
        pre, post = 1 << at, 1 << (len(left) - at - 1)
        view = value.reshape(pre, 2, post, rows, cols)
        mine = (me // bit) % 2
        send = lax.dynamic_index_in_dim(view, 1 - mine, 1, keepdims=False)
        keep = lax.dynamic_index_in_dim(view, mine, 1, keepdims=False)
        got = flip(send, bit, total)
        value = keep.astype(jnp.float32) + got.astype(jnp.float32)
        left.pop(at)
        if left:
            value = value.astype(jnp.bfloat16)
    return value.reshape(rows, cols)


def spatial_bias(scalar, rows):
    column = lax.broadcasted_iota(jnp.int32, (1, rows), 1)
    return jnp.where(column < scalar * scalar, 0.0, negative)


def temporal_bias(frames_local, scalar, rows):
    def place(axis):
        index = lax.broadcasted_iota(jnp.int32, (rows, rows), axis)
        slot, at = index % GROUP, index // GROUP
        frame = ((at // frames_local) ^ scalar) * frames_local + at % frames_local
        return slot, frame

    slot_q, frame_q = place(0)
    slot_k, frame_k = place(1)
    return jnp.where((slot_q == slot_k) & (frame_q >= frame_k), 0.0, negative)


def lower_half(rows):
    return lax.broadcasted_iota(jnp.int32, (rows, LANES), 1) < E


def dot_t(a, b):
    return lax.dot_general(a, b, (((1,), (1,)), ((), ())), preferred_element_type=jnp.float32)


def t_dot(a, b):
    return lax.dot_general(a, b, (((0,), (0,)), ((), ())), preferred_element_type=jnp.float32)


def attention_forward(make_bias, scalar_ref, qkv_ref, out_ref):
    a, b, width = qkv_ref.shape
    rows, width = a * b, width // 3
    bias = make_bias(scalar_ref[0], rows)
    half = lower_half(rows)
    factor = E ** (-0.5)
    for c in range(0, width, LANES):
        q = qkv_ref[:, :, c : c + LANES].reshape(rows, LANES) * jnp.bfloat16(factor)
        k = qkv_ref[:, :, width + c : width + c + LANES].reshape(rows, LANES)
        v = qkv_ref[:, :, 2 * width + c : 2 * width + c + LANES].reshape(rows, LANES)
        pair = []
        for head in range(2):
            pick = half if head == 0 else ~half
            scores = dot_t(jnp.where(pick, q, 0), k) + bias
            weights = jnp.exp(scores - jnp.max(scores, axis=-1, keepdims=True))
            total = jnp.sum(weights, axis=-1, keepdims=True)
            probs = (weights * (1.0 / total)).astype(jnp.bfloat16)
            pair.append(jnp.dot(probs, v, preferred_element_type=jnp.float32))
        mixed = jnp.where(half, pair[0], pair[1]).astype(out_ref.dtype)
        out_ref[:, :, c : c + LANES] = mixed.reshape(a, b, LANES)


def attention_backward(make_bias, scalar_ref, qkv_ref, grad_ref, out_ref):
    a, b, width = qkv_ref.shape
    rows, width = a * b, width // 3
    bias = make_bias(scalar_ref[0], rows)
    half = lower_half(rows)
    factor = E ** (-0.5)
    for c in range(0, width, LANES):
        q = qkv_ref[:, :, c : c + LANES].reshape(rows, LANES) * jnp.bfloat16(factor)
        k = qkv_ref[:, :, width + c : width + c + LANES].reshape(rows, LANES)
        v = qkv_ref[:, :, 2 * width + c : 2 * width + c + LANES].reshape(rows, LANES)
        g = grad_ref[:, :, c : c + LANES].reshape(rows, LANES)
        dq, dk, dv = [], [], []
        for head in range(2):
            pick = half if head == 0 else ~half
            scores = dot_t(jnp.where(pick, q, 0), k) + bias
            weights = jnp.exp(scores - jnp.max(scores, axis=-1, keepdims=True))
            total = jnp.sum(weights, axis=-1, keepdims=True)
            probs = weights * (1.0 / total)
            prob_grad = dot_t(jnp.where(pick, g, 0), v)
            delta = jnp.sum(probs * prob_grad, axis=-1, keepdims=True)
            score_grad = (probs * (prob_grad - delta)).astype(jnp.bfloat16)
            dq.append(jnp.dot(score_grad, k, preferred_element_type=jnp.float32) * factor)
            dk.append(t_dot(score_grad, q))
            dv.append(t_dot(probs.astype(jnp.bfloat16), g))
        for index, pair in enumerate((dq, dk, dv)):
            merged = jnp.where(half, pair[0], pair[1]).astype(out_ref.dtype)
            start = index * width + c
            out_ref[:, :, start : start + LANES] = merged.reshape(a, b, LANES)


def run_attention(body, scalar, block, grid, index, inputs, out_width):
    a, b = block
    outer = inputs[0].shape[:2]
    rows = outer[0] * outer[1]
    return pl.pallas_call(
        body,
        grid=(grid,),
        in_specs=[pl.BlockSpec(memory_space=pltpu.SMEM)]
        + [pl.BlockSpec((a, b, x.shape[-1]), index) for x in inputs],
        out_specs=pl.BlockSpec((a, b, out_width), index),
        out_shape=jax.ShapeDtypeStruct((*outer, out_width), jnp.bfloat16),
        compiler_params=pltpu.CompilerParams(vmem_limit_bytes=VMEM),
        cost_estimate=pl.CostEstimate(
            flops=rows * H * E * 2 * a * b * 4,
            bytes_accessed=rows * 2 * (sum(x.shape[-1] for x in inputs) + out_width),
            transcendentals=rows * H * a * b,
        ),
    )(scalar, *inputs)


def normalise(inputs):
    average = jnp.mean(inputs, axis=-1, keepdims=True)
    centered = inputs - average
    variance = jnp.mean(centered * centered, axis=-1, keepdims=True)
    scale = lax.rsqrt(variance + 1e-05)
    return centered * scale, scale


def normalise_back(inputs, gain, grad):
    unit, scale = normalise(inputs)
    scaled = grad * gain
    first = jnp.mean(scaled, axis=-1, keepdims=True)
    second = jnp.mean(scaled * unit, axis=-1, keepdims=True)
    axes = tuple(range(grad.ndim - 1))
    return (
        scale * (scaled - first - unit * second),
        jnp.sum(grad * unit, axis=axes),
        jnp.sum(grad, axis=axes),
    )


def matmul(inputs, weight):
    return jnp.dot(inputs, weight, preferred_element_type=jnp.float32)


def on_device(
    tokens,
    actions,
    sides,
    action_table,
    norm_gains,
    norm_shifts,
    s_qkv,
    s_out,
    t_qkv,
    t_out,
    w_up,
    b_up,
    w_down,
    b_down,
    grad_out,
):
    frames_local, _, slots, width = tokens.shape
    tm_size, clip_size = lax.axis_size("tm"), lax.axis_size("clip")
    total = tm_size * clip_size
    me_tm, me_clip = lax.axis_index("tm"), lax.axis_index("clip")
    me = me_tm * clip_size + me_clip
    slots_local = slots // tm_size
    row_count = frames_local * slots
    bf16, f32 = jnp.bfloat16, jnp.float32

    clip_bits = [1 << i for i in reversed(range(clip_size.bit_length() - 1))]
    tm_bits = [clip_size << i for i in reversed(range(tm_size.bit_length() - 1))]
    z_bits, x_bits = clip_bits[:2], clip_bits[2:]
    y_bits, core_bits = tm_bits[:-1], tm_bits[-1:]
    order_xy = core_bits + x_bits + y_bits + z_bits
    order_yx = core_bits + y_bits + x_bits + z_bits

    def to_slots(value):
        view = value.reshape(frames_local, tm_size, slots_local, value.shape[-1])
        parts = []
        for o in range(tm_size):
            part = lax.dynamic_index_in_dim(view, me_tm ^ o, 1, keepdims=False)
            parts.append(flip(part, o * clip_size, total) if o else part)
        return jnp.concatenate(parts, axis=0)

    def from_slots(value):
        view = value.reshape(tm_size, frames_local, slots_local, value.shape[-1])
        parts = [flip(view[o], o * clip_size, total) if o else view[o] for o in range(tm_size)]
        parts = unscramble(parts, me_tm)
        return jnp.stack(parts, axis=1).reshape(frames_local, slots, value.shape[-1])

    small = jnp.concatenate(
        [x.reshape(-1) for x in (action_table, norm_gains, norm_shifts, b_up, b_down)]
    )
    sizes = [action_table.size, norm_gains.size, norm_shifts.size, b_up.size, b_down.size]
    padded = -(-sum(sizes) // 2048) * 2048
    small = jnp.pad(small, (0, padded - sum(sizes))).reshape(padded // LANES, LANES)
    small = gather_small(small, me, total).reshape(total, padded).astype(f32)
    ends = [sum(sizes[:i]) for i in range(len(sizes) + 1)]

    def unpack(i, rows):
        part = small[:, ends[i] : ends[i + 1]]
        return jnp.moveaxis(part.reshape(total, rows, -1), 1, 0).reshape(rows, -1)

    action_rows, gains, shifts = unpack(0, ACTIONS), unpack(1, 3), unpack(2, 3)
    up_bias, down_bias = unpack(3, 1), unpack(4, 1)

    def gathered(x):
        return lax.all_gather(x, AXES, axis=0, tiled=True)

    sq_full = gathered(s_qkv)
    middle = gathered(jnp.concatenate([s_out, t_qkv, t_out], axis=1))
    so_full = middle[:, :width]
    tq_full = middle[:, width : 4 * width]
    to_full = middle[:, 4 * width :]
    up_full = gathered(w_up)
    down_full = gathered(w_down)

    side = sides.reshape(1)
    onehot = (actions == jnp.arange(ACTIONS)[None, :]).astype(f32)
    embedded = jnp.dot(onehot, action_rows, precision=highest)
    hidden0 = tokens.reshape(frames_local, slots, width).astype(f32) + embedded[:, None, :]
    unit, _ = normalise(hidden0)
    normed1 = (unit * gains[0] + shifts[0]).astype(bf16).reshape(row_count, width)
    spatial = matmul(normed1, sq_full).astype(bf16).reshape(frames_local, slots, 3 * width)

    def frame_index(i):
        return (i, 0, 0)

    s_mixed = run_attention(
        partial(attention_forward, spatial_bias),
        side, (1, slots), frames_local, frame_index, [spatial], width,
    ).reshape(row_count, width)
    hidden1 = hidden0 + matmul(s_mixed, so_full).reshape(hidden0.shape)

    cotangent = to_slots(grad_out.reshape(frames_local, slots, width))
    hidden1 = to_slots(hidden1.astype(bf16)).astype(f32)
    frames = hidden1.shape[0]
    slot_at = me_tm * slots_local + jnp.arange(slots_local)
    mask = (slot_at < sides[0] * sides[0]).astype(f32)[None, :, None]
    unit, _ = normalise(hidden1)
    normed2 = (unit * gains[1] + shifts[1]).astype(bf16).reshape(row_count, width)
    temporal = matmul(normed2, tq_full).astype(bf16).reshape(frames, slots_local, 3 * width)

    def slot_index(i):
        return (0, i, 0)

    me_tm_array = me_tm.astype(jnp.int32).reshape(1)
    t_mixed = run_attention(
        partial(attention_forward, partial(temporal_bias, frames_local)),
        me_tm_array, (frames, GROUP), slots_local // GROUP, slot_index, [temporal], width,
    ).reshape(row_count, width)
    hidden2 = hidden1 + matmul(t_mixed, to_full).reshape(hidden1.shape)
    unit, _ = normalise(hidden2)
    normed3 = (unit * gains[2] + shifts[2]).astype(bf16).reshape(row_count, width)
    inner = matmul(normed3, up_full) + up_bias
    active, gelu_back = jax.vjp(partial(jax.nn.gelu, approximate=False), inner)
    active = active.astype(bf16)
    hidden3 = hidden2 + (matmul(active, down_full) + down_bias).reshape(hidden2.shape)
    mixed = from_slots((hidden3 * mask).astype(bf16))

    def blocks(grad):
        return grad.astype(bf16).reshape(total, grad.shape[0] // total, grad.shape[1])

    def halves(grad):
        half = grad.shape[1] // 2
        return jnp.concatenate(
            [
                scatter(blocks(grad[:, :half]), order_xy, me, total),
                scatter(blocks(grad[:, half:]), order_yx, me, total),
            ],
            axis=1,
        )

    grad3 = cotangent.astype(f32) * mask
    down_in = grad3.astype(bf16).reshape(row_count, width)
    g_w_down = scatter(blocks(t_dot(active, down_in)), order_xy, me, total)
    g_b_down = jnp.sum(down_in.astype(f32), axis=0)
    inner_grad = gelu_back(dot_t(down_in, down_full))[0].astype(bf16)
    g_w_up = scatter(blocks(t_dot(normed3, inner_grad)), order_yx, me, total)
    g_b_up = jnp.sum(inner_grad.astype(f32), axis=0)
    back3 = normalise_back(hidden2, gains[2], dot_t(inner_grad, up_full).reshape(hidden2.shape))
    grad2 = grad3 + back3[0]
    t_in = grad2.astype(bf16).reshape(row_count, width)
    g_t_out = scatter(blocks(t_dot(t_mixed, t_in)), order_yx, me, total)
    t_mix_grad = dot_t(t_in, to_full).astype(bf16).reshape(frames, slots_local, width)
    t_grad = run_attention(
        partial(attention_backward, partial(temporal_bias, frames_local)),
        me_tm_array, (frames, GROUP), slots_local // GROUP, slot_index, [temporal, t_mix_grad],
        3 * width,
    ).reshape(row_count, 3 * width)
    g_t_qkv = scatter(blocks(t_dot(normed2, t_grad)), order_xy, me, total)
    back2 = normalise_back(hidden1, gains[1], dot_t(t_grad, tq_full).reshape(hidden1.shape))
    grad1 = from_slots((grad2 + back2[0]).astype(bf16))
    s_in = grad1.reshape(row_count, width)
    g_s_out = scatter(blocks(t_dot(s_mixed, s_in)), order_yx, me, total)
    mix_grad = dot_t(s_in, so_full).astype(bf16).reshape(frames_local, slots, width)
    s_grad = run_attention(
        partial(attention_backward, spatial_bias),
        side, (1, slots), frames_local, frame_index, [spatial, mix_grad], 3 * width,
    ).reshape(row_count, 3 * width)
    g_s_qkv = halves(t_dot(normed1, s_grad))
    back1 = normalise_back(hidden0, gains[0], dot_t(s_grad, sq_full).reshape(hidden0.shape))
    input_grad = grad1.astype(f32) + back1[0]
    g_actions = jnp.dot(onehot.T, jnp.sum(input_grad, axis=1), precision=highest)

    terms = [
        g_actions,
        jnp.stack([back1[1], back2[1], back3[1]]),
        jnp.stack([back1[2], back2[2], back3[2]]),
        g_b_up[None],
        g_b_down[None],
    ]
    packed = [jnp.moveaxis(x.reshape(x.shape[0], total, -1), 1, 0).reshape(total, -1) for x in terms]
    packed = jnp.concatenate(packed, axis=1)
    packed = jnp.pad(packed, ((0, 0), (0, -packed.shape[1] % LANES)))
    summed = scatter_small(packed, me, total)

    def piece(i, rows):
        return summed[ends[i] : ends[i + 1]].reshape(rows, -1)

    shape = tokens.shape
    return (
        mixed.reshape(shape),
        input_grad.reshape(shape),
        piece(0, ACTIONS),
        piece(1, 3),
        piece(2, 3),
        g_s_qkv,
        g_s_out,
        g_t_qkv,
        g_t_out,
        g_w_up,
        piece(3, 1).reshape(-1),
        g_w_down,
        piece(4, 1).reshape(-1),
    )


def solution(mesh):
    whole = P(("tm", "clip"), None)
    columns = P(None, ("tm", "clip"))
    frames = P("tm", "clip", None, None)
    vector = P(("tm", "clip"))
    return jax.shard_map(
        on_device,
        mesh=mesh,
        in_specs=(
            frames, P("tm", "clip"), P("clip"), columns, columns, columns, whole, whole, whole,
            whole, whole, vector, whole, vector, frames,
        ),
        out_specs=(
            frames, frames, columns, columns, columns, whole, whole, whole, whole, whole, vector,
            whole, vector,
        ),
        check_vma=False,
    )
```

```python
from functools import partial

import jax
import jax.numpy as jnp
from jax import lax
from jax.experimental import pallas as pl
from jax.experimental.pallas import tpu as pltpu
from jax.sharding import PartitionSpec as P

H = 16
E = 64
ACTIONS = 8
FRAMES = 16
AXES = ("tm", "clip")
LANES = 128
GROUP = 16

negative = -1e30
highest = lax.Precision.HIGHEST
VMEM = 48 * 1024 * 1024
bf16, f32 = jnp.bfloat16, jnp.float32


class Place:
    def __init__(self):
        tm_size, clip_size = lax.axis_size("tm"), lax.axis_size("clip")
        self.tm_size, self.clip_size, self.total = tm_size, clip_size, tm_size * clip_size
        self.tm = lax.axis_index("tm")
        self.me = self.tm * clip_size + lax.axis_index("clip")
        self.core_bit = clip_size
        self.core = self.bit_of(clip_size)
        clip_bits = [1 << i for i in range(clip_size.bit_length() - 1)]
        tm_bits = [clip_size << i for i in range(tm_size.bit_length() - 1)]
        x, z, y = clip_bits[:-2], clip_bits[-2:], tm_bits[1:]
        self.z = [(b, b) for b in z]
        self.xy = list(zip(x + y, y + x))

    def bit_of(self, bit):
        return (self.me // bit) % 2

    def mine(self, pair):
        return jnp.where(self.core == 0, self.bit_of(pair[0]), self.bit_of(pair[1]))

    def choose(self, pair):
        return jnp.where(self.core == 0, pair[0], pair[1])

    def flip(self, value, pair):
        moves = [(i, i ^ pair[(i // self.core_bit) % 2]) for i in range(self.total)]
        return lax.ppermute(value, AXES, moves)

    def tm_flip(self, value, offset):
        moves = [(i, i ^ (offset * self.clip_size)) for i in range(self.total)]
        return lax.ppermute(value, AXES, moves)


def below(have, bit):
    return sum(1 for b in have if b < bit)


def unscramble(parts, me):
    bit = 1
    while bit < len(parts):
        swap = (me & bit) != 0
        parts = [jnp.where(swap, parts[p ^ bit], parts[p]) for p in range(len(parts))]
        bit *= 2
    return parts


def position(m, value, k):
    m = jnp.int32(m)
    high = lax.shift_left(lax.shift_right_logical(m, k), k + 1)
    return high | lax.shift_left(value, k) | (m & (lax.shift_left(jnp.int32(1), k) - 1))


def merge_body(info_ref, mine_ref, other_ref, out_ref):
    k, value = info_ref[0], info_ref[1]
    for m in range(mine_ref.shape[0]):
        out_ref[position(m, value, k)] = mine_ref[m]
        out_ref[position(m, 1 - value, k)] = other_ref[m]


def column_block(shape):
    blocks, rows, cols = shape
    return cols if blocks * rows * cols <= 512 * 1024 else min(cols, 512)


def merge(mine, other, k, value):
    m, r, n = mine.shape
    block = column_block((2 * m, r, n))
    spec = pl.BlockSpec((m, r, block), lambda j: (0, 0, j))
    return pl.pallas_call(
        merge_body,
        grid=(n // block,),
        in_specs=[pl.BlockSpec(memory_space=pltpu.SMEM), spec, spec],
        out_specs=pl.BlockSpec((2 * m, r, block), lambda j: (0, 0, j)),
        out_shape=jax.ShapeDtypeStruct((2 * m, r, n), mine.dtype),
        compiler_params=pltpu.CompilerParams(vmem_limit_bytes=VMEM),
        cost_estimate=pl.CostEstimate(
            flops=0, bytes_accessed=4 * m * r * n * mine.dtype.itemsize, transcendentals=0
        ),
    )(jnp.stack([jnp.int32(k), value.astype(jnp.int32)]), mine, other)


def split_body(ends, info_ref, *refs):
    k, value, step = info_ref[0], info_ref[1], pl.program_id(0)
    send_ref, keep_ref = refs[-2:]
    for p in range(len(ends) - 1):

        @pl.when((step >= ends[p]) & (step < ends[p + 1]))
        def _(a_ref=refs[2 * p], b_ref=refs[2 * p + 1]):
            for m in range(send_ref.shape[0]):
                for out_ref, at in ((send_ref, 1 - value), (keep_ref, value)):
                    i = position(m, at, k)
                    total = a_ref[i].astype(f32) + b_ref[i].astype(f32)
                    out_ref[m] = total.astype(out_ref.dtype)


def split(pairs, k, value, dtype):
    blocks, r, _ = pairs[0][0].shape
    widths = [a.shape[-1] for a, _ in pairs]
    n = sum(widths)
    block = min([column_block((blocks, r, n))] + widths)
    ends = [sum(widths[:i]) // block for i in range(len(widths) + 1)]
    in_specs = [pl.BlockSpec(memory_space=pltpu.SMEM)]
    for low, high in zip(ends[:-1], ends[1:]):

        def index(j, low=low, high=high):
            return (0, 0, jnp.clip(j - low, 0, high - low - 1))

        in_specs += [pl.BlockSpec((blocks, r, block), index)] * 2
    out = jax.ShapeDtypeStruct((blocks // 2, r, n), dtype)
    return pl.pallas_call(
        partial(split_body, ends),
        grid=(n // block,),
        in_specs=in_specs,
        out_specs=[pl.BlockSpec((blocks // 2, r, block), lambda j: (0, 0, j))] * 2,
        out_shape=[out, out],
        compiler_params=pltpu.CompilerParams(vmem_limit_bytes=VMEM),
        cost_estimate=pl.CostEstimate(
            flops=blocks * r * n, bytes_accessed=6 * blocks * r * n, transcendentals=0
        ),
    )(jnp.stack([jnp.int32(k), value.astype(jnp.int32)]), *[x for pair in pairs for x in pair])


def gather_small(place, value):
    core = (place.core_bit, place.core_bit)
    x_and_y = [(b, b) for b, _ in place.xy]
    count = len(x_and_y) // 2
    blocks, have = value[None], []
    for pair in x_and_y[:count] + [core] + x_and_y[count:] + place.z:
        (send,) = yield [blocks]
        (got,) = yield [place.flip(send, pair)]
        blocks = merge(blocks, got, below(have, pair[0]), place.bit_of(pair[0]))
        have.append(pair[0])
    return blocks


def scatter_small(place, value):
    bit = place.total // 2
    while bit:
        low_half, high_half = value[:bit], value[bit:]
        mine = (place.me & bit) != 0
        keep = jnp.where(mine, high_half, low_half)
        (send,) = yield [jnp.where(mine, low_half, high_half)]
        (got,) = yield [place.flip(send, (bit, bit))]
        value = keep + got
        bit //= 2
    return value[0]


def gather(place, keep, send):
    core = (place.core_bit, place.core_bit)
    have = ([], [])
    blocks, out = keep[None], send[None]
    for pair in [core] + place.z[::-1] + place.xy:
        (out,) = yield [out]
        (got,) = yield [place.flip(out, pair)]
        k = [below(h, b) for h, b in zip(have, pair)]
        blocks = out = merge(blocks, got, place.choose(k), place.mine(pair))
        have = (have[0] + [pair[0]], have[1] + [pair[1]])
    (out,) = yield [out]
    (got,) = yield [place.flip(out, core)]
    return blocks, got


def scatter(place, pairs):
    core = (place.core_bit, place.core_bit)
    bits = [1 << i for i in range(place.total.bit_length() - 1)]
    have = (bits, bits)
    for pair in place.xy[::-1] + place.z + [core]:
        have = tuple([b for b in h if b != bit] for h, bit in zip(have, pair))
        k = [below(h, b) for h, b in zip(have, pair)]
        dtype = f32 if pair == core else bf16
        send, keep = split(pairs, place.choose(k), place.mine(pair), dtype)
        (send,) = yield [send]
        (got,) = yield [place.flip(send, pair)]
        pairs = [(keep, got)]
    return keep[0], got[0]


class Chain:
    def __init__(self, steps):
        self.steps, self.flying, self.result = steps, False, None
        self.pending = next(steps)

    def done(self):
        return self.result is not None

    def move(self):
        try:
            self.pending = self.steps.send(self.pending)
        except StopIteration as stop:
            self.result = stop.value
        self.flying = not self.flying


def along(value, *chains):
    ending = [c for c in chains if c.flying]
    if ending:
        value, got = lax.optimization_barrier((value, [c.pending for c in ending]))
        for c, g in zip(ending, got):
            c.pending = g
            c.move()
    starting = [c for c in chains if not c.done()]
    if starting:
        value, sent = lax.optimization_barrier((value, [c.pending for c in starting]))
        for c, g in zip(starting, sent):
            c.pending = g
            c.move()
    return value


def finish(chain):
    while not chain.done():
        chain.move()
    return chain.result


def spatial_bias(scalar, rows, keys):
    key = lax.broadcasted_iota(jnp.int32, (1, rows) if keys == 1 else (rows, 1), keys)
    return jnp.where(key < scalar * scalar, 0.0, negative)


def temporal_bias(frames_local, scalar, rows, keys):
    def place(axis):
        index = lax.broadcasted_iota(jnp.int32, (rows, rows), axis)
        slot, at = index % GROUP, index // GROUP
        frame = ((at // frames_local) ^ scalar) * frames_local + at % frames_local
        return slot, frame

    slot_q, frame_q = place(1 - keys)
    slot_k, frame_k = place(keys)
    return jnp.where((slot_q == slot_k) & (frame_q >= frame_k), 0.0, negative)


def dot_t(a, b):
    return lax.dot_general(a, b, (((1,), (1,)), ((), ())), preferred_element_type=f32)


def t_dot(a, b):
    return lax.dot_general(a, b, (((0,), (0,)), ((), ())), preferred_element_type=f32)


def columns(scalar_ref, side, start):
    half = H * E // 2
    return pl.ds(pl.multiple_of((scalar_ref[1] ^ side) * half + start, LANES), LANES)


def two_heads(rows):
    half = lax.broadcasted_iota(jnp.int32, (rows, LANES), 1) < E

    def apart(x):
        return jnp.concatenate([jnp.where(half, x, 0), jnp.where(half, 0, x)], axis=0)

    def together(x):
        return jnp.where(half, x[:rows], x[rows:])

    return apart, together


def attention_forward(make_bias, scalar_ref, own_ref, other_ref, out_ref):
    a, b, width = own_ref.shape
    rows, width = a * b, width // 3
    bias = make_bias(scalar_ref[0], rows, 1)
    apart, together = two_heads(rows)
    factor = E ** (-0.5)
    for side, qkv_ref in enumerate((own_ref, other_ref)):
        for c in range(0, width, LANES):
            q = qkv_ref[:, :, c : c + LANES].reshape(rows, LANES) * bf16(factor)
            k = qkv_ref[:, :, width + c : width + c + LANES].reshape(rows, LANES)
            v = qkv_ref[:, :, 2 * width + c : 2 * width + c + LANES].reshape(rows, LANES)
            scores = dot_t(apart(q), k).reshape(2, rows, rows) + bias[None]
            weights = jnp.exp(scores - jnp.max(scores, axis=2, keepdims=True))
            scale = 1.0 / jnp.sum(weights, axis=2, keepdims=True)
            weights = weights.astype(bf16).reshape(2 * rows, rows)
            mixed = jnp.dot(weights, v, preferred_element_type=f32)
            mixed = together(mixed * scale.reshape(2 * rows, 1)).astype(out_ref.dtype)
            out_ref[:, :, columns(scalar_ref, side, c)] = mixed.reshape(a, b, LANES)


def attention_backward(make_bias, sides, scalar_ref, *refs):
    grad_ref = refs[len(sides)]
    a, b, width = refs[0].shape
    rows, width = a * b, width // 3
    bias = make_bias(scalar_ref[0], rows, 0)
    apart, together = two_heads(rows)
    factor = E ** (-0.5)
    for i, side in enumerate(sides):
        qkv_ref, out_ref = refs[i], refs[len(sides) + 1 + i]
        for c in range(0, width, LANES):
            q = qkv_ref[:, :, c : c + LANES].reshape(rows, LANES) * bf16(factor)
            k = qkv_ref[:, :, width + c : width + c + LANES].reshape(rows, LANES)
            v = qkv_ref[:, :, 2 * width + c : 2 * width + c + LANES].reshape(rows, LANES)
            g = grad_ref[:, :, columns(scalar_ref, side, c)].reshape(rows, LANES)
            scores = dot_t(apart(k), q).reshape(2, rows, rows) + bias[None]
            weights = jnp.exp(scores - jnp.max(scores, axis=1, keepdims=True))
            probs = weights * (1.0 / jnp.sum(weights, axis=1, keepdims=True))
            prob_grad = dot_t(apart(v), g).reshape(2, rows, rows)
            delta = jnp.sum(probs * prob_grad, axis=1, keepdims=True)
            score_grad = (probs * (prob_grad - delta)).astype(bf16)
            turned = jnp.concatenate([score_grad[0].T, score_grad[1].T], axis=0)
            dq = jnp.dot(turned, k, preferred_element_type=f32) * factor
            dk = jnp.dot(score_grad.reshape(2 * rows, rows), q, preferred_element_type=f32)
            dv = jnp.dot(
                probs.astype(bf16).reshape(2 * rows, rows), g, preferred_element_type=f32
            )
            for index, grad in enumerate((dq, dk, dv)):
                start = index * width + c
                merged = together(grad).astype(out_ref.dtype)
                out_ref[:, :, start : start + LANES] = merged.reshape(a, b, LANES)


def run_attention(body, scalars, block, grid, index, inputs, out_widths):
    a, b = block
    outer = inputs[0].shape[:2]
    rows = outer[0] * outer[1]
    return pl.pallas_call(
        body,
        grid=(grid,),
        in_specs=[pl.BlockSpec(memory_space=pltpu.SMEM)]
        + [pl.BlockSpec((a, b, x.shape[-1]), index) for x in inputs],
        out_specs=[pl.BlockSpec((a, b, width), index) for width in out_widths],
        out_shape=[jax.ShapeDtypeStruct((*outer, width), bf16) for width in out_widths],
        compiler_params=pltpu.CompilerParams(vmem_limit_bytes=VMEM),
        cost_estimate=pl.CostEstimate(
            flops=rows * H * E * 2 * a * b * 4,
            bytes_accessed=rows * 2 * (sum(x.shape[-1] for x in inputs) + sum(out_widths)),
            transcendentals=rows * H * a * b,
        ),
    )(scalars, *inputs)


def centre(x):
    average = jnp.mean(x, axis=-1, keepdims=True)
    centered = x - average
    variance = jnp.mean(centered * centered, axis=-1, keepdims=True)
    scale = lax.rsqrt(variance + 1e-05)
    return centered * scale, scale


def norm_body(x_ref, added_ref, gain_ref, shift_ref, out_ref):
    unit, _ = centre(x_ref[0].astype(f32) + added_ref[0])
    out_ref[0] = (unit * gain_ref[...] + shift_ref[...]).astype(out_ref.dtype)


def norm_back_body(x_ref, added_ref, gain_ref, grad_ref, rest_ref, out_ref, sums_ref):
    unit, scale = centre(x_ref[0].astype(f32) + added_ref[0])
    grad = grad_ref[0]
    scaled = grad * gain_ref[...]
    first = jnp.mean(scaled, axis=-1, keepdims=True)
    second = jnp.mean(scaled * unit, axis=-1, keepdims=True)
    out = rest_ref[0].astype(f32) + scale * (scaled - first - unit * second)
    out_ref[0] = out.astype(out_ref.dtype)
    terms = (grad * unit, grad, out)
    sums_ref[0] = jnp.concatenate([jnp.sum(x, axis=0, keepdims=True) for x in terms], axis=0)


def by_rows(body, arrays, rows, outs):
    blocks = arrays[0].shape[0]
    specs = []
    for x in arrays:
        if x.ndim == 2:
            specs.append(pl.BlockSpec(x.shape, lambda i: (0, 0)))
        else:
            at = (lambda i: (i, 0, 0)) if x.shape[0] == blocks else (lambda i: (0, 0, 0))
            specs.append(pl.BlockSpec((1, *x.shape[1:]), at))
    count = sum(x.size for x in arrays)
    return pl.pallas_call(
        body,
        grid=(blocks,),
        in_specs=specs,
        out_specs=[pl.BlockSpec((1, *shape[1:]), lambda i: (i, 0, 0)) for shape, _ in outs],
        out_shape=[jax.ShapeDtypeStruct(shape, dtype) for shape, dtype in outs],
        compiler_params=pltpu.CompilerParams(vmem_limit_bytes=VMEM),
        cost_estimate=pl.CostEstimate(
            flops=10 * count, bytes_accessed=4 * count, transcendentals=0
        ),
    )(*arrays)


def norm(x, added, gain, shift):
    shape = (x.shape[0] * x.shape[1] // 256, 256, x.shape[2])
    arrays = [x.reshape(shape), added, gain[None], shift[None]]
    (out,) = by_rows(norm_body, arrays, 256, [(shape, bf16)])
    return out.reshape(-1, shape[2])


def norm_back(x, added, gain, grad, rest, dtype):
    shape = (x.shape[0] * x.shape[1] // 256, 256, x.shape[2])
    arrays = [x.reshape(shape), added, gain[None], grad.reshape(shape), rest.reshape(shape)]
    sums = ((shape[0], 3, shape[2]), f32)
    out, sums = by_rows(norm_back_body, arrays, 256, [(shape, dtype), sums])
    return out.reshape(x.shape), sums


def matmul(inputs, weight):
    return jnp.dot(inputs, weight, preferred_element_type=f32)


TAIL = (
    0.14760860800743103, 0.14761532843112946, 0.127163827419281, 0.09018292278051376,
    0.013407237827777863, 0.06451446563005447, -0.19429759681224823, 0.13513216376304626,
    -0.031326886266469955,
)


def gelu(inner):
    size = jnp.abs(inner)
    t = 1.0 / (1.0 + 0.37 * size)
    bell = jnp.exp(inner * inner * -0.5)
    series = TAIL[-1]
    for term in reversed(TAIL[:-1]):
        series = series * t + term
    tail = series * t * bell
    cdf = jnp.where(inner > 0, 1.0 - tail, tail)
    return inner * cdf, cdf + inner * bell * 0.3989422804014327


def up_body(x_ref, w_ref, bias_ref, active_ref, slope_ref):
    rows = x_ref.shape[0]
    step = min(rows, 256)
    for r in range(0, rows, step):
        inner = jnp.dot(x_ref[r : r + step], w_ref[...], preferred_element_type=f32)
        active, slope = gelu(inner + bias_ref[...])
        active_ref[r : r + step] = active.astype(active_ref.dtype)
        slope_ref[r : r + step] = slope.astype(slope_ref.dtype)


def up_project(x, weight, bias):
    rows, width = x.shape
    cols, block = weight.shape[1], 512
    out = jax.ShapeDtypeStruct((rows, cols), bf16)
    return pl.pallas_call(
        up_body,
        grid=(cols // block,),
        in_specs=[
            pl.BlockSpec((rows, width), lambda i: (0, 0)),
            pl.BlockSpec((width, block), lambda i: (0, i)),
            pl.BlockSpec((1, block), lambda i: (0, i)),
        ],
        out_specs=[pl.BlockSpec((rows, block), lambda i: (0, i))] * 2,
        out_shape=[out, out],
        compiler_params=pltpu.CompilerParams(vmem_limit_bytes=VMEM),
        cost_estimate=pl.CostEstimate(
            flops=2 * rows * width * cols,
            bytes_accessed=2 * (rows * width + width * cols + 2 * rows * cols),
            transcendentals=rows * cols,
        ),
    )(x, weight, bias)


def on_device(
    tokens,
    actions,
    sides,
    action_table,
    norm_gains,
    norm_shifts,
    s_qkv,
    s_out,
    t_qkv,
    t_out,
    w_up,
    b_up,
    w_down,
    b_down,
    grad_out,
):
    shape = tokens.shape
    frames_local, _, slots, width = shape
    place = Place()
    total, core, tm_size = place.total, place.core, place.tm_size
    slots_local = slots // tm_size
    row_count = frames_local * slots
    half = width // 2

    def to_slots(value):
        view = value.reshape(frames_local, tm_size, slots_local, value.shape[-1])
        parts = []
        for o in range(tm_size):
            part = lax.dynamic_index_in_dim(view, place.tm ^ o, 1, keepdims=False)
            parts.append(place.tm_flip(part, o) if o else part)
        return parts

    def from_slots(value):
        view = value.reshape(tm_size, frames_local, slots_local, value.shape[-1])
        return [place.tm_flip(view[o], o) if o else view[o] for o in range(tm_size)]

    def in_slots(parts):
        return jnp.concatenate(parts, axis=0)

    def in_frames(parts):
        return jnp.stack(unscramble(parts, place.tm), axis=1).reshape(frames_local, slots, -1)

    def own_and_other(value, axis):
        first, second = (lax.index_in_dim(value, i, axis, keepdims=False) for i in (0, 1))
        return jnp.where(core == 0, first, second), jnp.where(core == 0, second, first)

    def in_order(own, other, axis):
        pair = [jnp.where(core == 0, own, other), jnp.where(core == 0, other, own)]
        return jnp.stack(pair, axis=axis)

    def halves(value):
        first, second = value[:, :half], value[:, half:]
        return jnp.where(core == 0, first, second), jnp.where(core == 0, second, first)

    def woven(own, other):
        cuts = [slice(i, i + half) for i in range(0, own.shape[1], half)]
        own_first = [x[:, cut] for cut in cuts for x in (own, other)]
        other_first = [x[:, cut] for cut in cuts for x in (other, own)]
        return jnp.where(
            core == 0,
            jnp.concatenate(own_first, axis=1),
            jnp.concatenate(other_first, axis=1),
        )

    def joined(own, other):
        return jnp.where(
            core == 0,
            jnp.concatenate([own, other], axis=1),
            jnp.concatenate([other, own], axis=1),
        )

    thin = width // total
    counts = [ACTIONS, 3, 3, 1]
    ends = [sum(counts[:i]) for i in range(len(counts) + 1)]
    small = jnp.concatenate([action_table, norm_gains, norm_shifts, b_down[None]], axis=0).T
    small = jnp.pad(small, ((0, 0), (0, LANES - ends[-1])))
    b_up = jnp.pad(b_up[None], ((0, GROUP - 1), (0, LANES - b_up.shape[0])))
    small = jnp.concatenate([small, b_up], axis=0)

    rows = s_qkv.shape[0]
    hidden_half = w_down.shape[0] // 2

    def attention_group(qkv, out):
        qkv = own_and_other(qkv.reshape(rows, 3, 2, half), 2)
        both = [
            jnp.concatenate([a.reshape(rows, 3 * half), b], axis=1)
            for a, b in zip(qkv, halves(out))
        ]
        return Chain(gather(place, *both))

    front = attention_group(s_qkv, s_out)
    tokens = along(tokens, front)
    tokens, small, grad_out = lax.optimization_barrier((tokens, small, grad_out))
    tokens = along(tokens, front)
    cotangent = to_slots(grad_out.reshape(frames_local, slots, width))
    small = Chain(gather_small(place, small))
    tokens = along(tokens, small)
    tokens = along(tokens, small)
    tokens, t_qkv, t_out = lax.optimization_barrier((tokens, t_qkv, t_out))
    tokens = along(tokens, front)
    middle = attention_group(t_qkv, t_out)
    tokens = along(tokens, middle)
    tokens, cotangent = lax.optimization_barrier((tokens, cotangent))
    tokens = along(tokens, front, small)
    tokens, w_up, w_down = lax.optimization_barrier((tokens, w_up, w_down))
    up_pair = own_and_other(w_up.reshape(rows, total, 2, hidden_half), 2)
    rising = Chain(gather(place, *[x.reshape(rows, -1) for x in up_pair]))
    falling = Chain(gather(place, *own_and_other(w_down.reshape(2, hidden_half, width), 0)))
    tokens = along(tokens, small, middle)
    while not small.done():
        tokens = along(tokens, small)
    small = small.result.astype(f32)
    table = small[:, :thin].reshape(width, LANES).T

    def unpack(i):
        return table[ends[i] : ends[i + 1]]

    action_rows, gains, shifts, down_bias = [unpack(i) for i in range(4)]
    up_bias = small[:, thin, : 2 * hidden_half].reshape(total, 2, hidden_half)
    up_bias = [x.reshape(1, -1) for x in own_and_other(up_bias, 1)]

    onehot = (actions == jnp.arange(ACTIONS)[None, :]).astype(f32)
    embedded = jnp.dot(onehot, action_rows, precision=highest)
    tokens = tokens.reshape(frames_local, slots, width)
    embedded = embedded[:, None, :]
    tokens, embedded = along((tokens, embedded), front, middle)
    normed1 = norm(tokens, embedded, gains[0], shifts[0])
    normed1 = along(normed1, rising)
    normed1 = along(normed1, front, middle)
    whole = [x.reshape(width, -1) for x in finish(front)]
    sq_halves = [x[:, : 3 * half] for x in whole]

    def project(x, halves, outer):
        return [matmul(x, w).astype(bf16).reshape(*outer, -1) for w in halves]

    spatial = project(normed1, sq_halves, (frames_local, slots))
    spatial = along(spatial, middle, rising)

    def frame_index(i):
        return (i, 0, 0)

    def slot_index(i):
        return (0, i, 0)

    spatial_place = (
        jnp.stack([sides[0], core.astype(jnp.int32)]), (1, slots), frames_local, frame_index,
    )
    (s_mixed,) = run_attention(
        partial(attention_forward, spatial_bias), *spatial_place, spatial, [width]
    )
    s_mixed = s_mixed.reshape(row_count, width)
    so_full = joined(*[x[:, 3 * half :] for x in whole])
    hidden0 = tokens.astype(f32) + embedded
    hidden1 = hidden0 + matmul(s_mixed, so_full).reshape(tokens.shape)

    hidden1 = along(hidden1.astype(bf16), middle, rising, falling)
    parts = to_slots(hidden1)
    hidden1 = in_slots(parts)
    frames = hidden1.shape[0]
    slot_at = place.tm * slots_local + jnp.arange(slots_local)
    mask = (slot_at < sides[0] * sides[0])[None, :, None]
    nothing = jnp.zeros((1, 1, width), f32)
    normed2 = norm(hidden1, nothing, gains[1], shifts[1])
    whole = [x.reshape(width, -1) for x in finish(middle)]
    tq_halves = [x[:, : 3 * half] for x in whole]
    to_full = joined(*[x[:, 3 * half :] for x in whole])
    normed2 = along(normed2, rising, falling)
    temporal = project(normed2, tq_halves, (frames, slots_local))
    temporal = along(temporal, rising, falling)
    temporal_place = (
        jnp.stack([place.tm.astype(jnp.int32), core.astype(jnp.int32)]), (frames, GROUP),
        slots_local // GROUP, slot_index,
    )
    make_bias = partial(temporal_bias, frames_local)
    (t_mixed,) = run_attention(
        partial(attention_forward, make_bias), *temporal_place, temporal, [width]
    )
    t_mixed = t_mixed.reshape(row_count, width)
    hidden2 = hidden1.astype(f32) + matmul(t_mixed, to_full).reshape(hidden1.shape)
    normed3 = norm(hidden2, nothing, gains[2], shifts[2])
    normed3 = along(normed3, rising, falling)
    up_halves = [x.reshape(width, -1) for x in finish(rising)]
    first = up_project(normed3, up_halves[0], up_bias[0])
    first = along(first, falling)
    normed3, first = lax.optimization_barrier((normed3, first))
    second = up_project(normed3, up_halves[1], up_bias[1])
    second = along(second, falling)
    (active, slope), (active2, slope2) = first, second
    down_halves = [x.reshape(-1, width) for x in finish(falling)]
    hidden3 = hidden2.reshape(row_count, width) + matmul(active, down_halves[0]) + down_bias
    hidden3 = hidden3 + matmul(active2, down_halves[1])
    mixed = from_slots(jnp.where(mask, hidden3.reshape(hidden2.shape), 0).astype(bf16))

    def blocks(grad):
        return grad.astype(bf16).reshape(total, grad.shape[0] // total, grad.shape[1])

    core_pair = (place.core_bit, place.core_bit)

    def exchanged(grad):
        return place.flip(blocks(grad), core_pair)

    def sums(keeps, gots):
        return Chain(scatter(place, [(blocks(x), y) for x, y in zip(keeps, gots)]))

    down_in = jnp.where(mask, in_slots(cotangent), 0).reshape(row_count, width)
    send = t_dot(active2, down_in).astype(bf16)
    down_in, send, active = lax.optimization_barrier((down_in, send, active))
    got = exchanged(send)
    keep = t_dot(active, down_in).astype(bf16)
    down_in, keep = lax.optimization_barrier((down_in, keep))
    inner_grad = (dot_t(down_in, down_halves[0]) * slope.astype(f32)).astype(bf16)
    s_down = sums([keep], [got])
    down_in, inner_grad = along((down_in, inner_grad), s_down)
    inner_grad2 = (dot_t(down_in, down_halves[1]) * slope2.astype(f32)).astype(bf16)
    send = t_dot(normed3, inner_grad2).astype(bf16)
    inner_grad, inner_grad2, send, mixed = lax.optimization_barrier(
        (inner_grad, inner_grad2, send, mixed)
    )
    mixed = in_frames(mixed)
    got = exchanged(send)
    keep = t_dot(normed3, inner_grad).astype(bf16)
    inner_grad, keep = lax.optimization_barrier((inner_grad, keep))
    normed3_grad = dot_t(inner_grad, up_halves[0])
    s_up = sums([keep], [got])
    normed3_grad, inner_grad2 = along((normed3_grad, inner_grad2), s_down, s_up)
    normed3_grad = normed3_grad + dot_t(inner_grad2, up_halves[1])
    g_b_down = jnp.sum(down_in.astype(f32), axis=0)
    g_b_up = in_order(
        *[jnp.sum(x.astype(f32), axis=0).reshape(total, -1) for x in (inner_grad, inner_grad2)], 1
    )
    grad2, sums3 = norm_back(hidden2, nothing, gains[2], normed3_grad, down_in, bf16)
    t_in = grad2.reshape(row_count, width)

    def out_grads(mixed_in, grad):
        return [t_dot(mixed_in, x).astype(bf16) for x in halves(grad)]

    g_t_out = out_grads(t_mixed, t_in)
    t_mix_grad = dot_t(t_in, to_full).astype(bf16).reshape(frames, slots_local, width)

    def back(side, where, make, values, grad):
        (out,) = run_attention(
            partial(attention_backward, make, (side,)), *where, [values[side], grad], [3 * half]
        )
        return out.reshape(row_count, -1)

    t_grad2 = back(1, temporal_place, make_bias, temporal, t_mix_grad)
    t_grad2, t_mix_grad, g_t_out = lax.optimization_barrier((t_grad2, t_mix_grad, g_t_out))
    t_mix_grad = along(t_mix_grad, s_down, s_up)
    t_grad = back(0, temporal_place, make_bias, temporal, t_mix_grad)
    t_grad, t_grad2 = lax.optimization_barrier((t_grad, t_grad2))
    normed2_grad = dot_t(t_grad, tq_halves[0]) + dot_t(t_grad2, tq_halves[1])
    grad1, sums2 = norm_back(hidden1, nothing, gains[1], normed2_grad, grad2, bf16)
    grad1, t_grad, t_grad2 = lax.optimization_barrier((grad1, t_grad, t_grad2))
    parts = from_slots(grad1)
    send = t_dot(normed2, t_grad2).astype(bf16)
    send, t_grad = lax.optimization_barrier((send, t_grad))
    t_gots = [exchanged(send), exchanged(g_t_out[1])]
    keep = t_dot(normed2, t_grad).astype(bf16)
    keep = along(keep, s_down, s_up)
    parts[0], keep = lax.optimization_barrier((parts[0], keep))
    s_time = sums([keep, g_t_out[0]], t_gots)
    grad1 = in_frames(parts)
    grad1 = along(grad1, s_time)
    s_in = grad1.reshape(row_count, width)
    g_s_out = out_grads(s_mixed, s_in)
    mix_grad = dot_t(s_in, so_full).astype(bf16).reshape(frames_local, slots, width)
    s_got = exchanged(g_s_out[1])
    mix_grad = along(mix_grad, s_up, s_down)
    s_grad2 = back(1, spatial_place, spatial_bias, spatial, mix_grad)
    mix_grad, s_grad2 = along((mix_grad, s_grad2), s_time, s_up)
    send = t_dot(normed1, s_grad2).astype(bf16)
    mix_grad, send = lax.optimization_barrier((mix_grad, send))
    got = exchanged(send)
    s_grad = back(0, spatial_place, spatial_bias, spatial, mix_grad)
    s_grad = along(s_grad, s_time)
    keep = t_dot(normed1, s_grad).astype(bf16)
    keep, s_grad, s_grad2, s_got = lax.optimization_barrier((keep, s_grad, s_grad2, s_got))
    s_space = sums([keep, g_s_out[0]], [got, s_got])
    s_grad, s_grad2 = along((s_grad, s_grad2), s_space)
    normed1_grad = dot_t(s_grad, sq_halves[0])
    normed1_grad, s_grad2 = along((normed1_grad, s_grad2), s_time)
    normed1_grad = normed1_grad + dot_t(s_grad2, sq_halves[1])
    input_grad, sums1 = norm_back(tokens, embedded, gains[0], normed1_grad, grad1, f32)
    sums1 = along(sums1, s_time, s_space)
    g_actions = jnp.dot(onehot.T, sums1[:, 2], precision=highest)

    terms = [
        g_actions,
        jnp.stack([jnp.sum(x[:, 0], axis=0) for x in (sums1, sums2, sums3)]),
        jnp.stack([jnp.sum(x[:, 1], axis=0) for x in (sums1, sums2, sums3)]),
        g_b_up.reshape(1, -1),
        g_b_down[None],
    ]
    packed = [jnp.moveaxis(x.reshape(x.shape[0], total, -1), 1, 0).reshape(total, -1) for x in terms]
    packed = jnp.concatenate(packed, axis=1)
    packed = jnp.pad(packed, ((0, 0), (0, -packed.shape[1] % LANES)))
    s_small = Chain(scatter_small(place, packed))
    g_w_down = in_order(*finish(s_down), 0).reshape(w_down.shape)
    g_w_up = in_order(*[x.reshape(rows, total, -1) for x in finish(s_up)], 2).reshape(w_up.shape)
    packed, g_w_down, g_w_up = lax.optimization_barrier((packed, g_w_down, g_w_up))
    while not (s_time.done() and s_space.done()):
        for _ in range(2):
            if not s_small.done():
                packed = along(packed, s_small)
        packed = along(packed, *[c for c in (s_space, s_time) if not c.done()])
    summed = finish(s_small)
    t_rows, s_rows = woven(*s_time.result), woven(*s_space.result)
    g_t_qkv, g_t_out = t_rows[:, : 3 * width], t_rows[:, 3 * width :]
    g_s_qkv, g_s_out = s_rows[:, : 3 * width], s_rows[:, 3 * width :]

    sizes = [x.size // total for x in terms]
    starts = [sum(sizes[:i]) for i in range(len(sizes) + 1)]

    def piece(i, count):
        return summed[starts[i] : starts[i + 1]].reshape(count, -1)

    return (
        mixed.reshape(shape),
        input_grad.reshape(shape),
        piece(0, ACTIONS),
        piece(1, 3),
        piece(2, 3),
        g_s_qkv,
        g_s_out,
        g_t_qkv,
        g_t_out,
        g_w_up,
        piece(3, 1).reshape(-1),
        g_w_down,
        piece(4, 1).reshape(-1),
    )


def solution(mesh):
    whole = P(("tm", "clip"), None)
    spread = P(None, ("tm", "clip"))
    frames = P("tm", "clip", None, None)
    vector = P(("tm", "clip"))
    return jax.shard_map(
        on_device,
        mesh=mesh,
        in_specs=(
            frames, P("tm", "clip"), P("clip"), spread, spread, spread, whole, whole, whole,
            whole, whole, vector, whole, vector, frames,
        ),
        out_specs=(
            frames, frames, spread, spread, spread, whole, whole, whole, whole, whole, vector,
            whole, vector,
        ),
        check_vma=False,
    )
```

```python
from functools import partial

import jax
import jax.numpy as jnp
from jax import lax
from jax.experimental import pallas as pl
from jax.experimental.pallas import tpu as pltpu
from jax.sharding import PartitionSpec as P

H = 16
E = 64
ACTIONS = 8
FRAMES = 16
AXES = ("tm", "clip")
LANES = 128
GROUP = 16

negative = -1e30
highest = lax.Precision.HIGHEST
VMEM = 48 * 1024 * 1024
bf16, f32 = jnp.bfloat16, jnp.float32
NO_COST = pl.CostEstimate(flops=0, bytes_accessed=0, transcendentals=0)


class Place:
    def __init__(self):
        tm_size, clip_size = lax.axis_size("tm"), lax.axis_size("clip")
        self.tm_size, self.clip_size, self.total = tm_size, clip_size, tm_size * clip_size
        self.tm = lax.axis_index("tm")
        self.me = self.tm * clip_size + lax.axis_index("clip")
        self.core_bit = clip_size
        self.core = self.bit_of(clip_size)
        clip_bits = [1 << i for i in range(clip_size.bit_length() - 1)]
        tm_bits = [clip_size << i for i in range(tm_size.bit_length() - 1)]
        x, z, y = clip_bits[:-2], clip_bits[-2:], tm_bits[1:]
        self.z = [(b, b) for b in z]
        self.xy = list(zip(x + y, y + x))

    def bit_of(self, bit):
        return (self.me // bit) % 2

    def mine(self, pair):
        return jnp.where(self.core == 0, self.bit_of(pair[0]), self.bit_of(pair[1]))

    def choose(self, pair):
        return jnp.where(self.core == 0, pair[0], pair[1])

    def flip(self, value, pair):
        moves = [(i, i ^ pair[(i // self.core_bit) % 2]) for i in range(self.total)]
        return lax.ppermute(value, AXES, moves)

    def tm_flip(self, value, offset):
        moves = [(i, i ^ (offset * self.clip_size)) for i in range(self.total)]
        return lax.ppermute(value, AXES, moves)


def below(have, bit):
    return sum(1 for b in have if b < bit)


def unscramble(parts, me):
    bit = 1
    while bit < len(parts):
        swap = (me & bit) != 0
        parts = [jnp.where(swap, parts[p ^ bit], parts[p]) for p in range(len(parts))]
        bit *= 2
    return parts


def position(m, value, k):
    m = jnp.int32(m)
    high = lax.shift_left(lax.shift_right_logical(m, k), k + 1)
    return high | lax.shift_left(value, k) | (m & (lax.shift_left(jnp.int32(1), k) - 1))


def merge_body(info_ref, mine_ref, other_ref, out_ref):
    k, value = info_ref[0], info_ref[1]
    for m in range(mine_ref.shape[0]):
        out_ref[position(m, value, k)] = mine_ref[m]
        out_ref[position(m, 1 - value, k)] = other_ref[m]


def column_block(shape):
    blocks, rows, cols = shape
    return cols if blocks * rows * cols <= 512 * 1024 else min(cols, 512)


def merge(mine, other, k, value):
    m, r, n = mine.shape
    block = column_block((2 * m, r, n))
    spec = pl.BlockSpec((m, r, block), lambda j: (0, 0, j))
    return pl.pallas_call(
        merge_body,
        grid=(n // block,),
        in_specs=[pl.BlockSpec(memory_space=pltpu.SMEM), spec, spec],
        out_specs=pl.BlockSpec((2 * m, r, block), lambda j: (0, 0, j)),
        out_shape=jax.ShapeDtypeStruct((2 * m, r, n), mine.dtype),
        compiler_params=pltpu.CompilerParams(vmem_limit_bytes=VMEM),
        cost_estimate=NO_COST,
    )(jnp.stack([jnp.int32(k), value.astype(jnp.int32)]), mine, other)


def part(info_ref, source_ref, send_ref, keep_ref):
    k, value = info_ref[0], info_ref[1]
    for m in range(send_ref.shape[0]):
        for out_ref, at in ((send_ref, 1 - value), (keep_ref, value)):
            out_ref[m] = source_ref[position(m, at, k)].astype(out_ref.dtype)


def split_body(info_ref, a_ref, b_ref, send_ref, keep_ref):
    k, value = info_ref[0], info_ref[1]
    for m in range(send_ref.shape[0]):
        for out_ref, at in ((send_ref, 1 - value), (keep_ref, value)):
            i = position(m, at, k)
            out_ref[m] = (a_ref[i].astype(f32) + b_ref[i].astype(f32)).astype(out_ref.dtype)


def split(a, b, k, value, dtype):
    blocks, r, n = a.shape
    block = column_block(a.shape)
    out = jax.ShapeDtypeStruct((blocks // 2, r, n), dtype)
    return pl.pallas_call(
        split_body,
        grid=(n // block,),
        in_specs=[pl.BlockSpec(memory_space=pltpu.SMEM)]
        + [pl.BlockSpec((blocks, r, block), lambda j: (0, 0, j))] * 2,
        out_specs=[pl.BlockSpec((blocks // 2, r, block), lambda j: (0, 0, j))] * 2,
        out_shape=[out, out],
        compiler_params=pltpu.CompilerParams(vmem_limit_bytes=VMEM),
        cost_estimate=NO_COST,
    )(jnp.stack([jnp.int32(k), value.astype(jnp.int32)]), a, b)


def gather_small(place, value):
    core = (place.core_bit, place.core_bit)
    x_and_y = [(b, b) for b, _ in place.xy]
    count = len(x_and_y) // 2
    blocks, have = value[None], []
    for pair in x_and_y[:count] + [core] + x_and_y[count:] + place.z:
        (send,) = yield [blocks]
        (got,) = yield [place.flip(send, pair)]
        blocks = merge(blocks, got, below(have, pair[0]), place.bit_of(pair[0]))
        have.append(pair[0])
    return blocks


def scatter_small(place, value):
    bit = place.total // 2
    while bit:
        low_half, high_half = value[:bit], value[bit:]
        mine = (place.me & bit) != 0
        keep = jnp.where(mine, high_half, low_half)
        (send,) = yield [jnp.where(mine, low_half, high_half)]
        (got,) = yield [place.flip(send, (bit, bit))]
        value = keep + got
        bit //= 2
    return value[0]


def gather(place, keep, send):
    core = (place.core_bit, place.core_bit)
    have = ([], [])
    blocks, out = keep[None], send[None]
    for pair in [core] + place.z[::-1] + place.xy:
        (out,) = yield [out]
        (got,) = yield [place.flip(out, pair)]
        k = [below(h, b) for h, b in zip(have, pair)]
        blocks = out = merge(blocks, got, place.choose(k), place.mine(pair))
        have = (have[0] + [pair[0]], have[1] + [pair[1]])
    (out,) = yield [out]
    (got,) = yield [place.flip(out, core)]
    return blocks, got


def scatter(place, first):
    core = (place.core_bit, place.core_bit)
    bits = [1 << i for i in range(place.total.bit_length() - 1)]
    have, pairs = (bits, bits), None
    for pair in place.xy[::-1] + place.z + [core]:
        have = tuple([b for b in h if b != bit] for h, bit in zip(have, pair))
        k = place.choose([below(h, b) for h, b in zip(have, pair)])
        dtype = f32 if pair == core else bf16
        if pairs is None:
            send, keep = first(k, place.mine(pair))
        else:
            send, keep = split(*pairs, k, place.mine(pair), dtype)
        (send,) = yield [send]
        (got,) = yield [place.flip(send, pair)]
        pairs = (keep, got)
    return keep[0], got[0]


class Chain:
    def __init__(self, steps):
        self.steps, self.flying, self.result = steps, False, None
        self.pending = next(steps)

    def done(self):
        return self.result is not None

    def move(self):
        try:
            self.pending = self.steps.send(self.pending)
        except StopIteration as stop:
            self.result = stop.value
        self.flying = not self.flying


def land(value, *chains, also=()):
    chains = [c for c in chains if c.flying]
    value, got, also = lax.optimization_barrier((value, [c.pending for c in chains], list(also)))
    for c, g in zip(chains, got):
        c.pending = g
        c.move()
    return (value, *also) if also else value


def launch(value, *chains, also=()):
    chains = [c for c in chains if not c.done() and not c.flying]
    value, sent, also = lax.optimization_barrier((value, [c.pending for c in chains], list(also)))
    for c, g in zip(chains, sent):
        c.pending = g
        c.move()
    return (value, *also) if also else value


def along(value, *chains):
    return launch(land(value, *chains), *chains)


def finish(chain):
    while not chain.done():
        chain.move()
    return chain.result


def spatial_bias(scalar, rows, keys):
    key = lax.broadcasted_iota(jnp.int32, (1, rows) if keys == 1 else (rows, 1), keys)
    return jnp.where(key < scalar * scalar, 0.0, negative)


def temporal_bias(frames_local, scalar, rows, keys):
    def place(axis):
        index = lax.broadcasted_iota(jnp.int32, (rows, rows), axis)
        slot, at = index % GROUP, index // GROUP
        frame = ((at // frames_local) ^ scalar) * frames_local + at % frames_local
        return slot, frame

    slot_q, frame_q = place(1 - keys)
    slot_k, frame_k = place(keys)
    return jnp.where((slot_q == slot_k) & (frame_q >= frame_k), 0.0, negative)


def dot_t(a, b):
    return lax.dot_general(a, b, (((1,), (1,)), ((), ())), preferred_element_type=f32)


def t_dot(a, b):
    return lax.dot_general(a, b, (((0,), (0,)), ((), ())), preferred_element_type=f32)


def columns(scalar_ref, side, start):
    half = H * E // 2
    return pl.ds(pl.multiple_of((scalar_ref[1] ^ side) * half + start, LANES), LANES)


def two_heads(rows):
    half = lax.broadcasted_iota(jnp.int32, (rows, LANES), 1) < E

    def apart(x):
        return jnp.concatenate([jnp.where(half, x, 0), jnp.where(half, 0, x)], axis=0)

    def together(x):
        return jnp.where(half, x[:rows], x[rows:])

    return apart, together


def attention_forward(make_bias, scalar_ref, own_ref, other_ref, out_ref):
    a, b, width = own_ref.shape
    rows, width = a * b, width // 3
    bias = make_bias(scalar_ref[0], rows, 1)
    apart, together = two_heads(rows)
    factor = E ** (-0.5)
    for side, qkv_ref in enumerate((own_ref, other_ref)):
        for c in range(0, width, LANES):
            q = qkv_ref[:, :, c : c + LANES].reshape(rows, LANES) * bf16(factor)
            k = qkv_ref[:, :, width + c : width + c + LANES].reshape(rows, LANES)
            v = qkv_ref[:, :, 2 * width + c : 2 * width + c + LANES].reshape(rows, LANES)
            scores = dot_t(apart(q), k).reshape(2, rows, rows) + bias[None]
            weights = jnp.exp(scores - jnp.max(scores, axis=2, keepdims=True))
            scale = 1.0 / jnp.sum(weights, axis=2, keepdims=True)
            weights = weights.astype(bf16).reshape(2 * rows, rows)
            mixed = jnp.dot(weights, v, preferred_element_type=f32)
            mixed = together(mixed * scale.reshape(2 * rows, 1)).astype(out_ref.dtype)
            out_ref[:, :, columns(scalar_ref, side, c)] = mixed.reshape(a, b, LANES)


def attention_backward(make_bias, sides, scalar_ref, *refs):
    grad_ref = refs[len(sides)]
    a, b, width = refs[0].shape
    rows, width = a * b, width // 3
    bias = make_bias(scalar_ref[0], rows, 0)
    apart, together = two_heads(rows)
    factor = E ** (-0.5)
    for i, side in enumerate(sides):
        qkv_ref, out_ref = refs[i], refs[len(sides) + 1 + i]
        for c in range(0, width, LANES):
            q = qkv_ref[:, :, c : c + LANES].reshape(rows, LANES) * bf16(factor)
            k = qkv_ref[:, :, width + c : width + c + LANES].reshape(rows, LANES)
            v = qkv_ref[:, :, 2 * width + c : 2 * width + c + LANES].reshape(rows, LANES)
            g = grad_ref[:, :, columns(scalar_ref, side, c)].reshape(rows, LANES)
            scores = dot_t(apart(k), q).reshape(2, rows, rows) + bias[None]
            weights = jnp.exp(scores - jnp.max(scores, axis=1, keepdims=True))
            probs = weights * (1.0 / jnp.sum(weights, axis=1, keepdims=True))
            prob_grad = dot_t(apart(v), g).reshape(2, rows, rows)
            delta = jnp.sum(probs * prob_grad, axis=1, keepdims=True)
            score_grad = (probs * (prob_grad - delta)).astype(bf16)
            turned = jnp.concatenate([score_grad[0].T, score_grad[1].T], axis=0)
            dq = jnp.dot(turned, k, preferred_element_type=f32) * factor
            dk = jnp.dot(score_grad.reshape(2 * rows, rows), q, preferred_element_type=f32)
            dv = jnp.dot(
                probs.astype(bf16).reshape(2 * rows, rows), g, preferred_element_type=f32
            )
            for index, grad in enumerate((dq, dk, dv)):
                start = index * width + c
                merged = together(grad).astype(out_ref.dtype)
                out_ref[:, :, start : start + LANES] = merged.reshape(a, b, LANES)


def run_attention(body, scalars, block, grid, index, inputs, out_widths):
    a, b = block
    outer = inputs[0].shape[:2]
    return pl.pallas_call(
        body,
        grid=(grid,),
        in_specs=[pl.BlockSpec(memory_space=pltpu.SMEM)]
        + [pl.BlockSpec((a, b, x.shape[-1]), index) for x in inputs],
        out_specs=[pl.BlockSpec((a, b, width), index) for width in out_widths],
        out_shape=[jax.ShapeDtypeStruct((*outer, width), bf16) for width in out_widths],
        compiler_params=pltpu.CompilerParams(vmem_limit_bytes=VMEM),
        cost_estimate=NO_COST,
    )(scalars, *inputs)


def centre(x):
    average = jnp.mean(x, axis=-1, keepdims=True)
    centered = x - average
    variance = jnp.mean(centered * centered, axis=-1, keepdims=True)
    scale = lax.rsqrt(variance + 1e-05)
    return centered * scale, scale


def norm_body(x_ref, added_ref, gain_ref, shift_ref, out_ref):
    unit, _ = centre(x_ref[0].astype(f32) + added_ref[0])
    out_ref[0] = (unit * gain_ref[...] + shift_ref[...]).astype(out_ref.dtype)


def by_rows(body, arrays, rows, outs):
    blocks = arrays[0].shape[0]
    specs = []
    for x in arrays:
        if x.ndim == 2:
            specs.append(pl.BlockSpec(x.shape, lambda i: (0, 0)))
        else:
            at = (lambda i: (i, 0, 0)) if x.shape[0] == blocks else (lambda i: (0, 0, 0))
            specs.append(pl.BlockSpec((1, *x.shape[1:]), at))
    return pl.pallas_call(
        body,
        grid=(blocks,),
        in_specs=specs,
        out_specs=[pl.BlockSpec((1, *shape[1:]), lambda i: (i, 0, 0)) for shape, _ in outs],
        out_shape=[jax.ShapeDtypeStruct(shape, dtype) for shape, dtype in outs],
        compiler_params=pltpu.CompilerParams(vmem_limit_bytes=VMEM),
        cost_estimate=NO_COST,
    )(*arrays)


def norm(x, added, gain, shift):
    shape = (x.shape[0] * x.shape[1] // 256, 256, x.shape[2])
    arrays = [x.reshape(shape), added, gain[None], shift[None]]
    (out,) = by_rows(norm_body, arrays, 256, [(shape, bf16)])
    return out.reshape(-1, shape[2])


BLOCK = 512


def dense(body, grid, scalars, inputs, outs, scratch=()):
    return pl.pallas_call(
        body,
        grid_spec=pltpu.PrefetchScalarGridSpec(
            num_scalar_prefetch=1,
            grid=grid,
            in_specs=[pl.BlockSpec(block, index) for _, block, index in inputs],
            out_specs=[pl.BlockSpec(block, index) for _, _, block, index in outs],
            scratch_shapes=list(scratch),
        ),
        out_shape=[jax.ShapeDtypeStruct(shape, dtype) for shape, dtype, _, _ in outs],
        compiler_params=pltpu.CompilerParams(vmem_limit_bytes=VMEM),
        cost_estimate=NO_COST,
    )(scalars, *[x for x, _, _ in inputs])


def at(*index):
    return lambda j, ref: index


def whole(x):
    return (x, x.shape, at(*[0] * x.ndim))


def rows_of(x, rows=256):
    return (x, (rows, x.shape[1]), lambda i, ref: (i, 0))


def project_body(_, x_ref, w_ref, out_ref):
    out_ref[...] = jnp.dot(x_ref[...], w_ref[...], preferred_element_type=f32).astype(bf16)


def project(x, w, cols, scalars):
    index = lambda j, ref: (0, j)
    rows = x.shape[0]
    (out,) = dense(
        project_body, (cols // BLOCK,), scalars,
        [whole(x), (w, (w.shape[0], BLOCK), index)],
        [((rows, cols), bf16, (rows, BLOCK), index)],
    )
    return out


def sides(core, own_ref, other_ref):
    for side, ref in ((core, own_ref), (1 - core, other_ref)):
        yield pl.ds(pl.multiple_of(side * BLOCK, BLOCK), BLOCK), ref


def hidden1_body(core_ref, mixed_ref, own_ref, other_ref, x_ref, added_ref, out_ref):
    for cols, w_ref in sides(core_ref[0], own_ref, other_ref):
        dot = jnp.dot(mixed_ref[...], w_ref[...], preferred_element_type=f32)
        out_ref[:, cols] = (x_ref[:, cols].astype(f32) + added_ref[0, :, cols] + dot).astype(bf16)


def out_half(w):
    return (w, (w.shape[0], BLOCK), at(0, w.shape[1] // BLOCK - 1))


def add_spatial(mixed, halves, x, added, scalars):
    rows, width = x.shape
    step = rows // added.shape[0]
    (out,) = dense(
        hidden1_body, (rows // step,), scalars,
        [rows_of(mixed, step), *[out_half(w) for w in halves], rows_of(x, step),
         (added, (1, 1, width), lambda i, ref: (i, 0, 0))],
        [((rows, width), bf16, (step, width), lambda i, ref: (i, 0))],
    )
    return out


def hidden2_body(
    core_ref, mixed_ref, own_ref, other_ref, x_ref, gain_ref, shift_ref, out_ref, norm_ref
):
    for cols, w_ref in sides(core_ref[0], own_ref, other_ref):
        dot = jnp.dot(mixed_ref[...], w_ref[...], preferred_element_type=f32)
        out_ref[:, cols] = x_ref[:, cols].astype(f32) + dot
    unit, _ = centre(out_ref[...])
    norm_ref[...] = (unit * gain_ref[...] + shift_ref[...]).astype(bf16)


def add_temporal(mixed, halves, x, gain, shift, scalars):
    rows, width = x.shape
    block = ((256, width), lambda i, ref: (i, 0))
    return dense(
        hidden2_body, (rows // 256,), scalars,
        [rows_of(mixed), *[out_half(w) for w in halves], rows_of(x), whole(gain[None]),
         whole(shift[None])],
        [((rows, width), f32, *block), ((rows, width), bf16, *block)],
    )


def hidden3_body(_, a_ref, b_ref, own_ref, other_ref, x_ref, bias_ref, mask_ref, out_ref):
    out = x_ref[...] + bias_ref[...]
    out += jnp.dot(a_ref[...], own_ref[...], preferred_element_type=f32)
    out += jnp.dot(b_ref[...], other_ref[...], preferred_element_type=f32)
    out_ref[...] = jnp.where(mask_ref[...] > 0, out, 0).astype(bf16)


def down_project(actives, halves, x, bias, mask, scalars):
    rows, width = x.shape
    (out,) = dense(
        hidden3_body, (rows // 256,), scalars,
        [*[rows_of(y) for y in actives], *[whole(w) for w in halves], rows_of(x), whole(bias),
         rows_of(mask)],
        [((rows, width), bf16, (256, width), lambda i, ref: (i, 0))],
    )
    return out


def inner_back_body(_, x_ref, w_ref, slope_ref, out_ref, sum_ref):
    grad = dot_t(x_ref[...], w_ref[...]) * slope_ref[...].astype(f32)
    out_ref[...] = grad.astype(bf16)
    sum_ref[...] = jnp.sum(out_ref[...].astype(f32), axis=0, keepdims=True)


def inner_back(x, w, slope, scalars):
    rows, cols = slope.shape
    index = lambda j, ref: (0, j)
    return dense(
        inner_back_body, (cols // BLOCK,), scalars,
        [whole(x), (w, (BLOCK, w.shape[1]), lambda j, ref: (j, 0)), (slope, (rows, BLOCK), index)],
        [((rows, cols), bf16, (rows, BLOCK), index), ((1, cols), f32, (1, BLOCK), index)],
    )


def norm_back_body(
    _, a_ref, b_ref, own_ref, other_ref, x_ref, added_ref, gain_ref, rest_ref, out_ref, sums_ref
):
    grad = dot_t(a_ref[...], own_ref[...]) + dot_t(b_ref[...], other_ref[...])
    unit, scale = centre(x_ref[...].astype(f32) + added_ref[0])
    scaled = grad * gain_ref[...]
    first = jnp.mean(scaled, axis=-1, keepdims=True)
    second = jnp.mean(scaled * unit, axis=-1, keepdims=True)
    out = rest_ref[...].astype(f32) + scale * (scaled - first - unit * second)
    out_ref[...] = out.astype(out_ref.dtype)
    terms = (grad * unit, grad, out)
    sums_ref[0] = jnp.concatenate([jnp.sum(x, axis=0, keepdims=True) for x in terms], axis=0)


def norm_back(grads, halves, x, added, gain, rest, dtype, scalars):
    rows, width = x.shape
    step, cols = 256, grads[0].shape[1]
    added_at = (lambda i, ref: (i, 0, 0)) if added.shape[0] > 1 else at(0, 0, 0)
    return dense(
        norm_back_body, (rows // step,), scalars,
        [*[rows_of(g) for g in grads], *[(w, (w.shape[0], cols), at(0, 0)) for w in halves],
         rows_of(x), (added, (1, 1, width), added_at), whole(gain[None]), rows_of(rest)],
        [((rows, width), dtype, (step, width), lambda i, ref: (i, 0)),
         ((rows // step, 3, width), f32, (1, 3, width), lambda i, ref: (i, 0, 0))],
    )


def mixed_back_body(core_ref, x_ref, own_ref, other_ref, out_ref):
    grad = 0
    for cols, w_ref in sides(core_ref[0], own_ref, other_ref):
        grad += dot_t(x_ref[:, cols], w_ref[...])
    out_ref[...] = grad.astype(bf16)


def mixed_back(x, halves, scalars):
    rows, width = x.shape
    last = halves[0].shape[1] // BLOCK - 1
    (out,) = dense(
        mixed_back_body, (width // BLOCK,), scalars,
        [whole(x), *[(w, (BLOCK, BLOCK), lambda j, ref: (j, last)) for w in halves]],
        [((rows, width), bf16, (rows, BLOCK), lambda j, ref: (0, j))],
    )
    return out


def weight_grad_body(_, x_ref, y_ref, out_ref):
    out_ref[...] = t_dot(x_ref[...], y_ref[...]).astype(bf16).reshape(out_ref.shape)


def weight_grad(x, y, total, scalars, half=None):
    rows, count = x.shape
    cols = y.shape[1] if half is None else BLOCK
    shift = (lambda j, ref: (0, j)) if half is None else (lambda j, ref: (0, ref[0] ^ half))
    shape = (total, count // total)
    (out,) = dense(
        weight_grad_body, (cols // BLOCK,), scalars,
        [whole(x), (y, (rows, BLOCK), shift)],
        [((*shape, cols), bf16, (*shape, BLOCK), lambda j, ref: (0, 0, j))],
    )
    return out


def weight_split_body(ends, info_ref, *refs):
    send_ref, keep_ref, sum_ref = refs[-3:]
    step = pl.program_id(0)
    for p in range(len(ends) - 1):

        @pl.when((step >= ends[p]) & (step < ends[p + 1]))
        def _(x_ref=refs[3 * p], y_ref=refs[3 * p + 1], got_ref=refs[3 * p + 2]):
            grad = t_dot(x_ref[...], y_ref[...]).reshape(sum_ref.shape)
            sum_ref[...] = grad + got_ref[...].astype(f32)

    part(info_ref, sum_ref, send_ref, keep_ref)


def weight_split(parts, k, value, core):
    scalars = jnp.stack([jnp.int32(k), value.astype(jnp.int32), core.astype(jnp.int32)])
    total, r, _ = parts[0][2].shape
    widths = [got.shape[2] for _, _, got, _ in parts]
    ends = [sum(widths[:i]) // BLOCK for i in range(len(parts) + 1)]
    inputs = []
    for (x, y, got, half), low, high in zip(parts, ends[:-1], ends[1:]):
        place = lambda j, low=low, high=high: jnp.clip(j - low, 0, high - low - 1)
        if half is None:
            index = lambda j, ref, place=place: (0, place(j))
        else:
            index = lambda j, ref, half=half: (0, ref[2] ^ half)
        inputs += [
            whole(x),
            (y, (y.shape[0], BLOCK), index),
            (got, (total, r, BLOCK), lambda j, ref, place=place: (0, 0, place(j))),
        ]
    shape = (total // 2, r)
    out = ((*shape, sum(widths)), bf16, (*shape, BLOCK), lambda j, ref: (0, 0, j))
    return dense(
        partial(weight_split_body, ends), (ends[-1],), scalars, inputs, [out, out],
        [pltpu.VMEM((total, r, BLOCK), f32)],
    )


TAIL = (
    0.14760860800743103, 0.14761532843112946, 0.127163827419281, 0.09018292278051376,
    0.013407237827777863, 0.06451446563005447, -0.19429759681224823, 0.13513216376304626,
    -0.031326886266469955,
)


def gelu(inner):
    size = jnp.abs(inner)
    t = 1.0 / (1.0 + 0.37 * size)
    bell = jnp.exp(inner * inner * -0.5)
    series = TAIL[-1]
    for term in reversed(TAIL[:-1]):
        series = series * t + term
    tail = series * t * bell
    cdf = jnp.where(inner > 0, 1.0 - tail, tail)
    return inner * cdf, cdf + inner * bell * 0.3989422804014327


def up_body(x_ref, w_ref, bias_ref, active_ref, slope_ref):
    rows = x_ref.shape[0]
    step = min(rows, 128)
    for r in range(0, rows, step):
        inner = jnp.dot(x_ref[r : r + step], w_ref[...], preferred_element_type=f32)
        active, slope = gelu(inner + bias_ref[...])
        active_ref[r : r + step] = active.astype(active_ref.dtype)
        slope_ref[r : r + step] = slope.astype(slope_ref.dtype)


def up_project(x, weight, bias):
    rows, width = x.shape
    cols, block = weight.shape[1], 512
    out = jax.ShapeDtypeStruct((rows, cols), bf16)
    return pl.pallas_call(
        up_body,
        grid=(cols // block,),
        in_specs=[
            pl.BlockSpec((rows, width), lambda i: (0, 0)),
            pl.BlockSpec((width, block), lambda i: (0, i)),
            pl.BlockSpec((1, block), lambda i: (0, i)),
        ],
        out_specs=[pl.BlockSpec((rows, block), lambda i: (0, i))] * 2,
        out_shape=[out, out],
        compiler_params=pltpu.CompilerParams(vmem_limit_bytes=VMEM),
        cost_estimate=NO_COST,
    )(x, weight, bias)


def on_device(
    tokens,
    actions,
    sides,
    action_table,
    norm_gains,
    norm_shifts,
    s_qkv,
    s_out,
    t_qkv,
    t_out,
    w_up,
    b_up,
    w_down,
    b_down,
    grad_out,
):
    shape = tokens.shape
    frames_local, _, slots, width = shape
    place = Place()
    total, core, tm_size = place.total, place.core, place.tm_size
    slots_local = slots // tm_size
    row_count = frames_local * slots
    half = width // 2

    def to_slots(value):
        view = value.reshape(frames_local, tm_size, slots_local, value.shape[-1])
        parts = []
        for o in range(tm_size):
            part = lax.dynamic_index_in_dim(view, place.tm ^ o, 1, keepdims=False)
            parts.append(place.tm_flip(part, o) if o else part)
        return parts

    def from_slots(value):
        view = value.reshape(tm_size, frames_local, slots_local, value.shape[-1])
        return [place.tm_flip(view[o], o) if o else view[o] for o in range(tm_size)]

    def in_slots(parts):
        return jnp.concatenate(parts, axis=0)

    def in_frames(parts):
        return jnp.stack(unscramble(parts, place.tm), axis=1).reshape(frames_local, slots, -1)

    def own_and_other(value, axis):
        first, second = (lax.index_in_dim(value, i, axis, keepdims=False) for i in (0, 1))
        return jnp.where(core == 0, first, second), jnp.where(core == 0, second, first)

    def in_order(own, other, axis):
        pair = [jnp.where(core == 0, own, other), jnp.where(core == 0, other, own)]
        return jnp.stack(pair, axis=axis)

    def woven(own, other):
        cuts = [slice(i, i + half) for i in range(0, own.shape[1], half)]
        own_first = [x[:, cut] for cut in cuts for x in (own, other)]
        other_first = [x[:, cut] for cut in cuts for x in (other, own)]
        return jnp.where(
            core == 0,
            jnp.concatenate(own_first, axis=1),
            jnp.concatenate(other_first, axis=1),
        )

    thin = width // total
    counts = [ACTIONS, 3, 3, 1]
    ends = [sum(counts[:i]) for i in range(len(counts) + 1)]
    rows = s_qkv.shape[0]
    hidden_half = w_down.shape[0] // 2

    def attention_group(qkv, out):
        qkv = own_and_other(qkv.reshape(rows, 3, 2, half), 2)
        both = [
            jnp.concatenate([a.reshape(rows, 3 * half), b], axis=1)
            for a, b in zip(qkv, own_and_other(out.reshape(rows, 2, half), 1))
        ]
        return Chain(gather(place, *both))

    front = attention_group(s_qkv, s_out)
    tokens = along(tokens, front)
    rows_in = (action_table, norm_gains, norm_shifts, b_down)
    tokens, rows_in, b_up, grad_out = lax.optimization_barrier((tokens, rows_in, b_up, grad_out))
    action_table, norm_gains, norm_shifts, b_down = rows_in
    small = jnp.concatenate([action_table, norm_gains, norm_shifts, b_down[None]], axis=0).T
    small = jnp.pad(small, ((0, 0), (0, LANES - ends[-1])))
    b_up = jnp.pad(b_up[None], ((0, GROUP - 1), (0, LANES - b_up.shape[0])))
    small = jnp.concatenate([small, b_up], axis=0)
    tokens = along(tokens, front)
    tokens, grad_out = lax.optimization_barrier((tokens, grad_out))
    cotangent = to_slots(grad_out.reshape(frames_local, slots, width))
    small = Chain(gather_small(place, small))
    tokens = along(tokens, small)
    tokens = along(tokens, small)
    tokens, t_qkv, t_out = lax.optimization_barrier((tokens, t_qkv, t_out))
    tokens = along(tokens, front)
    middle = attention_group(t_qkv, t_out)
    tokens = along(tokens, middle)
    tokens, cotangent = lax.optimization_barrier((tokens, cotangent))
    tokens = along(tokens, front, middle)
    tokens = along(tokens, small)
    tokens = along(tokens, small)
    tokens = along(tokens, front, middle)
    while not small.done():
        tokens = along(tokens, small)
    tokens, w_up, w_down = lax.optimization_barrier((tokens, w_up, w_down))
    up_pair = own_and_other(w_up.reshape(rows, total, 2, hidden_half), 2)
    rising = Chain(gather(place, *[x.reshape(rows, -1) for x in up_pair]))
    falling = Chain(gather(place, *own_and_other(w_down.reshape(2, hidden_half, width), 0)))
    small = small.result.astype(f32)
    table = small[:, :thin].reshape(width, LANES).T

    def unpack(i):
        return table[ends[i] : ends[i + 1]]

    action_rows, gains, shifts, down_bias = [unpack(i) for i in range(4)]
    up_bias = small[:, thin, : 2 * hidden_half].reshape(total, 2, hidden_half)
    up_bias = [x.reshape(1, -1) for x in own_and_other(up_bias, 1)]

    onehot = (actions == jnp.arange(ACTIONS)[None, :]).astype(f32)
    embedded = jnp.dot(onehot, action_rows, precision=highest)
    tokens = tokens.reshape(frames_local, slots, width)
    embedded = embedded[:, None, :]
    normed1 = norm(tokens, embedded, gains[0], shifts[0])
    normed1 = along(normed1, front, middle, rising)
    s_halves = [x.reshape(width, -1) for x in finish(front)]
    here = core.astype(jnp.int32).reshape(1)

    def projected(x, w, outer):
        return project(x, w, 3 * half, here).reshape(*outer, -1)

    spatial = [projected(normed1, w, (frames_local, slots)) for w in s_halves]
    spatial = along(spatial, middle, rising)

    def frame_index(i):
        return (i, 0, 0)

    def slot_index(i):
        return (0, i, 0)

    spatial_place = (
        jnp.stack([sides[0], core.astype(jnp.int32)]), (1, slots), frames_local, frame_index,
    )
    (s_mixed,) = run_attention(
        partial(attention_forward, spatial_bias), *spatial_place, spatial, [width]
    )
    s_mixed = s_mixed.reshape(row_count, width)
    flat = tokens.reshape(row_count, width)
    hidden1 = add_spatial(s_mixed, s_halves, flat, embedded, here)

    hidden1 = along(hidden1, middle, rising, falling)
    parts = to_slots(hidden1.reshape(tokens.shape))
    parts = land(parts, middle, rising, falling)
    hidden1 = in_slots(parts)
    frames = hidden1.shape[0]
    slot_at = place.tm * slots_local + jnp.arange(slots_local)
    mask = (slot_at < sides[0] * sides[0])[None, :, None]
    nothing = jnp.zeros((1, 1, width), f32)
    normed2 = norm(hidden1, nothing, gains[1], shifts[1])
    hidden1 = hidden1.reshape(row_count, width)
    normed2 = launch(normed2, rising, falling)
    t_halves = [x.reshape(width, -1) for x in finish(middle)]
    temporal = [projected(normed2, w, (frames, slots_local)) for w in t_halves]
    temporal = along(temporal, rising, falling)
    temporal_place = (
        jnp.stack([place.tm.astype(jnp.int32), core.astype(jnp.int32)]), (frames, GROUP),
        slots_local // GROUP, slot_index,
    )
    make_bias = partial(temporal_bias, frames_local)
    (t_mixed,) = run_attention(
        partial(attention_forward, make_bias), *temporal_place, temporal, [width]
    )
    t_mixed = t_mixed.reshape(row_count, width)
    hidden2, normed3 = add_temporal(t_mixed, t_halves, hidden1, gains[2], shifts[2], here)
    normed3 = along(normed3, rising, falling)
    up_halves = [x.reshape(width, -1) for x in finish(rising)]
    first = up_project(normed3, up_halves[0], up_bias[0])
    first = along(first, falling)
    normed3, first = lax.optimization_barrier((normed3, first))
    second = up_project(normed3, up_halves[1], up_bias[1])
    second = along(second, falling)
    (active, slope), (active2, slope2) = first, second

    core_pair = (place.core_bit, place.core_bit)

    def exchanged(grad):
        return place.flip(grad, core_pair)

    def sums(*parts):
        return Chain(scatter(place, lambda k, value: weight_split(parts, k, value, core)))

    down_in = jnp.where(mask, in_slots(cotangent), 0).reshape(row_count, width)
    send = weight_grad(active2, down_in, total, here)
    hidden2 = land(hidden2, falling)
    down_halves = [x.reshape(-1, width) for x in finish(falling)]
    hidden2, send = launch(hidden2, also=[send])
    got = exchanged(send)
    mask_rows = jnp.broadcast_to(mask, (frames, slots_local, 1)).reshape(row_count, 1).astype(f32)
    mixed = down_project([active, active2], down_halves, hidden2, down_bias, mask_rows, here)
    down_in, mixed, got = lax.optimization_barrier((down_in, mixed, got))
    s_down = sums((active, down_in, got, None))
    down_in = launch(down_in, s_down)

    inner_grad, b_sum = inner_back(down_in, down_halves[0], slope, here)
    inner_grad2, b_sum2 = inner_back(down_in, down_halves[1], slope2, here)
    send = weight_grad(normed3, inner_grad2, total, here)
    inner_grad, inner_grad2, send = land((inner_grad, inner_grad2, send), s_down)
    inner_grads, send = launch((inner_grad, inner_grad2), s_down, also=[send])
    got = exchanged(send)

    grad2, sums3 = norm_back(
        inner_grads, up_halves, hidden2, nothing, gains[2], down_in, bf16, here
    )
    t_mix_grad = mixed_back(grad2, t_halves, here)
    t_mix_grad, got = land(t_mix_grad, s_down, also=[got])
    s_up = sums((normed3, inner_grads[0], got, None))
    t_mix_grad = launch(t_mix_grad, s_down, s_up)
    t_mix_grad = t_mix_grad.reshape(frames, slots_local, width)

    def back(side, where, make, values, grad):
        (out,) = run_attention(
            partial(attention_backward, make, (side,)), *where, [values[side], grad], [3 * half]
        )
        return out.reshape(row_count, -1)

    t_grad2 = back(1, temporal_place, make_bias, temporal, t_mix_grad)
    send = weight_grad(normed2, t_grad2, total, here)
    send2 = weight_grad(t_mixed, grad2, total, here, 1)
    t_grad = back(0, temporal_place, make_bias, temporal, t_mix_grad)
    t_grads = land((t_grad, t_grad2), s_down, s_up)
    t_grads, send, send2 = launch(t_grads, s_down, s_up, also=[send, send2])
    gots = [exchanged(send), exchanged(send2)]

    grad1, sums2 = norm_back(t_grads, t_halves, hidden1, nothing, gains[1], grad2, bf16, here)
    grad1, *gots = land(grad1, s_down, s_up, also=gots)
    grad1 = launch(grad1, s_down, s_up)
    parts = from_slots(grad1)
    s_time = sums((normed2, t_grads[0], gots[0], None), (t_mixed, grad2, gots[1], 0))
    parts[0], s_time.pending = lax.optimization_barrier((parts[0], s_time.pending))
    parts = land(parts, s_down, s_up)
    grad1 = in_frames(parts).reshape(row_count, width)
    grad1 = launch(grad1, s_down, s_up, s_time)

    send2 = weight_grad(s_mixed, grad1, total, here, 1)
    mix_grad = mixed_back(grad1, s_halves, here).reshape(frames_local, slots, width)
    s_grad2 = back(1, spatial_place, spatial_bias, spatial, mix_grad)
    send = weight_grad(normed1, s_grad2, total, here)
    mix_grad, send, send2 = land((mix_grad, send, send2), s_down, s_up, s_time)
    mix_grad, send, send2 = launch(mix_grad, s_down, s_up, s_time, also=[send, send2])
    gots = [exchanged(send), exchanged(send2)]

    s_grad = back(0, spatial_place, spatial_bias, spatial, mix_grad)
    s_grad, *gots = land(s_grad, s_down, s_up, s_time, also=gots)
    s_space = sums((normed1, s_grad, gots[0], None), (s_mixed, grad1, gots[1], 0))
    s_grads = launch((s_grad, s_grad2), s_time, s_space)

    input_grad, sums1 = norm_back(
        s_grads, s_halves, flat, embedded, gains[0], grad1, f32, here
    )
    sums1, input_grad = land((sums1, input_grad), s_time, s_space)
    sums1, input_grad = launch((sums1, input_grad), s_time, s_space)
    g_actions = jnp.dot(onehot.T, sums1[:, 2], precision=highest)
    sums1, b_sum, b_sum2, down_in, mixed = lax.optimization_barrier(
        (sums1, b_sum, b_sum2, down_in, mixed)
    )
    g_b_down = jnp.sum(down_in.astype(f32), axis=0)
    g_b_up = in_order(*[x.reshape(total, -1) for x in (b_sum, b_sum2)], 1)

    terms = [
        g_actions,
        jnp.stack([jnp.sum(x[:, 0], axis=0) for x in (sums1, sums2, sums3)]),
        jnp.stack([jnp.sum(x[:, 1], axis=0) for x in (sums1, sums2, sums3)]),
        g_b_up.reshape(1, -1),
        g_b_down[None],
    ]
    packed = [jnp.moveaxis(x.reshape(x.shape[0], total, -1), 1, 0).reshape(total, -1) for x in terms]
    packed = jnp.concatenate(packed, axis=1)
    packed = jnp.pad(packed, ((0, 0), (0, -packed.shape[1] % LANES)))
    s_small = Chain(scatter_small(place, packed))
    packed = launch(packed, s_small)
    packed = land(packed, s_time, s_space, s_small)
    packed, mixed = launch((packed, mixed), s_time, s_space, s_small)
    mixed = from_slots(mixed.reshape(frames, slots_local, width))
    g_w_down = in_order(*finish(s_down), 0).reshape(w_down.shape)
    g_w_up = in_order(*[x.reshape(rows, total, -1) for x in finish(s_up)], 2).reshape(w_up.shape)
    packed, g_w_down, g_w_up = lax.optimization_barrier((packed, g_w_down, g_w_up))
    packed = along(packed, s_small)
    packed = along(packed, s_time, s_space, s_small)
    packed, mixed = lax.optimization_barrier((packed, mixed))
    mixed = in_frames(mixed)
    packed = along(packed, s_small)
    while not (s_time.done() and s_space.done() and s_small.done()):
        packed = along(packed, s_time, s_space, s_small)
    summed = s_small.result
    t_rows, s_rows = woven(*s_time.result), woven(*s_space.result)
    g_t_qkv, g_t_out = t_rows[:, : 3 * width], t_rows[:, 3 * width :]
    g_s_qkv, g_s_out = s_rows[:, : 3 * width], s_rows[:, 3 * width :]

    sizes = [x.size // total for x in terms]
    starts = [sum(sizes[:i]) for i in range(len(sizes) + 1)]

    def piece(i, count):
        return summed[starts[i] : starts[i + 1]].reshape(count, -1)

    return (
        mixed.reshape(shape),
        input_grad.reshape(shape),
        piece(0, ACTIONS),
        piece(1, 3),
        piece(2, 3),
        g_s_qkv,
        g_s_out,
        g_t_qkv,
        g_t_out,
        g_w_up,
        piece(3, 1).reshape(-1),
        g_w_down,
        piece(4, 1).reshape(-1),
    )


def solution(mesh):
    whole = P(("tm", "clip"), None)
    spread = P(None, ("tm", "clip"))
    frames = P("tm", "clip", None, None)
    vector = P(("tm", "clip"))
    return jax.shard_map(
        on_device,
        mesh=mesh,
        in_specs=(
            frames, P("tm", "clip"), P("clip"), spread, spread, spread, whole, whole, whole,
            whole, whole, vector, whole, vector, frames,
        ),
        out_specs=(
            frames, frames, spread, spread, spread, whole, whole, whole, whole, whole, vector,
            whole, vector,
        ),
        check_vma=False,
    )
```

```python
import math
from functools import partial

import jax
import jax.numpy as jnp
from jax import lax
from jax.experimental import pallas as pl
from jax.experimental.pallas import tpu as pltpu
from jax.sharding import PartitionSpec as P

H = 16
E = 64
ACTIONS = 8
FRAMES = 16
AXES = ("tm", "clip")
LANES = 128
GROUP = 16

negative = -1e30
highest = lax.Precision.HIGHEST
MIB = 1024 * 1024
bf16, f32 = jnp.bfloat16, jnp.float32
NO_COST = pl.CostEstimate(flops=0, bytes_accessed=0, transcendentals=0)


def params(blocks, margin=6):
    size = sum(math.prod(shape) * jnp.dtype(dtype).itemsize * n for shape, dtype, n in blocks)
    return pltpu.CompilerParams(vmem_limit_bytes=(-(-size // MIB) + margin) * MIB)


class Place:
    def __init__(self):
        tm_size, clip_size = lax.axis_size("tm"), lax.axis_size("clip")
        self.tm_size, self.clip_size, self.total = tm_size, clip_size, tm_size * clip_size
        self.tm = lax.axis_index("tm")
        self.me = self.tm * clip_size + lax.axis_index("clip")
        self.core_bit = clip_size
        self.core = self.bit_of(clip_size)
        clip_bits = [1 << i for i in range(clip_size.bit_length() - 1)]
        tm_bits = [clip_size << i for i in range(tm_size.bit_length() - 1)]
        x, z, y = clip_bits[:-2], clip_bits[-2:], tm_bits[1:]
        self.z = [(b, b) for b in z]
        self.xy = list(zip(x + y, y + x))

    def bit_of(self, bit):
        return (self.me // bit) % 2

    def mine(self, pair):
        return jnp.where(self.core == 0, self.bit_of(pair[0]), self.bit_of(pair[1]))

    def choose(self, pair):
        return jnp.where(self.core == 0, pair[0], pair[1])

    def flip(self, value, pair):
        moves = [(i, i ^ pair[(i // self.core_bit) % 2]) for i in range(self.total)]
        return lax.ppermute(value, AXES, moves)

    def tm_flip(self, value, offset):
        moves = [(i, i ^ (offset * self.clip_size)) for i in range(self.total)]
        return lax.ppermute(value, AXES, moves)


def below(have, bit):
    return sum(1 for b in have if b < bit)


def unscramble(parts, me):
    bit = 1
    while bit < len(parts):
        swap = (me & bit) != 0
        parts = [jnp.where(swap, parts[p ^ bit], parts[p]) for p in range(len(parts))]
        bit *= 2
    return parts


def position(m, value, k):
    m = jnp.int32(m)
    high = lax.shift_left(lax.shift_right_logical(m, k), k + 1)
    return high | lax.shift_left(value, k) | (m & (lax.shift_left(jnp.int32(1), k) - 1))


def merge_body(info_ref, mine_ref, other_ref, out_ref):
    k, value = info_ref[0], info_ref[1]
    for m in range(mine_ref.shape[0]):
        out_ref[position(m, value, k)] = mine_ref[m]
        out_ref[position(m, 1 - value, k)] = other_ref[m]


def column_block(shape):
    blocks, rows, cols = shape
    return cols if blocks * rows * cols <= 512 * 1024 else min(cols, 512)


def merge(mine, other, k, value):
    m, r, n = mine.shape
    block = column_block((2 * m, r, n))
    spec = pl.BlockSpec((m, r, block), lambda j: (0, 0, j))
    return pl.pallas_call(
        merge_body,
        grid=(n // block,),
        in_specs=[pl.BlockSpec(memory_space=pltpu.SMEM), spec, spec],
        out_specs=pl.BlockSpec((2 * m, r, block), lambda j: (0, 0, j)),
        out_shape=jax.ShapeDtypeStruct((2 * m, r, n), mine.dtype),
        compiler_params=params([((4 * m, r, block), mine.dtype, 2)], 2),
        cost_estimate=NO_COST,
    )(jnp.stack([jnp.int32(k), value.astype(jnp.int32)]), mine, other)


def part(info_ref, source_ref, send_ref, keep_ref):
    k, value = info_ref[0], info_ref[1]
    for m in range(send_ref.shape[0]):
        for out_ref, at in ((send_ref, 1 - value), (keep_ref, value)):
            out_ref[m] = source_ref[position(m, at, k)].astype(out_ref.dtype)


def split_body(info_ref, a_ref, b_ref, send_ref, keep_ref):
    k, value = info_ref[0], info_ref[1]
    for m in range(send_ref.shape[0]):
        for out_ref, at in ((send_ref, 1 - value), (keep_ref, value)):
            i = position(m, at, k)
            out_ref[m] = (a_ref[i].astype(f32) + b_ref[i].astype(f32)).astype(out_ref.dtype)


def split(a, b, k, value, dtype):
    blocks, r, n = a.shape
    block = column_block(a.shape)
    out = jax.ShapeDtypeStruct((blocks // 2, r, n), dtype)
    return pl.pallas_call(
        split_body,
        grid=(n // block,),
        in_specs=[pl.BlockSpec(memory_space=pltpu.SMEM)]
        + [pl.BlockSpec((blocks, r, block), lambda j: (0, 0, j))] * 2,
        out_specs=[pl.BlockSpec((blocks // 2, r, block), lambda j: (0, 0, j))] * 2,
        out_shape=[out, out],
        compiler_params=params([((3 * blocks, r, block), dtype, 2)], 3),
        cost_estimate=NO_COST,
    )(jnp.stack([jnp.int32(k), value.astype(jnp.int32)]), a, b)


def gather_small(place, value):
    core = (place.core_bit, place.core_bit)
    x_and_y = [(b, b) for b, _ in place.xy]
    count = len(x_and_y) // 2
    blocks, have = value[None], []
    for pair in x_and_y[:count] + [core] + x_and_y[count:] + place.z:
        (send,) = yield [blocks]
        (got,) = yield [place.flip(send, pair)]
        blocks = merge(blocks, got, below(have, pair[0]), place.bit_of(pair[0]))
        have.append(pair[0])
    return blocks


def scatter_small(place, value):
    bit = place.total // 2
    while bit:
        half = value.shape[1] // 2
        low_half, high_half = value[:, :half], value[:, half:]
        mine = (place.me & bit) != 0
        (send,) = yield [jnp.where(mine, low_half, high_half)]
        (got,) = yield [place.flip(send, (bit, bit))]
        value = jnp.where(mine, high_half, low_half) + got
        bit //= 2
    return value


def gather(place, keep, send, ahead=0):
    core = (place.core_bit, place.core_bit)
    have = ([], [])
    blocks, out = keep[None], send[None]
    for pair in [core] + place.xy[:ahead] + place.z[::-1] + place.xy[ahead:]:
        (out,) = yield [out]
        (got,) = yield [place.flip(out, pair)]
        k = [below(h, b) for h, b in zip(have, pair)]
        blocks = out = merge(blocks, got, place.choose(k), place.mine(pair))
        have = (have[0] + [pair[0]], have[1] + [pair[1]])
    (out,) = yield [out]
    (got,) = yield [place.flip(out, core)]
    return blocks, got


def scatter(place, first):
    core = (place.core_bit, place.core_bit)
    bits = [1 << i for i in range(place.total.bit_length() - 1)]
    have, pairs = (bits, bits), None
    for pair in place.xy[::-1] + place.z + [core]:
        have = tuple([b for b in h if b != bit] for h, bit in zip(have, pair))
        k = place.choose([below(h, b) for h, b in zip(have, pair)])
        dtype = f32 if pair == core else bf16
        if pairs is None:
            send, keep = first(k, place.mine(pair))
        else:
            send, keep = split(*pairs, k, place.mine(pair), dtype)
        (send,) = yield [send]
        (got,) = yield [place.flip(send, pair)]
        pairs = (keep, got)
    return keep[0], got[0]


class Chain:
    def __init__(self, steps):
        self.steps, self.flying, self.result = steps, False, None
        self.pending = next(steps)

    def done(self):
        return self.result is not None

    def move(self):
        try:
            self.pending = self.steps.send(self.pending)
        except StopIteration as stop:
            self.result = stop.value
        self.flying = not self.flying


def land(value, *chains, also=()):
    chains = [c for c in chains if c.flying]
    value, got, also = lax.optimization_barrier((value, [c.pending for c in chains], list(also)))
    for c, g in zip(chains, got):
        c.pending = g
        c.move()
    return (value, *also) if also else value


def launch(value, *chains, also=()):
    chains = [c for c in chains if not c.done() and not c.flying]
    value, sent, also = lax.optimization_barrier((value, [c.pending for c in chains], list(also)))
    for c, g in zip(chains, sent):
        c.pending = g
        c.move()
    return (value, *also) if also else value


def along(value, *chains):
    return launch(land(value, *chains), *chains)


def finish(chain):
    while not chain.done():
        chain.move()
    return chain.result


def spatial_bias(scalar, rows, keys):
    key = lax.broadcasted_iota(jnp.int32, (1, rows) if keys == 1 else (rows, 1), keys)
    return jnp.where(key < scalar * scalar, 0.0, negative)


def temporal_bias(frames_local, scalar, rows, keys):
    def place(axis):
        index = lax.broadcasted_iota(jnp.int32, (rows, rows), axis)
        slot, at = index % GROUP, index // GROUP
        frame = ((at // frames_local) ^ scalar) * frames_local + at % frames_local
        return slot, frame

    slot_q, frame_q = place(1 - keys)
    slot_k, frame_k = place(keys)
    return jnp.where((slot_q == slot_k) & (frame_q >= frame_k), 0.0, negative)


def dot_t(a, b):
    return lax.dot_general(a, b, (((1,), (1,)), ((), ())), preferred_element_type=f32)


def t_dot(a, b):
    return lax.dot_general(a, b, (((0,), (0,)), ((), ())), preferred_element_type=f32)


def columns(scalar_ref, side, start):
    half = H * E // 2
    return pl.ds(pl.multiple_of((scalar_ref[1] ^ side) * half + start, LANES), LANES)


def two_heads(rows):
    half = lax.broadcasted_iota(jnp.int32, (rows, LANES), 1) < E

    def apart(x):
        return jnp.concatenate([jnp.where(half, x, 0), jnp.where(half, 0, x)], axis=0)

    def together(x):
        return jnp.where(half, x[:rows], x[rows:])

    return apart, together


def head_pairs(sides, refs):
    a, b, width = refs[0].shape
    rows, width = a * b, width // 3
    for i, side in enumerate(sides):
        for c in range(0, width, LANES):
            q, k, v = (
                refs[i][:, :, at : at + LANES].reshape(rows, LANES)
                for at in (c, width + c, 2 * width + c)
            )
            yield i, side, c, q * bf16(E ** (-0.5)), k, v


def in_turn(items, first, last):
    waiting = None
    for item in items:
        ready = first(*item)
        if waiting is not None:
            last(*waiting)
        waiting = ready
    last(*waiting)


def attention_forward(make_bias, scalar_ref, own_ref, other_ref, out_ref):
    a, b, width = own_ref.shape
    rows, width = a * b, width // 3
    bias = make_bias(scalar_ref[0], rows, 1)
    apart, together = two_heads(rows)

    def first(i, side, c, q, k, v):
        scores = dot_t(apart(q), k).reshape(2, rows, rows) + bias[None]
        weights = jnp.exp(scores - jnp.max(scores, axis=2, keepdims=True))
        scale = 1.0 / jnp.sum(weights, axis=2, keepdims=True)
        return side, c, v, weights.astype(bf16).reshape(2 * rows, rows), scale

    def last(side, c, v, weights, scale):
        mixed = jnp.dot(weights, v, preferred_element_type=f32) * scale.reshape(2 * rows, 1)
        mixed = together(mixed).astype(out_ref.dtype)
        out_ref[:, :, columns(scalar_ref, side, c)] = mixed.reshape(a, b, LANES)

    in_turn(head_pairs((0, 1), (own_ref, other_ref)), first, last)


def attention_backward(make_bias, sides, scalar_ref, *refs):
    grad_ref = refs[len(sides)]
    a, b, width = refs[0].shape
    rows, width = a * b, width // 3
    bias = make_bias(scalar_ref[0], rows, 0)
    apart, together = two_heads(rows)

    def first(i, side, c, q, k, v):
        g = grad_ref[:, :, columns(scalar_ref, side, c)].reshape(rows, LANES)
        scores = dot_t(apart(k), q).reshape(2, rows, rows) + bias[None]
        prob_grad = dot_t(apart(v), g).reshape(2, rows, rows)
        weights = jnp.exp(scores - jnp.max(scores, axis=1, keepdims=True))
        probs = weights * (1.0 / jnp.sum(weights, axis=1, keepdims=True))
        delta = jnp.sum(probs * prob_grad, axis=1, keepdims=True)
        return i, c, q, k, g, probs.astype(bf16), (probs * (prob_grad - delta)).astype(bf16)

    def last(i, c, q, k, g, probs, score_grad):
        turned = jnp.concatenate([score_grad[0].T, score_grad[1].T], axis=0)
        dq = jnp.dot(turned, k, preferred_element_type=f32) * E ** (-0.5)
        dk = jnp.dot(score_grad.reshape(2 * rows, rows), q, preferred_element_type=f32)
        dv = jnp.dot(probs.reshape(2 * rows, rows), g, preferred_element_type=f32)
        for index, grad in enumerate((dq, dk, dv)):
            start = index * width + c
            merged = together(grad).astype(bf16).reshape(a, b, LANES)
            refs[len(sides) + 1 + i][:, :, start : start + LANES] = merged

    in_turn(head_pairs(sides, refs), first, last)


def run_attention(body, scalars, block, grid, index, inputs, out_widths):
    a, b = block
    outer = inputs[0].shape[:2]
    return pl.pallas_call(
        body,
        grid=(grid,),
        in_specs=[pl.BlockSpec(memory_space=pltpu.SMEM)]
        + [pl.BlockSpec((a, b, x.shape[-1]), index) for x in inputs],
        out_specs=[pl.BlockSpec((a, b, width), index) for width in out_widths],
        out_shape=[jax.ShapeDtypeStruct((*outer, width), bf16) for width in out_widths],
        compiler_params=params(
            [((a, b, width), bf16, 2) for width in (*(x.shape[-1] for x in inputs), *out_widths)], 8
        ),
        cost_estimate=NO_COST,
    )(scalars, *inputs)


def centre(x):
    average = jnp.mean(x, axis=-1, keepdims=True)
    centered = x - average
    variance = jnp.mean(centered * centered, axis=-1, keepdims=True)
    scale = lax.rsqrt(variance + 1e-05)
    return centered * scale, scale


def norm_body(x_ref, added_ref, gain_ref, shift_ref, out_ref):
    unit, _ = centre(x_ref[0].astype(f32) + added_ref[0])
    out_ref[0] = (unit * gain_ref[...] + shift_ref[...]).astype(out_ref.dtype)


def by_rows(body, arrays, rows, outs):
    blocks = arrays[0].shape[0]
    specs = []
    for x in arrays:
        if x.ndim == 2:
            specs.append(pl.BlockSpec(x.shape, lambda i: (0, 0)))
        else:
            at = (lambda i: (i, 0, 0)) if x.shape[0] == blocks else (lambda i: (0, 0, 0))
            specs.append(pl.BlockSpec((1, *x.shape[1:]), at))
    return pl.pallas_call(
        body,
        grid=(blocks,),
        in_specs=specs,
        out_specs=[pl.BlockSpec((1, *shape[1:]), lambda i: (i, 0, 0)) for shape, _ in outs],
        out_shape=[jax.ShapeDtypeStruct(shape, dtype) for shape, dtype in outs],
        compiler_params=params([(x.shape[1:], f32, 4) for x in arrays]),
        cost_estimate=NO_COST,
    )(*arrays)


def norm(x, added, gain, shift):
    shape = (x.shape[0] * x.shape[1] // 256, 256, x.shape[2])
    arrays = [x.reshape(shape), added, gain[None], shift[None]]
    (out,) = by_rows(norm_body, arrays, 256, [(shape, bf16)])
    return out.reshape(-1, shape[2])


BLOCK = 512


def dense(body, grid, scalars, inputs, outs, scratch=(), margin=6):
    used = [(block, x.dtype, 1 if index is FIXED else 2) for x, block, index in inputs]
    used += [(block, dtype, 2) for _, dtype, block, _ in outs]
    used += [(x.shape, x.dtype, 1) for x in scratch]

    def spec(block, index):
        if index is FIXED:
            zeros = (0,) * len(block)
            return pl.BlockSpec(block, lambda *_: zeros, pipeline_mode=pl.Buffered(1))
        return pl.BlockSpec(block, index)

    return pl.pallas_call(
        body,
        grid_spec=pltpu.PrefetchScalarGridSpec(
            num_scalar_prefetch=1,
            grid=grid,
            in_specs=[spec(block, index) for _, block, index in inputs],
            out_specs=[pl.BlockSpec(block, index) for _, _, block, index in outs],
            scratch_shapes=list(scratch),
        ),
        out_shape=[jax.ShapeDtypeStruct(shape, dtype) for shape, dtype, _, _ in outs],
        compiler_params=params(used, margin),
        cost_estimate=NO_COST,
    )(scalars, *[x for x, _, _ in inputs])


FIXED = None


def at(*index):
    return lambda j, ref: index


def whole(x):
    return (x, x.shape, FIXED)


def rows_of(x, rows=256):
    return (x, (rows, x.shape[1]), lambda i, ref: (i, 0))


def project_body(_, x_ref, w_ref, out_ref):
    out_ref[...] = jnp.dot(x_ref[...], w_ref[...], preferred_element_type=f32).astype(bf16)


def project(x, w, cols, scalars):
    index = lambda j, ref: (0, j)
    rows = x.shape[0]
    (out,) = dense(
        project_body, (cols // BLOCK,), scalars,
        [whole(x), (w, (w.shape[0], BLOCK), index)],
        [((rows, cols), bf16, (rows, BLOCK), index)],
    )
    return out


def sides(core, own_ref, other_ref):
    for side, ref in ((core, own_ref), (1 - core, other_ref)):
        yield pl.ds(pl.multiple_of(side * BLOCK, BLOCK), BLOCK), ref


def hidden1_body(core_ref, mixed_ref, own_ref, other_ref, x_ref, added_ref, out_ref):
    for cols, w_ref in sides(core_ref[0], own_ref, other_ref):
        dot = jnp.dot(mixed_ref[...], w_ref[...], preferred_element_type=f32)
        out_ref[:, cols] = (x_ref[:, cols].astype(f32) + added_ref[0, :, cols] + dot).astype(bf16)


def out_half(w):
    return (w, (w.shape[0], BLOCK), at(0, w.shape[1] // BLOCK - 1))


def add_spatial(mixed, halves, x, added, scalars):
    rows, width = x.shape
    step = rows // added.shape[0]
    (out,) = dense(
        hidden1_body, (rows // step,), scalars,
        [rows_of(mixed, step), *[out_half(w) for w in halves], rows_of(x, step),
         (added, (1, 1, width), lambda i, ref: (i, 0, 0))],
        [((rows, width), bf16, (step, width), lambda i, ref: (i, 0))],
    )
    return out


def hidden2_body(
    core_ref, mixed_ref, own_ref, other_ref, x_ref, gain_ref, shift_ref, out_ref, norm_ref
):
    for cols, w_ref in sides(core_ref[0], own_ref, other_ref):
        dot = jnp.dot(mixed_ref[...], w_ref[...], preferred_element_type=f32)
        out_ref[:, cols] = x_ref[:, cols].astype(f32) + dot
    unit, _ = centre(out_ref[...])
    norm_ref[...] = (unit * gain_ref[...] + shift_ref[...]).astype(bf16)


def add_temporal(mixed, halves, x, gain, shift, scalars):
    rows, width = x.shape
    block = ((256, width), lambda i, ref: (i, 0))
    return dense(
        hidden2_body, (rows // 256,), scalars,
        [rows_of(mixed), *[out_half(w) for w in halves], rows_of(x), whole(gain[None]),
         whole(shift[None])],
        [((rows, width), f32, *block), ((rows, width), bf16, *block)],
    )


def hidden3_body(_, a_ref, b_ref, own_ref, other_ref, x_ref, bias_ref, mask_ref, out_ref):
    out = x_ref[...] + bias_ref[...]
    out += jnp.dot(a_ref[...], own_ref[...], preferred_element_type=f32)
    out += jnp.dot(b_ref[...], other_ref[...], preferred_element_type=f32)
    out_ref[...] = jnp.where(mask_ref[...] > 0, out, 0).astype(bf16)


def down_project(actives, halves, x, bias, mask, scalars):
    rows, width = x.shape
    (out,) = dense(
        hidden3_body, (rows // 256,), scalars,
        [*[rows_of(y) for y in actives], *[whole(w) for w in halves], rows_of(x), whole(bias),
         rows_of(mask)],
        [((rows, width), bf16, (256, width), lambda i, ref: (i, 0))], margin=30,
    )
    return out


def inner_back_body(_, x_ref, w_ref, slope_ref, out_ref, sum_ref):
    grad = dot_t(x_ref[...], w_ref[...]) * slope_ref[...].astype(f32)
    out_ref[...] = grad.astype(bf16)
    sum_ref[...] = jnp.sum(out_ref[...].astype(f32), axis=0, keepdims=True)


def inner_back(x, w, slope, scalars):
    rows, cols = slope.shape
    index = lambda j, ref: (0, j)
    return dense(
        inner_back_body, (cols // BLOCK,), scalars,
        [whole(x), (w, (BLOCK, w.shape[1]), lambda j, ref: (j, 0)), (slope, (rows, BLOCK), index)],
        [((rows, cols), bf16, (rows, BLOCK), index), ((1, cols), f32, (1, BLOCK), index)],
    )


def norm_back_body(
    _, a_ref, b_ref, own_ref, other_ref, x_ref, added_ref, gain_ref, rest_ref, out_ref, sums_ref
):
    grad = dot_t(a_ref[...], own_ref[...]) + dot_t(b_ref[...], other_ref[...])
    unit, scale = centre(x_ref[...].astype(f32) + added_ref[0])
    scaled = grad * gain_ref[...]
    first = jnp.mean(scaled, axis=-1, keepdims=True)
    second = jnp.mean(scaled * unit, axis=-1, keepdims=True)
    out = rest_ref[...].astype(f32) + scale * (scaled - first - unit * second)
    out_ref[...] = out.astype(out_ref.dtype)
    terms = (grad * unit, grad, out)
    sums_ref[0] = jnp.concatenate([jnp.sum(x, axis=0, keepdims=True) for x in terms], axis=0)


def norm_back(grads, halves, x, added, gain, rest, dtype, scalars):
    rows, width = x.shape
    step, cols = 256, grads[0].shape[1]
    added_at = (lambda i, ref: (i, 0, 0)) if added.shape[0] > 1 else at(0, 0, 0)
    return dense(
        norm_back_body, (rows // step,), scalars,
        [*[rows_of(g) for g in grads], *[(w, (w.shape[0], cols), FIXED) for w in halves],
         rows_of(x), (added, (1, 1, width), added_at), whole(gain[None]), rows_of(rest)],
        [((rows, width), dtype, (step, width), lambda i, ref: (i, 0)),
         ((rows // step, 3, width), f32, (1, 3, width), lambda i, ref: (i, 0, 0))],
        margin=30 if dtype == f32 else 6,
    )


def mixed_back_body(core_ref, x_ref, own_ref, other_ref, out_ref):
    grad = 0
    for cols, w_ref in sides(core_ref[0], own_ref, other_ref):
        grad += dot_t(x_ref[:, cols], w_ref[...])
    out_ref[...] = grad.astype(bf16)


def mixed_back(x, halves, scalars):
    rows, width = x.shape
    last = halves[0].shape[1] // BLOCK - 1
    (out,) = dense(
        mixed_back_body, (width // BLOCK,), scalars,
        [whole(x), *[(w, (BLOCK, BLOCK), lambda j, ref: (j, last)) for w in halves]],
        [((rows, width), bf16, (rows, BLOCK), lambda j, ref: (0, j))],
    )
    return out


def weight_grad_body(_, x_ref, y_ref, out_ref):
    out_ref[...] = t_dot(x_ref[...], y_ref[...]).astype(bf16).reshape(out_ref.shape)


def weight_grad(x, y, total, scalars, half=None):
    rows, count = x.shape
    cols = y.shape[1] if half is None else BLOCK
    shift = (lambda j, ref: (0, j)) if half is None else (lambda j, ref: (0, ref[0] ^ half))
    shape = (total, count // total)
    (out,) = dense(
        weight_grad_body, (cols // BLOCK,), scalars,
        [whole(x), (y, (rows, BLOCK), shift)],
        [((*shape, cols), bf16, (*shape, BLOCK), lambda j, ref: (0, 0, j))],
    )
    return out


def weight_split_body(ends, info_ref, *refs):
    send_ref, keep_ref, sum_ref = refs[-3:]
    step = pl.program_id(0)
    for p in range(len(ends) - 1):

        @pl.when((step >= ends[p]) & (step < ends[p + 1]))
        def _(x_ref=refs[3 * p], y_ref=refs[3 * p + 1], got_ref=refs[3 * p + 2]):
            grad = t_dot(x_ref[...], y_ref[...]).reshape(sum_ref.shape)
            sum_ref[...] = grad + got_ref[...].astype(f32)

    part(info_ref, sum_ref, send_ref, keep_ref)


def weight_split(parts, k, value, core):
    scalars = jnp.stack([jnp.int32(k), value.astype(jnp.int32), core.astype(jnp.int32)])
    total, r, _ = parts[0][2].shape
    widths = [got.shape[2] for _, _, got, _ in parts]
    ends = [sum(widths[:i]) // BLOCK for i in range(len(parts) + 1)]
    inputs = []
    for (x, y, got, half), low, high in zip(parts, ends[:-1], ends[1:]):
        place = lambda j, low=low, high=high: jnp.clip(j - low, 0, high - low - 1)
        if half is None:
            index = lambda j, ref, place=place: (0, place(j))
        else:
            index = lambda j, ref, half=half: (0, ref[2] ^ half)
        inputs += [
            whole(x),
            (y, (y.shape[0], BLOCK), index),
            (got, (total, r, BLOCK), lambda j, ref, place=place: (0, 0, place(j))),
        ]
    shape = (total // 2, r)
    out = ((*shape, sum(widths)), bf16, (*shape, BLOCK), lambda j, ref: (0, 0, j))
    return dense(
        partial(weight_split_body, ends), (ends[-1],), scalars, inputs, [out, out],
        [pltpu.VMEM((total, r, BLOCK), f32)],
    )


TAIL = (
    0.14760860800743103, 0.14761532843112946, 0.127163827419281, 0.09018292278051376,
    0.013407237827777863, 0.06451446563005447, -0.19429759681224823, 0.13513216376304626,
    -0.031326886266469955,
)


def gelu(inner):
    size = 1.0 + 0.37 * jnp.abs(inner)
    t = pl.reciprocal(size, approx=True)
    t = t * (2.0 - size * t)
    bell = jnp.exp2(inner * inner * -0.7213475204444817)
    series = TAIL[-1]
    for term in reversed(TAIL[:-1]):
        series = series * t + term
    tail = series * t * bell
    cdf = jnp.where(inner > 0, 1.0 - tail, tail)
    return inner * cdf, cdf + inner * bell * 0.3989422804014327


def up_body(x_ref, w_ref, bias_ref, active_ref, slope_ref):
    rows = x_ref.shape[0]
    step = min(rows, 128)
    for r in range(0, rows, step):
        inner = jnp.dot(x_ref[r : r + step], w_ref[...], preferred_element_type=f32)
        active, slope = gelu(inner + bias_ref[...])
        active_ref[r : r + step] = active.astype(active_ref.dtype)
        slope_ref[r : r + step] = slope.astype(slope_ref.dtype)


def up_project(x, weight, bias):
    rows, width = x.shape
    cols, block = weight.shape[1], 512
    out = jax.ShapeDtypeStruct((rows, cols), bf16)
    return pl.pallas_call(
        up_body,
        grid=(cols // block,),
        in_specs=[
            pl.BlockSpec((rows, width), lambda i: (0, 0)),
            pl.BlockSpec((width, block), lambda i: (0, i)),
            pl.BlockSpec((1, block), lambda i: (0, i)),
        ],
        out_specs=[pl.BlockSpec((rows, block), lambda i: (0, i))] * 2,
        out_shape=[out, out],
        compiler_params=params(
            [(x.shape, bf16, 2), ((width, block), bf16, 2), ((rows, block), bf16, 4)]
        ),
        cost_estimate=NO_COST,
    )(x, weight, bias)


def on_device(
    tokens,
    actions,
    sides,
    action_table,
    norm_gains,
    norm_shifts,
    s_qkv,
    s_out,
    t_qkv,
    t_out,
    w_up,
    b_up,
    w_down,
    b_down,
    grad_out,
):
    shape = tokens.shape
    frames_local, _, slots, width = shape
    place = Place()
    total, core, tm_size = place.total, place.core, place.tm_size
    slots_local = slots // tm_size
    row_count = frames_local * slots
    half = width // 2

    def to_slots(value):
        view = value.reshape(frames_local, tm_size, slots_local, value.shape[-1])
        parts = []
        for o in range(tm_size):
            part = lax.dynamic_index_in_dim(view, place.tm ^ o, 1, keepdims=False)
            parts.append(place.tm_flip(part, o) if o else part)
        return parts

    def from_slots(value, offsets=range(tm_size)):
        view = value.reshape(tm_size, frames_local, slots_local, value.shape[-1])
        return [place.tm_flip(view[o], o) if o else view[o] for o in offsets]

    def in_slots(parts):
        return jnp.concatenate(parts, axis=0)

    def in_frames(parts):
        return jnp.stack(unscramble(parts, place.tm), axis=1).reshape(frames_local, slots, -1)

    def own_and_other(value, axis):
        first, second = (lax.index_in_dim(value, i, axis, keepdims=False) for i in (0, 1))
        return jnp.where(core == 0, first, second), jnp.where(core == 0, second, first)

    def in_order(own, other, axis):
        pair = [jnp.where(core == 0, own, other), jnp.where(core == 0, other, own)]
        return jnp.stack(pair, axis=axis)

    def woven(own, other):
        cuts = [slice(i, i + half) for i in range(0, own.shape[1], half)]
        own_first = [x[:, cut] for cut in cuts for x in (own, other)]
        other_first = [x[:, cut] for cut in cuts for x in (other, own)]
        return jnp.where(
            core == 0,
            jnp.concatenate(own_first, axis=1),
            jnp.concatenate(other_first, axis=1),
        )

    thin = width // total
    counts = [ACTIONS, 3, 3, 1]
    ends = [sum(counts[:i]) for i in range(len(counts) + 1)]
    rows = s_qkv.shape[0]
    hidden_half = w_down.shape[0] // 2

    def attention_group(qkv, out):
        qkv = own_and_other(qkv.reshape(rows, 3, 2, half), 2)
        both = [
            jnp.concatenate([a.reshape(rows, 3 * half), b], axis=1)
            for a, b in zip(qkv, own_and_other(out.reshape(rows, 2, half), 1))
        ]
        return Chain(gather(place, *both))

    front = attention_group(s_qkv, s_out)
    tokens = along(tokens, front)
    rows_in = (action_table, norm_gains, norm_shifts, b_down)
    tokens, rows_in, b_up, grad_out = lax.optimization_barrier((tokens, rows_in, b_up, grad_out))
    action_table, norm_gains, norm_shifts, b_down = rows_in
    small = jnp.concatenate([action_table, norm_gains, norm_shifts, b_down[None]], axis=0).T
    small = jnp.pad(small, ((0, 0), (0, LANES - ends[-1])))
    b_up = jnp.pad(b_up[None], ((0, GROUP - 1), (0, LANES - b_up.shape[0])))
    small = jnp.concatenate([small, b_up], axis=0)
    tokens = along(tokens, front)
    tokens, grad_out = lax.optimization_barrier((tokens, grad_out))
    cotangent = to_slots(grad_out.reshape(frames_local, slots, width))
    small = Chain(gather_small(place, small))
    tokens = along(tokens, small)
    tokens = along(tokens, small)
    tokens, t_qkv, t_out = lax.optimization_barrier((tokens, t_qkv, t_out))
    tokens = along(tokens, front)
    middle = attention_group(t_qkv, t_out)
    tokens = along(tokens, middle)
    tokens, cotangent = lax.optimization_barrier((tokens, cotangent))
    tokens = along(tokens, front, middle)
    tokens = along(tokens, small)
    tokens = along(tokens, small)
    tokens = along(tokens, front, middle)
    while not small.done():
        tokens = along(tokens, small)
    tokens, w_up, w_down = lax.optimization_barrier((tokens, w_up, w_down))
    up_pair = own_and_other(w_up.reshape(rows, total, 2, hidden_half), 2)
    rising = Chain(gather(place, *[x.reshape(rows, -1) for x in up_pair]))
    falling = Chain(gather(place, *own_and_other(w_down.reshape(2, hidden_half, width), 0)))
    small = small.result.astype(f32)
    table = small[:, :thin].reshape(width, LANES).T

    def unpack(i):
        return table[ends[i] : ends[i + 1]]

    action_rows, gains, shifts, down_bias = [unpack(i) for i in range(4)]
    up_bias = small[:, thin, : 2 * hidden_half].reshape(total, 2, hidden_half)
    up_bias = [x.reshape(1, -1) for x in own_and_other(up_bias, 1)]

    onehot = (actions == jnp.arange(ACTIONS)[None, :]).astype(f32)
    embedded = jnp.dot(onehot, action_rows, precision=highest)
    tokens = tokens.reshape(frames_local, slots, width)
    embedded = embedded[:, None, :]
    normed1 = norm(tokens, embedded, gains[0], shifts[0])
    normed1 = along(normed1, front, middle, rising)
    s_halves = [x.reshape(width, -1) for x in finish(front)]
    here = core.astype(jnp.int32).reshape(1)

    def projected(x, w, outer):
        return project(x, w, 3 * half, here).reshape(*outer, -1)

    spatial = [projected(normed1, w, (frames_local, slots)) for w in s_halves]
    spatial = along(spatial, middle, rising)

    def frame_index(i):
        return (i, 0, 0)

    def slot_index(i):
        return (0, i, 0)

    spatial_place = (
        jnp.stack([sides[0], core.astype(jnp.int32)]), (1, slots), frames_local, frame_index,
    )
    (s_mixed,) = run_attention(
        partial(attention_forward, spatial_bias), *spatial_place, spatial, [width]
    )
    s_mixed = s_mixed.reshape(row_count, width)
    flat = tokens.reshape(row_count, width)
    hidden1 = add_spatial(s_mixed, s_halves, flat, embedded, here)

    hidden1 = along(hidden1, middle, rising, falling)
    parts = to_slots(hidden1.reshape(tokens.shape))
    parts = land(parts, middle, rising, falling)
    hidden1 = in_slots(parts)
    frames = hidden1.shape[0]
    slot_at = place.tm * slots_local + jnp.arange(slots_local)
    mask = (slot_at < sides[0] * sides[0])[None, :, None]
    nothing = jnp.zeros((1, 1, width), f32)
    normed2 = norm(hidden1, nothing, gains[1], shifts[1])
    hidden1 = hidden1.reshape(row_count, width)
    normed2 = launch(normed2, rising, falling)
    t_halves = [x.reshape(width, -1) for x in finish(middle)]
    temporal = [projected(normed2, w, (frames, slots_local)) for w in t_halves]
    temporal = along(temporal, rising, falling)
    temporal_place = (
        jnp.stack([place.tm.astype(jnp.int32), core.astype(jnp.int32)]), (frames, GROUP),
        slots_local // GROUP, slot_index,
    )
    make_bias = partial(temporal_bias, frames_local)
    (t_mixed,) = run_attention(
        partial(attention_forward, make_bias), *temporal_place, temporal, [width]
    )
    t_mixed = t_mixed.reshape(row_count, width)
    hidden2, normed3 = add_temporal(t_mixed, t_halves, hidden1, gains[2], shifts[2], here)
    normed3 = along(normed3, rising, falling)
    up_halves = [x.reshape(width, -1) for x in finish(rising)]
    first = up_project(normed3, up_halves[0], up_bias[0])
    first = along(first, falling)
    normed3, first = lax.optimization_barrier((normed3, first))
    second = up_project(normed3, up_halves[1], up_bias[1])
    second = along(second, falling)
    (active, slope), (active2, slope2) = first, second

    core_pair = (place.core_bit, place.core_bit)

    def exchanged(grad):
        return place.flip(grad, core_pair)

    def sums(*parts):
        return Chain(scatter(place, lambda k, value: weight_split(parts, k, value, core)))

    down_in = jnp.where(mask, in_slots(cotangent), 0).reshape(row_count, width)
    send = weight_grad(active2, down_in, total, here)
    hidden2 = land(hidden2, falling)
    down_halves = [x.reshape(-1, width) for x in finish(falling)]
    hidden2, send = launch(hidden2, also=[send])
    got = exchanged(send)
    mask_rows = jnp.broadcast_to(mask, (frames, slots_local, 1)).reshape(row_count, 1).astype(f32)
    mixed = down_project([active, active2], down_halves, hidden2, down_bias, mask_rows, here)
    down_in, mixed, got = lax.optimization_barrier((down_in, mixed, got))
    s_down = sums((active, down_in, got, None))
    down_in = launch(down_in, s_down)

    inner_grad, b_sum = inner_back(down_in, down_halves[0], slope, here)
    inner_grad2, b_sum2 = inner_back(down_in, down_halves[1], slope2, here)
    send = weight_grad(normed3, inner_grad2, total, here)
    inner_grad, inner_grad2, send = land((inner_grad, inner_grad2, send), s_down)
    inner_grads, send = launch((inner_grad, inner_grad2), s_down, also=[send])
    got = exchanged(send)

    b_sums = [x.reshape(total, -1, thin).swapaxes(0, 1) for x in (b_sum, b_sum2)]
    late_rows = [x.reshape(-1, width) for x in b_sums]
    late_rows = jnp.where(
        core == 0, jnp.concatenate(late_rows, axis=0), jnp.concatenate(late_rows[::-1], axis=0)
    )
    late_rows = jnp.concatenate([jnp.sum(down_in.astype(f32), axis=0)[None], late_rows], axis=0)

    grad2, sums3 = norm_back(
        inner_grads, up_halves, hidden2, nothing, gains[2], down_in, bf16, here
    )
    t_mix_grad = mixed_back(grad2, t_halves, here)
    t_mix_grad, got = land(t_mix_grad, s_down, also=[got])
    s_up = sums((normed3, inner_grads[0], got, None))
    t_mix_grad = launch(t_mix_grad, s_down, s_up)
    t_mix_grad = t_mix_grad.reshape(frames, slots_local, width)

    def back(side, where, make, values, grad):
        (out,) = run_attention(
            partial(attention_backward, make, (side,)), *where, [values[side], grad], [3 * half]
        )
        return out.reshape(row_count, -1)

    t_grad2 = back(1, temporal_place, make_bias, temporal, t_mix_grad)
    send = weight_grad(normed2, t_grad2, total, here)
    send2 = weight_grad(t_mixed, grad2, total, here, 1)
    t_grad = back(0, temporal_place, make_bias, temporal, t_mix_grad)
    t_grads = land((t_grad, t_grad2), s_down, s_up)
    t_grads, send, send2 = launch(t_grads, s_down, s_up, also=[send, send2])
    gots = [exchanged(send), exchanged(send2)]

    grad1, sums2 = norm_back(t_grads, t_halves, hidden1, nothing, gains[1], grad2, bf16, here)
    grad1, *gots = land(grad1, s_down, s_up, also=gots)
    grad1 = launch(grad1, s_down, s_up)
    parts = from_slots(grad1)
    s_time = sums((normed2, t_grads[0], gots[0], None), (t_mixed, grad2, gots[1], 0))
    parts[0], s_time.pending = lax.optimization_barrier((parts[0], s_time.pending))
    parts = land(parts, s_down, s_up)
    grad1 = in_frames(parts).reshape(row_count, width)
    grad1 = launch(grad1, s_down, s_up, s_time)

    send2 = weight_grad(s_mixed, grad1, total, here, 1)
    mix_grad = mixed_back(grad1, s_halves, here).reshape(frames_local, slots, width)
    s_grad2 = back(1, spatial_place, spatial_bias, spatial, mix_grad)
    send = weight_grad(normed1, s_grad2, total, here)
    mix_grad, send, send2 = land((mix_grad, send, send2), s_down, s_up, s_time)
    mix_grad, send, send2 = launch(mix_grad, s_down, s_up, s_time, also=[send, send2])
    gots = [exchanged(send), exchanged(send2)]

    s_grad = back(0, spatial_place, spatial_bias, spatial, mix_grad)
    s_grad, *gots = land(s_grad, s_down, s_up, s_time, also=gots)
    s_space = sums((normed1, s_grad, gots[0], None), (s_mixed, grad1, gots[1], 0))
    s_grads = launch((s_grad, s_grad2), s_time, s_space)

    input_grad, sums1 = norm_back(
        s_grads, s_halves, flat, embedded, gains[0], grad1, f32, here
    )
    sums1, input_grad = land((sums1, input_grad), s_time, s_space)
    sums1, input_grad = launch((sums1, input_grad), s_time, s_space)
    g_actions = jnp.sum(onehot[:, :, None] * sums1[:, 2][:, None, :], axis=0)
    all_sums = [jnp.sum(x[:, :2], axis=0) for x in (sums1, sums2, sums3)]
    both_norms = [jnp.stack([x[i] for x in all_sums]) for i in (0, 1)]
    packed = jnp.concatenate([g_actions, *both_norms, late_rows], axis=0)
    s_small = Chain(scatter_small(place, packed))
    packed = launch(packed, s_small)
    packed = land(packed, s_time, s_space, s_small)
    packed, mixed = launch((packed, mixed), s_time, s_space, s_small)
    near = from_slots(mixed, range(tm_size // 2 + 1))
    packed, down_sums, up_sums = lax.optimization_barrier((packed, finish(s_down), finish(s_up)))
    g_w_down = in_order(*down_sums, 0).reshape(w_down.shape)
    g_w_up = in_order(*[x.reshape(rows, total, -1) for x in up_sums], 2).reshape(w_up.shape)
    packed = along(packed, s_small)
    packed, *near = land(packed, s_time, s_space, s_small, also=near)
    packed, mixed = launch((packed, mixed), s_time, s_space, s_small)
    packed, g_w_down, g_w_up = lax.optimization_barrier((packed, g_w_down, g_w_up))
    far = from_slots(mixed, range(tm_size // 2 + 1, tm_size))
    packed = along(packed, s_small)
    packed, *far = land(packed, s_time, s_space, s_small, also=far)
    packed = launch(packed, s_time, s_space, s_small)
    mixed = in_frames(near + far)
    packed, mixed = lax.optimization_barrier((packed, mixed))
    while not (s_time.done() and s_space.done() and s_small.done()):
        packed = along(packed, s_time, s_space, s_small)
    summed = s_small.result
    t_rows, s_rows = woven(*s_time.result), woven(*s_space.result)
    g_t_qkv, g_t_out = t_rows[:, : 3 * width], t_rows[:, 3 * width :]
    g_s_qkv, g_s_out = s_rows[:, : 3 * width], s_rows[:, 3 * width :]

    return (
        mixed.reshape(shape),
        input_grad.reshape(shape),
        summed[:8],
        summed[8:11],
        summed[11:14],
        g_s_qkv,
        g_s_out,
        g_t_qkv,
        g_t_out,
        g_w_up,
        summed[15:].reshape(-1),
        g_w_down,
        summed[14],
    )


def solution(mesh):
    whole = P(("tm", "clip"), None)
    spread = P(None, ("tm", "clip"))
    frames = P("tm", "clip", None, None)
    vector = P(("tm", "clip"))
    return jax.shard_map(
        on_device,
        mesh=mesh,
        in_specs=(
            frames, P("tm", "clip"), P("clip"), spread, spread, spread, whole, whole, whole,
            whole, whole, vector, whole, vector, frames,
        ),
        out_specs=(
            frames, frames, spread, spread, spread, whole, whole, whole, whole, whole, vector,
            whole, vector,
        ),
        check_vma=False,
    )
```

```python
import math
from functools import partial

import jax
import jax.numpy as jnp
from jax import lax
from jax.experimental import pallas as pl
from jax.experimental.pallas import tpu as pltpu
from jax.sharding import PartitionSpec as P

H = 16
E = 64
ACTIONS = 8
FRAMES = 16
AXES = ("tm", "clip")
LANES = 128
GROUP = 16

negative = -1e30
highest = lax.Precision.HIGHEST
MIB = 1024 * 1024
bf16, f32 = jnp.bfloat16, jnp.float32
NO_COST = pl.CostEstimate(flops=0, bytes_accessed=0, transcendentals=0)


def params(blocks, margin=6):
    size = sum(math.prod(shape) * jnp.dtype(dtype).itemsize * n for shape, dtype, n in blocks)
    return pltpu.CompilerParams(vmem_limit_bytes=(-(-size // MIB) + margin) * MIB)


class Place:
    def __init__(self):
        tm_size, clip_size = lax.axis_size("tm"), lax.axis_size("clip")
        self.tm_size, self.clip_size, self.total = tm_size, clip_size, tm_size * clip_size
        self.tm = lax.axis_index("tm")
        self.me = self.tm * clip_size + lax.axis_index("clip")
        self.core_bit = clip_size
        self.core = self.bit_of(clip_size)
        clip_bits = [1 << i for i in range(clip_size.bit_length() - 1)]
        tm_bits = [clip_size << i for i in range(tm_size.bit_length() - 1)]
        x, z, y = clip_bits[:-2], clip_bits[-2:], tm_bits[1:]
        self.z = [(b, b) for b in z]
        self.xy = list(zip(x + y, y + x))

    def bit_of(self, bit):
        return (self.me // bit) % 2

    def mine(self, pair):
        return jnp.where(self.core == 0, self.bit_of(pair[0]), self.bit_of(pair[1]))

    def choose(self, pair):
        return jnp.where(self.core == 0, pair[0], pair[1])

    def flip(self, value, pair):
        moves = [(i, i ^ pair[(i // self.core_bit) % 2]) for i in range(self.total)]
        return lax.ppermute(value, AXES, moves)

    def tm_flip(self, value, offset):
        moves = [(i, i ^ (offset * self.clip_size)) for i in range(self.total)]
        return lax.ppermute(value, AXES, moves)


def below(have, bit):
    return sum(1 for b in have if b < bit)


def unscramble(parts, me):
    bit = 1
    while bit < len(parts):
        swap = (me & bit) != 0
        parts = [jnp.where(swap, parts[p ^ bit], parts[p]) for p in range(len(parts))]
        bit *= 2
    return parts


def position(m, value, k):
    m = jnp.int32(m)
    high = lax.shift_left(lax.shift_right_logical(m, k), k + 1)
    return high | lax.shift_left(value, k) | (m & (lax.shift_left(jnp.int32(1), k) - 1))


def merge_body(info_ref, mine_ref, other_ref, out_ref):
    k, value = info_ref[0], info_ref[1]
    for m in range(mine_ref.shape[0]):
        out_ref[position(m, value, k)] = mine_ref[m]
        out_ref[position(m, 1 - value, k)] = other_ref[m]


def column_block(shape):
    blocks, rows, cols = shape
    return cols if blocks * rows * cols <= 512 * 1024 else min(cols, 512)


def merge(mine, other, k, value):
    m, r, n = mine.shape
    block = column_block((2 * m, r, n))
    spec = pl.BlockSpec((m, r, block), lambda j: (0, 0, j))
    return pl.pallas_call(
        merge_body,
        grid=(n // block,),
        in_specs=[pl.BlockSpec(memory_space=pltpu.SMEM), spec, spec],
        out_specs=pl.BlockSpec((2 * m, r, block), lambda j: (0, 0, j)),
        out_shape=jax.ShapeDtypeStruct((2 * m, r, n), mine.dtype),
        compiler_params=params([((4 * m, r, block), mine.dtype, 2)], 2),
        cost_estimate=NO_COST,
    )(jnp.stack([jnp.int32(k), value.astype(jnp.int32)]), mine, other)


def part(info_ref, source_ref, send_ref, keep_ref):
    k, value = info_ref[0], info_ref[1]
    for m in range(send_ref.shape[0]):
        for out_ref, at in ((send_ref, 1 - value), (keep_ref, value)):
            out_ref[m] = source_ref[position(m, at, k)].astype(out_ref.dtype)


def split_body(info_ref, a_ref, b_ref, send_ref, keep_ref):
    k, value = info_ref[0], info_ref[1]
    for m in range(send_ref.shape[0]):
        for out_ref, at in ((send_ref, 1 - value), (keep_ref, value)):
            i = position(m, at, k)
            out_ref[m] = (a_ref[i].astype(f32) + b_ref[i].astype(f32)).astype(out_ref.dtype)


def split(a, b, k, value, dtype):
    blocks, r, n = a.shape
    block = column_block(a.shape)
    out = jax.ShapeDtypeStruct((blocks // 2, r, n), dtype)
    return pl.pallas_call(
        split_body,
        grid=(n // block,),
        in_specs=[pl.BlockSpec(memory_space=pltpu.SMEM)]
        + [pl.BlockSpec((blocks, r, block), lambda j: (0, 0, j))] * 2,
        out_specs=[pl.BlockSpec((blocks // 2, r, block), lambda j: (0, 0, j))] * 2,
        out_shape=[out, out],
        compiler_params=params([((3 * blocks, r, block), dtype, 2)], 3),
        cost_estimate=NO_COST,
    )(jnp.stack([jnp.int32(k), value.astype(jnp.int32)]), a, b)


def gather_small(place, value):
    core = (place.core_bit, place.core_bit)
    x_and_y = [(b, b) for b, _ in place.xy]
    count = len(x_and_y) // 2
    blocks, have = value[None], []
    for pair in x_and_y[:count] + [core] + x_and_y[count:] + place.z:
        (send,) = yield [blocks]
        (got,) = yield [place.flip(send, pair)]
        blocks = merge(blocks, got, below(have, pair[0]), place.bit_of(pair[0]))
        have.append(pair[0])
    return blocks


def scatter_small(place, value):
    bit = place.total // 2
    while bit:
        half = value.shape[1] // 2
        low_half, high_half = value[:, :half], value[:, half:]
        mine = (place.me & bit) != 0
        (send,) = yield [jnp.where(mine, low_half, high_half)]
        (got,) = yield [place.flip(send, (bit, bit))]
        value = jnp.where(mine, high_half, low_half) + got
        bit //= 2
    return value


def gather(place, keep, send, ahead=0):
    core = (place.core_bit, place.core_bit)
    have = ([], [])
    blocks, out = keep[None], send[None]
    for pair in [core] + place.xy[:ahead] + place.z[::-1] + place.xy[ahead:]:
        (out,) = yield [out]
        (got,) = yield [place.flip(out, pair)]
        k = [below(h, b) for h, b in zip(have, pair)]
        blocks = out = merge(blocks, got, place.choose(k), place.mine(pair))
        have = (have[0] + [pair[0]], have[1] + [pair[1]])
    (out,) = yield [out]
    (got,) = yield [place.flip(out, core)]
    return blocks, got


def scatter(place, first):
    core = (place.core_bit, place.core_bit)
    bits = [1 << i for i in range(place.total.bit_length() - 1)]
    have, pairs = (bits, bits), None
    for pair in place.xy[::-1] + place.z + [core]:
        have = tuple([b for b in h if b != bit] for h, bit in zip(have, pair))
        k = place.choose([below(h, b) for h, b in zip(have, pair)])
        dtype = f32 if pair == core else bf16
        if pairs is None:
            send, keep = first(k, place.mine(pair))
        else:
            send, keep = split(*pairs, k, place.mine(pair), dtype)
        (send,) = yield [send]
        (got,) = yield [place.flip(send, pair)]
        pairs = (keep, got)
    return keep[0], got[0]


class Chain:
    def __init__(self, steps):
        self.steps, self.flying, self.result = steps, False, None
        self.pending = next(steps)

    def done(self):
        return self.result is not None

    def move(self):
        try:
            self.pending = self.steps.send(self.pending)
        except StopIteration as stop:
            self.result = stop.value
        self.flying = not self.flying


def hold(value, *chains):
    chains = [c for c in chains if c.flying]
    value, got = lax.optimization_barrier((value, [c.pending for c in chains]))
    for c, g in zip(chains, got):
        c.pending = g
    return value


def land(value, *chains, also=()):
    chains = [c for c in chains if c.flying]
    value, got, also = lax.optimization_barrier((value, [c.pending for c in chains], list(also)))
    for c, g in zip(chains, got):
        c.pending = g
        c.move()
    return (value, *also) if also else value


def launch(value, *chains, also=()):
    chains = [c for c in chains if not c.done() and not c.flying]
    value, sent, also = lax.optimization_barrier((value, [c.pending for c in chains], list(also)))
    for c, g in zip(chains, sent):
        c.pending = g
        c.move()
    return (value, *also) if also else value


def along(value, *chains):
    return launch(land(value, *chains), *chains)


def finish(chain):
    while not chain.done():
        chain.move()
    return chain.result


def spatial_bias(scalar, rows, keys):
    key = lax.broadcasted_iota(jnp.int32, (1, rows) if keys == 1 else (rows, 1), keys)
    return jnp.where(key < scalar * scalar, 0.0, negative)


def temporal_bias(frames_local, scalar, rows, keys):
    def place(axis):
        index = lax.broadcasted_iota(jnp.int32, (rows, rows), axis)
        slot, at = index % GROUP, index // GROUP
        frame = ((at // frames_local) ^ scalar) * frames_local + at % frames_local
        return slot, frame

    slot_q, frame_q = place(1 - keys)
    slot_k, frame_k = place(keys)
    return jnp.where((slot_q == slot_k) & (frame_q >= frame_k), 0.0, negative)


def dot_t(a, b):
    return lax.dot_general(a, b, (((1,), (1,)), ((), ())), preferred_element_type=f32)


def t_dot(a, b):
    return lax.dot_general(a, b, (((0,), (0,)), ((), ())), preferred_element_type=f32)


def columns(scalar_ref, side, start):
    half = H * E // 2
    return pl.ds(pl.multiple_of((scalar_ref[1] ^ side) * half + start, LANES), LANES)


def two_heads(rows):
    half = lax.broadcasted_iota(jnp.int32, (rows, LANES), 1) < E

    def apart(x):
        return jnp.concatenate([jnp.where(half, x, 0), jnp.where(half, 0, x)], axis=0)

    def together(x):
        return jnp.where(half, x[:rows], x[rows:])

    return apart, together


def head_pairs(sides, refs):
    a, b, width = refs[0].shape
    rows, width = a * b, width // 3
    for i, side in enumerate(sides):
        for c in range(0, width, LANES):
            q, k, v = (
                refs[i][:, :, at : at + LANES].reshape(rows, LANES)
                for at in (c, width + c, 2 * width + c)
            )
            yield i, side, c, q * bf16(E ** (-0.5)), k, v


def in_turn(items, first, last):
    waiting = None
    for item in items:
        ready = first(*item)
        if waiting is not None:
            last(*waiting)
        waiting = ready
    last(*waiting)


def attention_forward(make_bias, scalar_ref, own_ref, other_ref, out_ref):
    a, b, width = own_ref.shape
    rows, width = a * b, width // 3
    bias = make_bias(scalar_ref[0], rows, 1)
    apart, together = two_heads(rows)

    def first(i, side, c, q, k, v):
        scores = dot_t(apart(q), k).reshape(2, rows, rows) + bias[None]
        weights = jnp.exp(scores - jnp.max(scores, axis=2, keepdims=True))
        scale = 1.0 / jnp.sum(weights, axis=2, keepdims=True)
        return side, c, v, weights.astype(bf16).reshape(2 * rows, rows), scale

    def last(side, c, v, weights, scale):
        mixed = jnp.dot(weights, v, preferred_element_type=f32) * scale.reshape(2 * rows, 1)
        mixed = together(mixed).astype(out_ref.dtype)
        out_ref[:, :, columns(scalar_ref, side, c)] = mixed.reshape(a, b, LANES)

    in_turn(head_pairs((0, 1), (own_ref, other_ref)), first, last)


def attention_backward(make_bias, sides, scalar_ref, *refs):
    grad_ref = refs[len(sides)]
    a, b, width = refs[0].shape
    rows, width = a * b, width // 3
    bias = make_bias(scalar_ref[0], rows, 0)
    apart, together = two_heads(rows)

    def first(i, side, c, q, k, v):
        g = grad_ref[:, :, columns(scalar_ref, side, c)].reshape(rows, LANES)
        scores = dot_t(apart(k), q).reshape(2, rows, rows) + bias[None]
        prob_grad = dot_t(apart(v), g).reshape(2, rows, rows)
        weights = jnp.exp(scores - jnp.max(scores, axis=1, keepdims=True))
        probs = weights * (1.0 / jnp.sum(weights, axis=1, keepdims=True))
        delta = jnp.sum(probs * prob_grad, axis=1, keepdims=True)
        return i, c, q, k, g, probs.astype(bf16), (probs * (prob_grad - delta)).astype(bf16)

    def last(i, c, q, k, g, probs, score_grad):
        turned = jnp.concatenate([score_grad[0].T, score_grad[1].T], axis=0)
        dq = jnp.dot(turned, k, preferred_element_type=f32) * E ** (-0.5)
        dk = jnp.dot(score_grad.reshape(2 * rows, rows), q, preferred_element_type=f32)
        dv = jnp.dot(probs.reshape(2 * rows, rows), g, preferred_element_type=f32)
        for index, grad in enumerate((dq, dk, dv)):
            start = index * width + c
            merged = together(grad).astype(bf16).reshape(a, b, LANES)
            refs[len(sides) + 1 + i][:, :, start : start + LANES] = merged

    in_turn(head_pairs(sides, refs), first, last)


def run_attention(body, scalars, block, grid, index, inputs, out_widths):
    a, b = block
    outer = inputs[0].shape[:2]
    return pl.pallas_call(
        body,
        grid=(grid,),
        in_specs=[pl.BlockSpec(memory_space=pltpu.SMEM)]
        + [pl.BlockSpec((a, b, x.shape[-1]), index) for x in inputs],
        out_specs=[pl.BlockSpec((a, b, width), index) for width in out_widths],
        out_shape=[jax.ShapeDtypeStruct((*outer, width), bf16) for width in out_widths],
        compiler_params=params(
            [((a, b, width), bf16, 2) for width in (*(x.shape[-1] for x in inputs), *out_widths)], 8
        ),
        cost_estimate=NO_COST,
    )(scalars, *inputs)


def centre(x):
    average = jnp.mean(x, axis=-1, keepdims=True)
    centered = x - average
    variance = jnp.mean(centered * centered, axis=-1, keepdims=True)
    scale = lax.rsqrt(variance + 1e-05)
    return centered * scale, scale


def norm_body(x_ref, added_ref, gain_ref, shift_ref, out_ref):
    unit, _ = centre(x_ref[0].astype(f32) + added_ref[0])
    out_ref[0] = (unit * gain_ref[...] + shift_ref[...]).astype(out_ref.dtype)


def by_rows(body, arrays, rows, outs):
    blocks = arrays[0].shape[0]
    specs = []
    for x in arrays:
        if x.ndim == 2:
            specs.append(pl.BlockSpec(x.shape, lambda i: (0, 0)))
        else:
            at = (lambda i: (i, 0, 0)) if x.shape[0] == blocks else (lambda i: (0, 0, 0))
            specs.append(pl.BlockSpec((1, *x.shape[1:]), at))
    return pl.pallas_call(
        body,
        grid=(blocks,),
        in_specs=specs,
        out_specs=[pl.BlockSpec((1, *shape[1:]), lambda i: (i, 0, 0)) for shape, _ in outs],
        out_shape=[jax.ShapeDtypeStruct(shape, dtype) for shape, dtype in outs],
        compiler_params=params([(x.shape[1:], f32, 4) for x in arrays]),
        cost_estimate=NO_COST,
    )(*arrays)


def norm(x, added, gain, shift):
    shape = (x.shape[0] * x.shape[1] // 256, 256, x.shape[2])
    arrays = [x.reshape(shape), added, gain[None], shift[None]]
    (out,) = by_rows(norm_body, arrays, 256, [(shape, bf16)])
    return out.reshape(-1, shape[2])


BLOCK = 512


def dense(body, grid, scalars, inputs, outs, scratch=(), margin=6):
    used = [(block, x.dtype, 1 if index is FIXED else 2) for x, block, index in inputs]
    used += [(block, dtype, 2) for _, dtype, block, _ in outs]
    used += [(x.shape, x.dtype, 1) for x in scratch]

    def spec(block, index):
        if index is FIXED:
            zeros = (0,) * len(block)
            return pl.BlockSpec(block, lambda *_: zeros, pipeline_mode=pl.Buffered(1))
        return pl.BlockSpec(block, index)

    return pl.pallas_call(
        body,
        grid_spec=pltpu.PrefetchScalarGridSpec(
            num_scalar_prefetch=1,
            grid=grid,
            in_specs=[spec(block, index) for _, block, index in inputs],
            out_specs=[pl.BlockSpec(block, index) for _, _, block, index in outs],
            scratch_shapes=list(scratch),
        ),
        out_shape=[jax.ShapeDtypeStruct(shape, dtype) for shape, dtype, _, _ in outs],
        compiler_params=params(used, margin),
        cost_estimate=NO_COST,
    )(scalars, *[x for x, _, _ in inputs])


FIXED = None


def at(*index):
    return lambda j, ref: index


def whole(x):
    return (x, x.shape, FIXED)


def rows_of(x, rows=256):
    return (x, (rows, x.shape[1]), lambda i, ref: (i, 0))


def project_body(_, x_ref, w_ref, out_ref):
    out_ref[...] = jnp.dot(x_ref[...], w_ref[...], preferred_element_type=f32).astype(bf16)


def project(x, w, cols, scalars):
    index = lambda j, ref: (0, j)
    rows = x.shape[0]
    (out,) = dense(
        project_body, (cols // BLOCK,), scalars,
        [whole(x), (w, (w.shape[0], BLOCK), index)],
        [((rows, cols), bf16, (rows, BLOCK), index)],
    )
    return out


def sides(core, own_ref, other_ref):
    for side, ref in ((core, own_ref), (1 - core, other_ref)):
        yield pl.ds(pl.multiple_of(side * BLOCK, BLOCK), BLOCK), ref


def hidden1_body(core_ref, mixed_ref, own_ref, other_ref, x_ref, added_ref, out_ref):
    for cols, w_ref in sides(core_ref[0], own_ref, other_ref):
        dot = jnp.dot(mixed_ref[...], w_ref[...], preferred_element_type=f32)
        out_ref[:, cols] = (x_ref[:, cols].astype(f32) + added_ref[0, :, cols] + dot).astype(bf16)


def out_half(w):
    return (w, (w.shape[0], BLOCK), at(0, w.shape[1] // BLOCK - 1))


def add_spatial(mixed, halves, x, added, scalars):
    rows, width = x.shape
    step = rows // added.shape[0]
    (out,) = dense(
        hidden1_body, (rows // step,), scalars,
        [rows_of(mixed, step), *[out_half(w) for w in halves], rows_of(x, step),
         (added, (1, 1, width), lambda i, ref: (i, 0, 0))],
        [((rows, width), bf16, (step, width), lambda i, ref: (i, 0))],
    )
    return out


def hidden2_body(
    core_ref, mixed_ref, own_ref, other_ref, x_ref, gain_ref, shift_ref, out_ref, norm_ref
):
    for cols, w_ref in sides(core_ref[0], own_ref, other_ref):
        dot = jnp.dot(mixed_ref[...], w_ref[...], preferred_element_type=f32)
        out_ref[:, cols] = x_ref[:, cols].astype(f32) + dot
    unit, _ = centre(out_ref[...])
    norm_ref[...] = (unit * gain_ref[...] + shift_ref[...]).astype(bf16)


def add_temporal(mixed, halves, x, gain, shift, scalars):
    rows, width = x.shape
    block = ((256, width), lambda i, ref: (i, 0))
    return dense(
        hidden2_body, (rows // 256,), scalars,
        [rows_of(mixed), *[out_half(w) for w in halves], rows_of(x), whole(gain[None]),
         whole(shift[None])],
        [((rows, width), f32, *block), ((rows, width), bf16, *block)],
    )


def hidden3_body(_, a_ref, b_ref, own_ref, other_ref, x_ref, bias_ref, mask_ref, out_ref):
    out = x_ref[...] + bias_ref[...]
    out += jnp.dot(a_ref[...], own_ref[...], preferred_element_type=f32)
    out += jnp.dot(b_ref[...], other_ref[...], preferred_element_type=f32)
    out_ref[...] = jnp.where(mask_ref[...] > 0, out, 0).astype(bf16)


def down_project(actives, halves, x, bias, mask, scalars):
    rows, width = x.shape
    (out,) = dense(
        hidden3_body, (rows // 256,), scalars,
        [*[rows_of(y) for y in actives], *[whole(w) for w in halves], rows_of(x), whole(bias),
         rows_of(mask)],
        [((rows, width), bf16, (256, width), lambda i, ref: (i, 0))], margin=30,
    )
    return out


def inner_back_body(_, x_ref, w_ref, slope_ref, out_ref, sum_ref):
    grad = dot_t(x_ref[...], w_ref[...]) * slope_ref[...].astype(f32)
    out_ref[...] = grad.astype(bf16)
    sum_ref[...] = jnp.sum(out_ref[...].astype(f32), axis=0, keepdims=True)


def inner_back(x, w, slope, scalars):
    rows, cols = slope.shape
    index = lambda j, ref: (0, j)
    return dense(
        inner_back_body, (cols // BLOCK,), scalars,
        [whole(x), (w, (BLOCK, w.shape[1]), lambda j, ref: (j, 0)), (slope, (rows, BLOCK), index)],
        [((rows, cols), bf16, (rows, BLOCK), index), ((1, cols), f32, (1, BLOCK), index)],
    )


def norm_back_body(
    _, a_ref, b_ref, own_ref, other_ref, x_ref, added_ref, gain_ref, rest_ref, out_ref, sums_ref
):
    grad = dot_t(a_ref[...], own_ref[...]) + dot_t(b_ref[...], other_ref[...])
    unit, scale = centre(x_ref[...].astype(f32) + added_ref[0])
    scaled = grad * gain_ref[...]
    first = jnp.mean(scaled, axis=-1, keepdims=True)
    second = jnp.mean(scaled * unit, axis=-1, keepdims=True)
    out = rest_ref[...].astype(f32) + scale * (scaled - first - unit * second)
    out_ref[...] = out.astype(out_ref.dtype)
    terms = (grad * unit, grad, out)
    sums_ref[0] = jnp.concatenate([jnp.sum(x, axis=0, keepdims=True) for x in terms], axis=0)


def norm_back(grads, halves, x, added, gain, rest, dtype, scalars):
    rows, width = x.shape
    step, cols = 256, grads[0].shape[1]
    added_at = (lambda i, ref: (i, 0, 0)) if added.shape[0] > 1 else at(0, 0, 0)
    return dense(
        norm_back_body, (rows // step,), scalars,
        [*[rows_of(g) for g in grads], *[(w, (w.shape[0], cols), FIXED) for w in halves],
         rows_of(x), (added, (1, 1, width), added_at), whole(gain[None]), rows_of(rest)],
        [((rows, width), dtype, (step, width), lambda i, ref: (i, 0)),
         ((rows // step, 3, width), f32, (1, 3, width), lambda i, ref: (i, 0, 0))],
        margin=30 if dtype == f32 else 6,
    )


def mixed_back_body(core_ref, x_ref, own_ref, other_ref, out_ref):
    grad = 0
    for cols, w_ref in sides(core_ref[0], own_ref, other_ref):
        grad += dot_t(x_ref[:, cols], w_ref[...])
    out_ref[...] = grad.astype(bf16)


def mixed_back(x, halves, scalars):
    rows, width = x.shape
    last = halves[0].shape[1] // BLOCK - 1
    (out,) = dense(
        mixed_back_body, (width // BLOCK,), scalars,
        [whole(x), *[(w, (BLOCK, BLOCK), lambda j, ref: (j, last)) for w in halves]],
        [((rows, width), bf16, (rows, BLOCK), lambda j, ref: (0, j))],
    )
    return out


def weight_grad_body(_, x_ref, y_ref, out_ref):
    out_ref[...] = t_dot(x_ref[...], y_ref[...]).astype(bf16).reshape(out_ref.shape)


def weight_grad(x, y, total, scalars, half=None):
    rows, count = x.shape
    cols = y.shape[1] if half is None else BLOCK
    shift = (lambda j, ref: (0, j)) if half is None else (lambda j, ref: (0, ref[0] ^ half))
    shape = (total, count // total)
    (out,) = dense(
        weight_grad_body, (cols // BLOCK,), scalars,
        [whole(x), (y, (rows, BLOCK), shift)],
        [((*shape, cols), bf16, (*shape, BLOCK), lambda j, ref: (0, 0, j))],
    )
    return out


def weight_split_body(ends, info_ref, *refs):
    send_ref, keep_ref, sum_ref = refs[-3:]
    step = pl.program_id(0)
    for p in range(len(ends) - 1):

        @pl.when((step >= ends[p]) & (step < ends[p + 1]))
        def _(x_ref=refs[3 * p], y_ref=refs[3 * p + 1], got_ref=refs[3 * p + 2]):
            grad = t_dot(x_ref[...], y_ref[...]).reshape(sum_ref.shape)
            sum_ref[...] = grad + got_ref[...].astype(f32)

    part(info_ref, sum_ref, send_ref, keep_ref)


def weight_split(parts, k, value, core):
    scalars = jnp.stack([jnp.int32(k), value.astype(jnp.int32), core.astype(jnp.int32)])
    total, r, _ = parts[0][2].shape
    widths = [got.shape[2] for _, _, got, _ in parts]
    ends = [sum(widths[:i]) // BLOCK for i in range(len(parts) + 1)]
    inputs = []
    for (x, y, got, half), low, high in zip(parts, ends[:-1], ends[1:]):
        place = lambda j, low=low, high=high: jnp.clip(j - low, 0, high - low - 1)
        if half is None:
            index = lambda j, ref, place=place: (0, place(j))
        else:
            index = lambda j, ref, half=half: (0, ref[2] ^ half)
        inputs += [
            whole(x),
            (y, (y.shape[0], BLOCK), index),
            (got, (total, r, BLOCK), lambda j, ref, place=place: (0, 0, place(j))),
        ]
    shape = (total // 2, r)
    out = ((*shape, sum(widths)), bf16, (*shape, BLOCK), lambda j, ref: (0, 0, j))
    return dense(
        partial(weight_split_body, ends), (ends[-1],), scalars, inputs, [out, out],
        [pltpu.VMEM((total, r, BLOCK), f32)],
    )


TAIL = (
    0.14760860800743103, 0.14761532843112946, 0.127163827419281, 0.09018292278051376,
    0.013407237827777863, 0.06451446563005447, -0.19429759681224823, 0.13513216376304626,
    -0.031326886266469955,
)


def gelu(inner):
    size = 1.0 + 0.37 * jnp.abs(inner)
    t = pl.reciprocal(size, approx=True)
    t = t * (2.0 - size * t)
    bell = jnp.exp2(inner * inner * -0.7213475204444817)
    series = TAIL[-1]
    for term in reversed(TAIL[:-1]):
        series = series * t + term
    tail = series * t * bell
    cdf = jnp.where(inner > 0, 1.0 - tail, tail)
    return inner * cdf, cdf + inner * bell * 0.3989422804014327


def up_body(x_ref, w_ref, bias_ref, active_ref, slope_ref):
    rows = x_ref.shape[0]
    step = min(rows, 128)
    for r in range(0, rows, step):
        inner = jnp.dot(x_ref[r : r + step], w_ref[...], preferred_element_type=f32)
        active, slope = gelu(inner + bias_ref[...])
        active_ref[r : r + step] = active.astype(active_ref.dtype)
        slope_ref[r : r + step] = slope.astype(slope_ref.dtype)


def up_project(x, weight, bias):
    rows, width = x.shape
    cols, block = weight.shape[1], 512
    out = jax.ShapeDtypeStruct((rows, cols), bf16)
    return pl.pallas_call(
        up_body,
        grid=(cols // block,),
        in_specs=[
            pl.BlockSpec((rows, width), lambda i: (0, 0)),
            pl.BlockSpec((width, block), lambda i: (0, i)),
            pl.BlockSpec((1, block), lambda i: (0, i)),
        ],
        out_specs=[pl.BlockSpec((rows, block), lambda i: (0, i))] * 2,
        out_shape=[out, out],
        compiler_params=params(
            [(x.shape, bf16, 2), ((width, block), bf16, 2), ((rows, block), bf16, 4)]
        ),
        cost_estimate=NO_COST,
    )(x, weight, bias)


def on_device(
    tokens,
    actions,
    sides,
    action_table,
    norm_gains,
    norm_shifts,
    s_qkv,
    s_out,
    t_qkv,
    t_out,
    w_up,
    b_up,
    w_down,
    b_down,
    grad_out,
):
    shape = tokens.shape
    frames_local, _, slots, width = shape
    place = Place()
    total, core, tm_size = place.total, place.core, place.tm_size
    slots_local = slots // tm_size
    row_count = frames_local * slots
    half = width // 2

    def to_slots(value):
        view = value.reshape(frames_local, tm_size, slots_local, value.shape[-1])
        parts = []
        for o in range(tm_size):
            part = lax.dynamic_index_in_dim(view, place.tm ^ o, 1, keepdims=False)
            parts.append(place.tm_flip(part, o) if o else part)
        return parts

    def from_slots(value, offsets=range(tm_size)):
        view = value.reshape(tm_size, frames_local, slots_local, value.shape[-1])
        return [place.tm_flip(view[o], o) if o else view[o] for o in offsets]

    def in_slots(parts):
        return jnp.concatenate(parts, axis=0)

    def in_frames(parts):
        return jnp.stack(unscramble(parts, place.tm), axis=1).reshape(frames_local, slots, -1)

    def own_and_other(value, axis):
        first, second = (lax.index_in_dim(value, i, axis, keepdims=False) for i in (0, 1))
        return jnp.where(core == 0, first, second), jnp.where(core == 0, second, first)

    def in_order(own, other, axis):
        pair = [jnp.where(core == 0, own, other), jnp.where(core == 0, other, own)]
        return jnp.stack(pair, axis=axis)

    def woven(own, other):
        cuts = [slice(i, i + half) for i in range(0, own.shape[1], half)]
        own_first = [x[:, cut] for cut in cuts for x in (own, other)]
        other_first = [x[:, cut] for cut in cuts for x in (other, own)]
        return jnp.where(
            core == 0,
            jnp.concatenate(own_first, axis=1),
            jnp.concatenate(other_first, axis=1),
        )

    thin = width // total
    counts = [ACTIONS, 3, 3, 1]
    ends = [sum(counts[:i]) for i in range(len(counts) + 1)]
    rows = s_qkv.shape[0]
    hidden_half = w_down.shape[0] // 2

    def attention_group(qkv, out):
        qkv = own_and_other(qkv.reshape(rows, 3, 2, half), 2)
        both = [
            jnp.concatenate([a.reshape(rows, 3 * half), b], axis=1)
            for a, b in zip(qkv, own_and_other(out.reshape(rows, 2, half), 1))
        ]
        return Chain(gather(place, *both))

    front = attention_group(s_qkv, s_out)
    tokens = along(tokens, front)
    rows_in = (action_table, norm_gains, norm_shifts, b_down)
    tokens, rows_in, b_up, grad_out = lax.optimization_barrier((tokens, rows_in, b_up, grad_out))
    action_table, norm_gains, norm_shifts, b_down = rows_in
    small = jnp.concatenate([action_table, norm_gains, norm_shifts, b_down[None]], axis=0).T
    small = jnp.pad(small, ((0, 0), (0, LANES - ends[-1])))
    b_up = jnp.pad(b_up[None], ((0, GROUP - 1), (0, LANES - b_up.shape[0])))
    small = jnp.concatenate([small, b_up], axis=0)
    tokens = along(tokens, front)
    tokens, grad_out = lax.optimization_barrier((tokens, grad_out))
    cotangent = to_slots(grad_out.reshape(frames_local, slots, width))
    small = Chain(gather_small(place, small))
    tokens = along(tokens, small)
    tokens = along(tokens, small)
    tokens, t_qkv, t_out = lax.optimization_barrier((tokens, t_qkv, t_out))
    tokens = along(tokens, front)
    middle = attention_group(t_qkv, t_out)
    tokens = along(tokens, middle)
    tokens, w_up = lax.optimization_barrier((tokens, w_up))
    up_pair = own_and_other(w_up.reshape(rows, total, 2, hidden_half), 2)
    rising = Chain(gather(place, *[x.reshape(rows, -1) for x in up_pair], len(place.xy) // 2))
    tokens, cotangent = lax.optimization_barrier((tokens, cotangent))
    tokens = along(tokens, front, middle, rising)
    tokens = along(tokens, small)
    tokens = along(tokens, small)
    tokens, w_down = lax.optimization_barrier((tokens, w_down))
    falling = Chain(gather(place, *own_and_other(w_down.reshape(2, hidden_half, width), 0)))
    tokens = along(tokens, front, middle, rising, falling)
    while not small.done():
        tokens = along(tokens, small)
    small = small.result.astype(f32)
    table = small[:, :thin].reshape(width, LANES).T

    def unpack(i):
        return table[ends[i] : ends[i + 1]]

    action_rows, gains, shifts, down_bias = [unpack(i) for i in range(4)]
    up_bias = small[:, thin, : 2 * hidden_half].reshape(total, 2, hidden_half)
    up_bias = [x.reshape(1, -1) for x in own_and_other(up_bias, 1)]

    onehot = (actions == jnp.arange(ACTIONS)[None, :]).astype(f32)
    embedded = jnp.dot(onehot, action_rows, precision=highest)
    tokens = tokens.reshape(frames_local, slots, width)
    embedded = embedded[:, None, :]
    normed1 = norm(tokens, embedded, gains[0], shifts[0])
    normed1 = land(normed1, front, middle, rising, falling)
    normed1 = launch(normed1, front, middle, falling)
    s_halves = [x.reshape(width, -1) for x in finish(front)]
    here = core.astype(jnp.int32).reshape(1)

    def projected(x, w, outer):
        return project(x, w, 3 * half, here).reshape(*outer, -1)

    spatial = [projected(normed1, w, (frames_local, slots)) for w in s_halves]
    spatial = land(spatial, middle, falling)
    spatial = launch(spatial, middle, rising)

    def frame_index(i):
        return (i, 0, 0)

    def slot_index(i):
        return (0, i, 0)

    spatial_place = (
        jnp.stack([sides[0], core.astype(jnp.int32)]), (1, slots), frames_local, frame_index,
    )
    (s_mixed,) = run_attention(
        partial(attention_forward, spatial_bias), *spatial_place, spatial, [width]
    )
    s_mixed = s_mixed.reshape(row_count, width)
    flat = tokens.reshape(row_count, width)
    hidden1 = add_spatial(s_mixed, s_halves, flat, embedded, here)

    hidden1 = hold(hidden1, middle, rising)
    parts = to_slots(hidden1.reshape(tokens.shape))
    parts[1] = along(parts[1], middle, rising)
    parts = land(parts, middle, rising)
    hidden1 = in_slots(parts)
    frames = hidden1.shape[0]
    slot_at = place.tm * slots_local + jnp.arange(slots_local)
    mask = (slot_at < sides[0] * sides[0])[None, :, None]
    nothing = jnp.zeros((1, 1, width), f32)
    normed2 = norm(hidden1, nothing, gains[1], shifts[1])
    hidden1 = hidden1.reshape(row_count, width)
    normed2 = launch(normed2, rising, falling)
    t_halves = [x.reshape(width, -1) for x in finish(middle)]
    temporal = [projected(normed2, w, (frames, slots_local)) for w in t_halves]
    temporal_place = (
        jnp.stack([place.tm.astype(jnp.int32), core.astype(jnp.int32)]), (frames, GROUP),
        slots_local // GROUP, slot_index,
    )
    make_bias = partial(temporal_bias, frames_local)
    (t_mixed,) = run_attention(
        partial(attention_forward, make_bias), *temporal_place, temporal, [width]
    )
    t_mixed = t_mixed.reshape(row_count, width)
    hidden2, normed3 = add_temporal(t_mixed, t_halves, hidden1, gains[2], shifts[2], here)
    normed3 = along(normed3, rising, falling)
    up_halves = [x.reshape(width, -1) for x in finish(rising)]
    first = up_project(normed3, up_halves[0], up_bias[0])
    first = along(first, falling)
    normed3, first = lax.optimization_barrier((normed3, first))
    second = up_project(normed3, up_halves[1], up_bias[1])
    (active, slope), (active2, slope2) = first, second

    core_pair = (place.core_bit, place.core_bit)

    def exchanged(grad):
        return place.flip(grad, core_pair)

    def sums(*parts):
        return Chain(scatter(place, lambda k, value: weight_split(parts, k, value, core)))

    down_in = jnp.where(mask, in_slots(cotangent), 0).reshape(row_count, width)
    send = weight_grad(active2, down_in, total, here)
    down_in, send = land((down_in, send), falling)
    own_rows = falling.pending[0].reshape(-1, width)
    down_in, send = launch(down_in, falling, also=[send])
    got = exchanged(send)
    inner_grad, b_sum = inner_back(down_in, own_rows, slope, here)
    hidden2, inner_grad = land((hidden2, inner_grad), falling)
    down_halves = [x.reshape(-1, width) for x in finish(falling)]
    mask_rows = jnp.broadcast_to(mask, (frames, slots_local, 1)).reshape(row_count, 1).astype(f32)
    mixed = down_project([active, active2], down_halves, hidden2, down_bias, mask_rows, here)
    down_in, mixed, got = lax.optimization_barrier((down_in, mixed, got))
    s_down = sums((active, down_in, got, None))
    down_in = launch(down_in, s_down)

    inner_grad2, b_sum2 = inner_back(down_in, down_halves[1], slope2, here)
    send = weight_grad(normed3, inner_grad2, total, here)
    inner_grads = (inner_grad, inner_grad2)
    grad2, sums3 = norm_back(
        inner_grads, up_halves, hidden2, nothing, gains[2], down_in, bf16, here
    )
    grad2, send = land((grad2, send), s_down)
    grad2, send = launch(grad2, s_down, also=[send])
    got = exchanged(send)
    b_sums = [x.reshape(total, -1, thin).swapaxes(0, 1) for x in (b_sum, b_sum2)]
    late_rows = [x.reshape(-1, width) for x in b_sums]
    late_rows = jnp.where(
        core == 0, jnp.concatenate(late_rows, axis=0), jnp.concatenate(late_rows[::-1], axis=0)
    )
    late_rows = jnp.concatenate([jnp.sum(down_in.astype(f32), axis=0)[None], late_rows], axis=0)

    t_mix_grad = mixed_back(grad2, t_halves, here)
    send2 = weight_grad(t_mixed, grad2, total, here, 1)
    (t_mix_grad, send2), got = land((t_mix_grad, send2), s_down, also=[got])
    s_up = sums((normed3, inner_grad, got, None))
    t_mix_grad = launch(t_mix_grad, s_down, s_up)
    t_mix_grad = t_mix_grad.reshape(frames, slots_local, width)

    def back(side, where, make, values, grad):
        (out,) = run_attention(
            partial(attention_backward, make, (side,)), *where, [values[side], grad], [3 * half]
        )
        return out.reshape(row_count, -1)

    t_grad2 = back(1, temporal_place, make_bias, temporal, t_mix_grad)
    send = weight_grad(normed2, t_grad2, total, here)
    t_grad = back(0, temporal_place, make_bias, temporal, t_mix_grad)
    t_grads = land((t_grad, t_grad2), s_down, s_up)
    t_grads, send, send2 = launch(t_grads, s_down, s_up, also=[send, send2])
    gots = [exchanged(send), exchanged(send2)]

    grad1, sums2 = norm_back(t_grads, t_halves, hidden1, nothing, gains[1], grad2, bf16, here)
    grad1 = hold(grad1, s_down, s_up)
    grad1, gots = lax.optimization_barrier((grad1, gots))
    parts = from_slots(grad1)
    parts[1] = along(parts[1], s_down, s_up)
    s_time = sums((normed2, t_grads[0], gots[0], None), (t_mixed, grad2, gots[1], 0))
    parts[0], s_time.pending = lax.optimization_barrier((parts[0], s_time.pending))
    parts = land(parts, s_down, s_up)
    grad1 = in_frames(parts).reshape(row_count, width)
    grad1 = launch(grad1, s_down, s_up, s_time)

    send2 = weight_grad(s_mixed, grad1, total, here, 1)
    mix_grad = mixed_back(grad1, s_halves, here).reshape(frames_local, slots, width)
    s_grad2 = back(1, spatial_place, spatial_bias, spatial, mix_grad)
    send = weight_grad(normed1, s_grad2, total, here)
    mix_grad, send, send2 = land((mix_grad, send, send2), s_down, s_up, s_time)
    mix_grad, send, send2 = launch(mix_grad, s_down, s_up, s_time, also=[send, send2])
    gots = [exchanged(send), exchanged(send2)]

    s_grad = back(0, spatial_place, spatial_bias, spatial, mix_grad)
    s_grad, *gots = land(s_grad, s_down, s_up, s_time, also=gots)
    s_space = sums((normed1, s_grad, gots[0], None), (s_mixed, grad1, gots[1], 0))
    s_grads = launch((s_grad, s_grad2), s_time, s_space)

    input_grad, sums1 = norm_back(
        s_grads, s_halves, flat, embedded, gains[0], grad1, f32, here
    )
    sums1, input_grad = land((sums1, input_grad), s_time, s_space)
    sums1, input_grad = launch((sums1, input_grad), s_time, s_space)
    g_actions = jnp.sum(onehot[:, :, None] * sums1[:, 2][:, None, :], axis=0)
    all_sums = [jnp.sum(x[:, :2], axis=0) for x in (sums1, sums2, sums3)]
    both_norms = [jnp.stack([x[i] for x in all_sums]) for i in (0, 1)]
    packed = jnp.concatenate([g_actions, *both_norms, late_rows], axis=0)
    s_small = Chain(scatter_small(place, packed))
    packed = launch(packed, s_small)
    packed = land(packed, s_time, s_space, s_small)
    packed, mixed = launch((packed, mixed), s_time, s_space, s_small)
    near = from_slots(mixed, range(tm_size // 2 + 1))
    packed, down_sums, up_sums = lax.optimization_barrier((packed, finish(s_down), finish(s_up)))
    g_w_down = in_order(*down_sums, 0).reshape(w_down.shape)
    g_w_up = in_order(*[x.reshape(rows, total, -1) for x in up_sums], 2).reshape(w_up.shape)
    packed = along(packed, s_small)
    packed, *near = land(packed, s_time, s_space, s_small, also=near)
    packed, mixed = launch((packed, mixed), s_time, s_space, s_small)
    packed, g_w_down, g_w_up = lax.optimization_barrier((packed, g_w_down, g_w_up))
    far = from_slots(mixed, range(tm_size // 2 + 1, tm_size))
    packed = along(packed, s_small)
    packed, *far = land(packed, s_time, s_space, s_small, also=far)
    packed = launch(packed, s_time, s_space, s_small)
    mixed = in_frames(near + far)
    packed, mixed = lax.optimization_barrier((packed, mixed))
    while not (s_time.done() and s_space.done() and s_small.done()):
        packed = along(packed, s_time, s_space, s_small)
    summed = s_small.result
    t_rows, s_rows = woven(*s_time.result), woven(*s_space.result)
    g_t_qkv, g_t_out = t_rows[:, : 3 * width], t_rows[:, 3 * width :]
    g_s_qkv, g_s_out = s_rows[:, : 3 * width], s_rows[:, 3 * width :]

    return (
        mixed.reshape(shape),
        input_grad.reshape(shape),
        summed[:8],
        summed[8:11],
        summed[11:14],
        g_s_qkv,
        g_s_out,
        g_t_qkv,
        g_t_out,
        g_w_up,
        summed[15:].reshape(-1),
        g_w_down,
        summed[14],
    )


def solution(mesh):
    whole = P(("tm", "clip"), None)
    spread = P(None, ("tm", "clip"))
    frames = P("tm", "clip", None, None)
    vector = P(("tm", "clip"))
    return jax.shard_map(
        on_device,
        mesh=mesh,
        in_specs=(
            frames, P("tm", "clip"), P("clip"), spread, spread, spread, whole, whole, whole,
            whole, whole, vector, whole, vector, frames,
        ),
        out_specs=(
            frames, frames, spread, spread, spread, whole, whole, whole, whole, whole, vector,
            whole, vector,
        ),
        check_vma=False,
    )
```

```python
import math
from functools import partial

import jax
import jax.numpy as jnp
from jax import lax
from jax.experimental import pallas as pl
from jax.experimental.pallas import tpu as pltpu
from jax.sharding import PartitionSpec as P

H = 16
E = 64
ACTIONS = 8
FRAMES = 16
AXES = ("tm", "clip")
LANES = 128
GROUP = 16

negative = -1e30
highest = lax.Precision.HIGHEST
MIB = 1024 * 1024
bf16, f32 = jnp.bfloat16, jnp.float32
NO_COST = pl.CostEstimate(flops=0, bytes_accessed=0, transcendentals=0)


def params(blocks, margin=6):
    size = sum(math.prod(shape) * jnp.dtype(dtype).itemsize * n for shape, dtype, n in blocks)
    return pltpu.CompilerParams(vmem_limit_bytes=(-(-size // MIB) + margin) * MIB)


class Place:
    def __init__(self):
        tm_size, clip_size = lax.axis_size("tm"), lax.axis_size("clip")
        self.tm_size, self.clip_size, self.total = tm_size, clip_size, tm_size * clip_size
        self.tm = lax.axis_index("tm")
        self.me = self.tm * clip_size + lax.axis_index("clip")
        self.core_bit = clip_size
        self.core = self.bit_of(clip_size)
        clip_bits = [1 << i for i in range(clip_size.bit_length() - 1)]
        tm_bits = [clip_size << i for i in range(tm_size.bit_length() - 1)]
        x, z, y = clip_bits[:-2], clip_bits[-2:], tm_bits[1:]
        self.z = [(b, b) for b in z]
        self.xy = list(zip(x + y, y + x))

    def bit_of(self, bit):
        return (self.me // bit) % 2

    def mine(self, pair):
        return jnp.where(self.core == 0, self.bit_of(pair[0]), self.bit_of(pair[1]))

    def choose(self, pair):
        return jnp.where(self.core == 0, pair[0], pair[1])

    def flip(self, value, pair):
        moves = [(i, i ^ pair[(i // self.core_bit) % 2]) for i in range(self.total)]
        return lax.ppermute(value, AXES, moves)

    def tm_flip(self, value, offset):
        moves = [(i, i ^ (offset * self.clip_size)) for i in range(self.total)]
        return lax.ppermute(value, AXES, moves)


def below(have, bit):
    return sum(1 for b in have if b < bit)


def unscramble(parts, me):
    bit = 1
    while bit < len(parts):
        swap = (me & bit) != 0
        parts = [jnp.where(swap, parts[p ^ bit], parts[p]) for p in range(len(parts))]
        bit *= 2
    return parts


def position(m, value, k):
    m = jnp.int32(m)
    high = lax.shift_left(lax.shift_right_logical(m, k), k + 1)
    return high | lax.shift_left(value, k) | (m & (lax.shift_left(jnp.int32(1), k) - 1))


def merge_body(info_ref, mine_ref, other_ref, out_ref):
    k, value = info_ref[0], info_ref[1]
    for m in range(mine_ref.shape[0]):
        out_ref[position(m, value, k)] = mine_ref[m]
        out_ref[position(m, 1 - value, k)] = other_ref[m]


def column_block(shape):
    blocks, rows, cols = shape
    return cols if blocks * rows * cols <= 512 * 1024 else min(cols, 512)


def merge(mine, other, k, value):
    m, r, n = mine.shape
    block = column_block((2 * m, r, n))
    spec = pl.BlockSpec((m, r, block), lambda j: (0, 0, j))
    return pl.pallas_call(
        merge_body,
        grid=(n // block,),
        in_specs=[pl.BlockSpec(memory_space=pltpu.SMEM), spec, spec],
        out_specs=pl.BlockSpec((2 * m, r, block), lambda j: (0, 0, j)),
        out_shape=jax.ShapeDtypeStruct((2 * m, r, n), mine.dtype),
        compiler_params=params([((4 * m, r, block), mine.dtype, 2)], 2),
        cost_estimate=NO_COST,
    )(jnp.stack([jnp.int32(k), value.astype(jnp.int32)]), mine, other)


def part(info_ref, source_ref, send_ref, keep_ref):
    k, value = info_ref[0], info_ref[1]
    for m in range(send_ref.shape[0]):
        for out_ref, at in ((send_ref, 1 - value), (keep_ref, value)):
            out_ref[m] = source_ref[position(m, at, k)].astype(out_ref.dtype)


def split_body(info_ref, a_ref, b_ref, send_ref, keep_ref):
    k, value = info_ref[0], info_ref[1]
    for m in range(send_ref.shape[0]):
        for out_ref, at in ((send_ref, 1 - value), (keep_ref, value)):
            i = position(m, at, k)
            out_ref[m] = (a_ref[i].astype(f32) + b_ref[i].astype(f32)).astype(out_ref.dtype)


def split(a, b, k, value, dtype):
    blocks, r, n = a.shape
    block = column_block(a.shape)
    out = jax.ShapeDtypeStruct((blocks // 2, r, n), dtype)
    return pl.pallas_call(
        split_body,
        grid=(n // block,),
        in_specs=[pl.BlockSpec(memory_space=pltpu.SMEM)]
        + [pl.BlockSpec((blocks, r, block), lambda j: (0, 0, j))] * 2,
        out_specs=[pl.BlockSpec((blocks // 2, r, block), lambda j: (0, 0, j))] * 2,
        out_shape=[out, out],
        compiler_params=params([((3 * blocks, r, block), dtype, 2)], 3),
        cost_estimate=NO_COST,
    )(jnp.stack([jnp.int32(k), value.astype(jnp.int32)]), a, b)


def gather_small(place, value):
    core = (place.core_bit, place.core_bit)
    x_and_y = [(b, b) for b, _ in place.xy]
    count = len(x_and_y) // 2
    blocks, have = value[None], []
    for pair in x_and_y[:count] + [core] + x_and_y[count:] + place.z:
        (send,) = yield [blocks]
        (got,) = yield [place.flip(send, pair)]
        blocks = merge(blocks, got, below(have, pair[0]), place.bit_of(pair[0]))
        have.append(pair[0])
    return blocks


def scatter_small(place, value):
    bit = place.total // 2
    while bit:
        half = value.shape[1] // 2
        low_half, high_half = value[:, :half], value[:, half:]
        mine = (place.me & bit) != 0
        (send,) = yield [jnp.where(mine, low_half, high_half)]
        (got,) = yield [place.flip(send, (bit, bit))]
        value = jnp.where(mine, high_half, low_half) + got
        bit //= 2
    return value


def gather(place, keep, send, ahead=0):
    core = (place.core_bit, place.core_bit)
    have = ([], [])
    blocks, out = keep[None], send[None]
    for pair in [core] + place.xy[:ahead] + place.z[::-1] + place.xy[ahead:]:
        (out,) = yield [out]
        (got,) = yield [place.flip(out, pair)]
        k = [below(h, b) for h, b in zip(have, pair)]
        blocks = out = merge(blocks, got, place.choose(k), place.mine(pair))
        have = (have[0] + [pair[0]], have[1] + [pair[1]])
    (out,) = yield [out]
    (got,) = yield [place.flip(out, core)]
    return blocks, got


def scatter(place, first):
    core = (place.core_bit, place.core_bit)
    bits = [1 << i for i in range(place.total.bit_length() - 1)]
    have, pairs = (bits, bits), None
    for pair in place.xy[::-1] + place.z + [core]:
        have = tuple([b for b in h if b != bit] for h, bit in zip(have, pair))
        k = place.choose([below(h, b) for h, b in zip(have, pair)])
        dtype = f32 if pair == core else bf16
        if pairs is None:
            send, keep = first(k, place.mine(pair))
        else:
            send, keep = split(*pairs, k, place.mine(pair), dtype)
        (send,) = yield [send]
        (got,) = yield [place.flip(send, pair)]
        pairs = (keep, got)
    return keep[0], got[0]


class Chain:
    def __init__(self, steps):
        self.steps, self.flying, self.result = steps, False, None
        self.pending = next(steps)

    def done(self):
        return self.result is not None

    def move(self):
        try:
            self.pending = self.steps.send(self.pending)
        except StopIteration as stop:
            self.result = stop.value
        self.flying = not self.flying


def hold(value, *chains):
    chains = [c for c in chains if c.flying]
    value, got = lax.optimization_barrier((value, [c.pending for c in chains]))
    for c, g in zip(chains, got):
        c.pending = g
    return value


def land(value, *chains, also=()):
    chains = [c for c in chains if c.flying]
    value, got, also = lax.optimization_barrier((value, [c.pending for c in chains], list(also)))
    for c, g in zip(chains, got):
        c.pending = g
        c.move()
    return (value, *also) if also else value


def launch(value, *chains, also=()):
    chains = [c for c in chains if not c.done() and not c.flying]
    value, sent, also = lax.optimization_barrier((value, [c.pending for c in chains], list(also)))
    for c, g in zip(chains, sent):
        c.pending = g
        c.move()
    return (value, *also) if also else value


def along(value, *chains):
    return launch(land(value, *chains), *chains)


def finish(chain):
    while not chain.done():
        chain.move()
    return chain.result


def spatial_bias(scalar, rows, keys):
    key = lax.broadcasted_iota(jnp.int32, (1, rows) if keys == 1 else (rows, 1), keys)
    return jnp.where(key < scalar * scalar, 0.0, negative)


def temporal_bias(frames_local, scalar, rows, keys):
    def place(axis):
        index = lax.broadcasted_iota(jnp.int32, (rows, rows), axis)
        slot, at = index % GROUP, index // GROUP
        frame = ((at // frames_local) ^ scalar) * frames_local + at % frames_local
        return slot, frame

    slot_q, frame_q = place(1 - keys)
    slot_k, frame_k = place(keys)
    return jnp.where((slot_q == slot_k) & (frame_q >= frame_k), 0.0, negative)


def dot_t(a, b):
    return lax.dot_general(a, b, (((1,), (1,)), ((), ())), preferred_element_type=f32)


def t_dot(a, b):
    return lax.dot_general(a, b, (((0,), (0,)), ((), ())), preferred_element_type=f32)


def columns(scalar_ref, side, start):
    half = H * E // 2
    return pl.ds(pl.multiple_of((scalar_ref[1] ^ side) * half + start, LANES), LANES)


def two_heads(rows):
    half = lax.broadcasted_iota(jnp.int32, (rows, LANES), 1) < E

    def apart(x):
        return jnp.concatenate([jnp.where(half, x, 0), jnp.where(half, 0, x)], axis=0)

    def together(x):
        return jnp.where(half, x[:rows], x[rows:])

    return apart, together


def head_pairs(sides, refs):
    a, b, width = refs[0].shape
    rows, width = a * b, width // 3
    for i, side in enumerate(sides):
        for c in range(0, width, LANES):
            q, k, v = (
                refs[i][:, :, at : at + LANES].reshape(rows, LANES)
                for at in (c, width + c, 2 * width + c)
            )
            yield i, side, c, q * bf16(E ** (-0.5)), k, v


def in_turn(items, first, last):
    waiting = None
    for item in items:
        ready = first(*item)
        if waiting is not None:
            last(*waiting)
        waiting = ready
    last(*waiting)


def attention_forward(make_bias, scalar_ref, own_ref, other_ref, out_ref):
    a, b, width = own_ref.shape
    rows, width = a * b, width // 3
    bias = make_bias(scalar_ref[0], rows, 1)
    apart, together = two_heads(rows)

    def first(i, side, c, q, k, v):
        scores = dot_t(apart(q), k).reshape(2, rows, rows) + bias[None]
        weights = jnp.exp(scores - jnp.max(scores, axis=2, keepdims=True))
        scale = 1.0 / jnp.sum(weights, axis=2, keepdims=True)
        return side, c, v, weights.astype(bf16).reshape(2 * rows, rows), scale

    def last(side, c, v, weights, scale):
        mixed = jnp.dot(weights, v, preferred_element_type=f32) * scale.reshape(2 * rows, 1)
        mixed = together(mixed).astype(out_ref.dtype)
        out_ref[:, :, columns(scalar_ref, side, c)] = mixed.reshape(a, b, LANES)

    in_turn(head_pairs((0, 1), (own_ref, other_ref)), first, last)


def attention_backward(make_bias, sides, scalar_ref, *refs):
    grad_ref = refs[len(sides)]
    a, b, width = refs[0].shape
    rows, width = a * b, width // 3
    bias = make_bias(scalar_ref[0], rows, 0)
    apart, together = two_heads(rows)

    def first(i, side, c, q, k, v):
        g = grad_ref[:, :, columns(scalar_ref, side, c)].reshape(rows, LANES)
        scores = dot_t(apart(k), q).reshape(2, rows, rows) + bias[None]
        prob_grad = dot_t(apart(v), g).reshape(2, rows, rows)
        weights = jnp.exp(scores - jnp.max(scores, axis=1, keepdims=True))
        probs = weights * (1.0 / jnp.sum(weights, axis=1, keepdims=True))
        delta = jnp.sum(probs * prob_grad, axis=1, keepdims=True)
        return i, c, q, k, g, probs.astype(bf16), (probs * (prob_grad - delta)).astype(bf16)

    def last(i, c, q, k, g, probs, score_grad):
        turned = jnp.concatenate([score_grad[0].T, score_grad[1].T], axis=0)
        dq = jnp.dot(turned, k, preferred_element_type=f32) * E ** (-0.5)
        dk = jnp.dot(score_grad.reshape(2 * rows, rows), q, preferred_element_type=f32)
        dv = jnp.dot(probs.reshape(2 * rows, rows), g, preferred_element_type=f32)
        for index, grad in enumerate((dq, dk, dv)):
            start = index * width + c
            merged = together(grad).astype(bf16).reshape(a, b, LANES)
            refs[len(sides) + 1 + i][:, :, start : start + LANES] = merged

    in_turn(head_pairs(sides, refs), first, last)


def run_attention(body, scalars, block, grid, index, inputs, out_widths):
    a, b = block
    outer = inputs[0].shape[:2]
    return pl.pallas_call(
        body,
        grid=(grid,),
        in_specs=[pl.BlockSpec(memory_space=pltpu.SMEM)]
        + [pl.BlockSpec((a, b, x.shape[-1]), index) for x in inputs],
        out_specs=[pl.BlockSpec((a, b, width), index) for width in out_widths],
        out_shape=[jax.ShapeDtypeStruct((*outer, width), bf16) for width in out_widths],
        compiler_params=params(
            [((a, b, width), bf16, 2) for width in (*(x.shape[-1] for x in inputs), *out_widths)], 8
        ),
        cost_estimate=NO_COST,
    )(scalars, *inputs)


def centre(x):
    average = jnp.mean(x, axis=-1, keepdims=True)
    centered = x - average
    variance = jnp.mean(centered * centered, axis=-1, keepdims=True)
    scale = lax.rsqrt(variance + 1e-05)
    return centered * scale, scale


def norm_body(x_ref, added_ref, gain_ref, shift_ref, out_ref):
    unit, _ = centre(x_ref[0].astype(f32) + added_ref[0])
    out_ref[0] = (unit * gain_ref[...] + shift_ref[...]).astype(out_ref.dtype)


def by_rows(body, arrays, rows, outs):
    blocks = arrays[0].shape[0]
    specs = []
    for x in arrays:
        if x.ndim == 2:
            specs.append(pl.BlockSpec(x.shape, lambda i: (0, 0)))
        else:
            at = (lambda i: (i, 0, 0)) if x.shape[0] == blocks else (lambda i: (0, 0, 0))
            specs.append(pl.BlockSpec((1, *x.shape[1:]), at))
    return pl.pallas_call(
        body,
        grid=(blocks,),
        in_specs=specs,
        out_specs=[pl.BlockSpec((1, *shape[1:]), lambda i: (i, 0, 0)) for shape, _ in outs],
        out_shape=[jax.ShapeDtypeStruct(shape, dtype) for shape, dtype in outs],
        compiler_params=params([(x.shape[1:], f32, 4) for x in arrays]),
        cost_estimate=NO_COST,
    )(*arrays)


def norm(x, added, gain, shift):
    shape = (x.shape[0] * x.shape[1] // 256, 256, x.shape[2])
    arrays = [x.reshape(shape), added, gain[None], shift[None]]
    (out,) = by_rows(norm_body, arrays, 256, [(shape, bf16)])
    return out.reshape(-1, shape[2])


BLOCK = 512


def dense(body, grid, scalars, inputs, outs, scratch=(), margin=6):
    used = [(block, x.dtype, 1 if index is FIXED else 2) for x, block, index in inputs]
    used += [(block, dtype, 2) for _, dtype, block, _ in outs]
    used += [(x.shape, x.dtype, 1) for x in scratch]

    def spec(block, index):
        if index is FIXED:
            zeros = (0,) * len(block)
            return pl.BlockSpec(block, lambda *_: zeros, pipeline_mode=pl.Buffered(1))
        return pl.BlockSpec(block, index)

    return pl.pallas_call(
        body,
        grid_spec=pltpu.PrefetchScalarGridSpec(
            num_scalar_prefetch=1,
            grid=grid,
            in_specs=[spec(block, index) for _, block, index in inputs],
            out_specs=[pl.BlockSpec(block, index) for _, _, block, index in outs],
            scratch_shapes=list(scratch),
        ),
        out_shape=[jax.ShapeDtypeStruct(shape, dtype) for shape, dtype, _, _ in outs],
        compiler_params=params(used, margin),
        cost_estimate=NO_COST,
    )(scalars, *[x for x, _, _ in inputs])


FIXED = None


def at(*index):
    return lambda j, ref: index


def whole(x):
    return (x, x.shape, FIXED)


def rows_of(x, rows=256):
    return (x, (rows, x.shape[1]), lambda i, ref: (i, 0))


def project_body(_, x_ref, w_ref, out_ref):
    out_ref[...] = jnp.dot(x_ref[...], w_ref[...], preferred_element_type=f32).astype(bf16)


def project(x, w, cols, scalars):
    index = lambda j, ref: (0, j)
    rows = x.shape[0]
    (out,) = dense(
        project_body, (cols // BLOCK,), scalars,
        [whole(x), (w, (w.shape[0], BLOCK), index)],
        [((rows, cols), bf16, (rows, BLOCK), index)],
    )
    return out


def sides(core, own_ref, other_ref):
    for side, ref in ((core, own_ref), (1 - core, other_ref)):
        yield pl.ds(pl.multiple_of(side * BLOCK, BLOCK), BLOCK), ref


def hidden1_body(core_ref, mixed_ref, own_ref, other_ref, x_ref, added_ref, out_ref):
    for cols, w_ref in sides(core_ref[0], own_ref, other_ref):
        dot = jnp.dot(mixed_ref[...], w_ref[...], preferred_element_type=f32)
        out_ref[:, cols] = (x_ref[:, cols].astype(f32) + added_ref[0, :, cols] + dot).astype(bf16)


def out_half(w):
    return (w, (w.shape[0], BLOCK), at(0, w.shape[1] // BLOCK - 1))


def add_spatial(mixed, halves, x, added, scalars):
    rows, width = x.shape
    step = rows // added.shape[0]
    (out,) = dense(
        hidden1_body, (rows // step,), scalars,
        [rows_of(mixed, step), *[out_half(w) for w in halves], rows_of(x, step),
         (added, (1, 1, width), lambda i, ref: (i, 0, 0))],
        [((rows, width), bf16, (step, width), lambda i, ref: (i, 0))],
    )
    return out


def hidden2_body(
    core_ref, mixed_ref, own_ref, other_ref, x_ref, gain_ref, shift_ref, out_ref, norm_ref
):
    for cols, w_ref in sides(core_ref[0], own_ref, other_ref):
        dot = jnp.dot(mixed_ref[...], w_ref[...], preferred_element_type=f32)
        out_ref[:, cols] = x_ref[:, cols].astype(f32) + dot
    unit, _ = centre(out_ref[...])
    norm_ref[...] = (unit * gain_ref[...] + shift_ref[...]).astype(bf16)


def add_temporal(mixed, halves, x, gain, shift, scalars):
    rows, width = x.shape
    block = ((256, width), lambda i, ref: (i, 0))
    return dense(
        hidden2_body, (rows // 256,), scalars,
        [rows_of(mixed), *[out_half(w) for w in halves], rows_of(x), whole(gain[None]),
         whole(shift[None])],
        [((rows, width), f32, *block), ((rows, width), bf16, *block)],
    )


def hidden3_body(_, a_ref, b_ref, own_ref, other_ref, x_ref, bias_ref, mask_ref, out_ref):
    out = x_ref[...] + bias_ref[...]
    out += jnp.dot(a_ref[...], own_ref[...], preferred_element_type=f32)
    out += jnp.dot(b_ref[...], other_ref[...], preferred_element_type=f32)
    out_ref[...] = jnp.where(mask_ref[...] > 0, out, 0).astype(bf16)


def down_project(actives, halves, x, bias, mask, scalars):
    rows, width = x.shape
    (out,) = dense(
        hidden3_body, (rows // 256,), scalars,
        [*[rows_of(y) for y in actives], *[whole(w) for w in halves], rows_of(x), whole(bias),
         rows_of(mask)],
        [((rows, width), bf16, (256, width), lambda i, ref: (i, 0))], margin=30,
    )
    return out


def inner_back_body(_, x_ref, w_ref, slope_ref, out_ref, sum_ref):
    grad = dot_t(x_ref[...], w_ref[...]) * slope_ref[...].astype(f32)
    out_ref[...] = grad.astype(bf16)
    sum_ref[...] = jnp.sum(out_ref[...].astype(f32), axis=0, keepdims=True)


def inner_back(x, w, slope, scalars):
    rows, cols = slope.shape
    index = lambda j, ref: (0, j)
    return dense(
        inner_back_body, (cols // BLOCK,), scalars,
        [whole(x), (w, (BLOCK, w.shape[1]), lambda j, ref: (j, 0)), (slope, (rows, BLOCK), index)],
        [((rows, cols), bf16, (rows, BLOCK), index), ((1, cols), f32, (1, BLOCK), index)],
    )


def norm_back_body(
    _, a_ref, b_ref, own_ref, other_ref, x_ref, added_ref, gain_ref, rest_ref, out_ref, sums_ref
):
    grad = dot_t(a_ref[...], own_ref[...]) + dot_t(b_ref[...], other_ref[...])
    unit, scale = centre(x_ref[...].astype(f32) + added_ref[0])
    scaled = grad * gain_ref[...]
    first = jnp.mean(scaled, axis=-1, keepdims=True)
    second = jnp.mean(scaled * unit, axis=-1, keepdims=True)
    out = rest_ref[...].astype(f32) + scale * (scaled - first - unit * second)
    out_ref[...] = out.astype(out_ref.dtype)
    terms = (grad * unit, grad, out)
    sums_ref[0] = jnp.concatenate([jnp.sum(x, axis=0, keepdims=True) for x in terms], axis=0)


def norm_back(grads, halves, x, added, gain, rest, dtype, scalars):
    rows, width = x.shape
    step, cols = 256, grads[0].shape[1]
    added_at = (lambda i, ref: (i, 0, 0)) if added.shape[0] > 1 else at(0, 0, 0)
    return dense(
        norm_back_body, (rows // step,), scalars,
        [*[rows_of(g) for g in grads], *[(w, (w.shape[0], cols), FIXED) for w in halves],
         rows_of(x), (added, (1, 1, width), added_at), whole(gain[None]), rows_of(rest)],
        [((rows, width), dtype, (step, width), lambda i, ref: (i, 0)),
         ((rows // step, 3, width), f32, (1, 3, width), lambda i, ref: (i, 0, 0))],
        margin=30 if dtype == f32 or cols > 3 * BLOCK else 6,
    )


def mixed_back_body(core_ref, x_ref, own_ref, other_ref, out_ref):
    grad = 0
    for cols, w_ref in sides(core_ref[0], own_ref, other_ref):
        grad += dot_t(x_ref[:, cols], w_ref[...])
    out_ref[...] = grad.astype(bf16)


def mixed_back(x, halves, scalars):
    rows, width = x.shape
    last = halves[0].shape[1] // BLOCK - 1
    (out,) = dense(
        mixed_back_body, (width // BLOCK,), scalars,
        [whole(x), *[(w, (BLOCK, BLOCK), lambda j, ref: (j, last)) for w in halves]],
        [((rows, width), bf16, (rows, BLOCK), lambda j, ref: (0, j))],
    )
    return out


def weight_grad_body(_, x_ref, y_ref, out_ref):
    out_ref[...] = t_dot(x_ref[...], y_ref[...]).astype(bf16).reshape(out_ref.shape)


def weight_grad(x, y, total, scalars, half=None):
    rows, count = x.shape
    cols = y.shape[1] if half is None else BLOCK
    shift = (lambda j, ref: (0, j)) if half is None else (lambda j, ref: (0, ref[0] ^ half))
    shape = (total, count // total)
    (out,) = dense(
        weight_grad_body, (cols // BLOCK,), scalars,
        [whole(x), (y, (rows, BLOCK), shift)],
        [((*shape, cols), bf16, (*shape, BLOCK), lambda j, ref: (0, 0, j))],
    )
    return out


def weight_split_body(ends, info_ref, *refs):
    send_ref, keep_ref, sum_ref = refs[-3:]
    step = pl.program_id(0)
    for p in range(len(ends) - 1):

        @pl.when((step >= ends[p]) & (step < ends[p + 1]))
        def _(x_ref=refs[3 * p], y_ref=refs[3 * p + 1], got_ref=refs[3 * p + 2]):
            grad = t_dot(x_ref[...], y_ref[...]).reshape(sum_ref.shape)
            sum_ref[...] = grad + got_ref[...].astype(f32)

    part(info_ref, sum_ref, send_ref, keep_ref)


def weight_split(parts, k, value, core):
    scalars = jnp.stack([jnp.int32(k), value.astype(jnp.int32), core.astype(jnp.int32)])
    total, r, _ = parts[0][2].shape
    widths = [got.shape[2] for _, _, got, _ in parts]
    ends = [sum(widths[:i]) // BLOCK for i in range(len(parts) + 1)]
    inputs = []
    for (x, y, got, half), low, high in zip(parts, ends[:-1], ends[1:]):
        place = lambda j, low=low, high=high: jnp.clip(j - low, 0, high - low - 1)
        if half is None:
            index = lambda j, ref, place=place: (0, place(j))
        else:
            index = lambda j, ref, half=half: (0, ref[2] ^ half)
        inputs += [
            whole(x),
            (y, (y.shape[0], BLOCK), index),
            (got, (total, r, BLOCK), lambda j, ref, place=place: (0, 0, place(j))),
        ]
    shape = (total // 2, r)
    out = ((*shape, sum(widths)), bf16, (*shape, BLOCK), lambda j, ref: (0, 0, j))
    return dense(
        partial(weight_split_body, ends), (ends[-1],), scalars, inputs, [out, out],
        [pltpu.VMEM((total, r, BLOCK), f32)],
    )


TAIL = (
    0.14760860800743103, 0.14761532843112946, 0.127163827419281, 0.09018292278051376,
    0.013407237827777863, 0.06451446563005447, -0.19429759681224823, 0.13513216376304626,
    -0.031326886266469955,
)


def gelu(inner):
    size = 1.0 + 0.37 * jnp.abs(inner)
    t = pl.reciprocal(size, approx=True)
    t = t * (2.0 - size * t)
    bell = jnp.exp2(inner * inner * -0.7213475204444817)
    series = TAIL[-1]
    for term in reversed(TAIL[:-1]):
        series = series * t + term
    tail = series * t * bell
    cdf = jnp.where(inner > 0, 1.0 - tail, tail)
    return inner * cdf, cdf + inner * bell * 0.3989422804014327


def up_body(x_ref, w_ref, bias_ref, active_ref, slope_ref):
    rows = x_ref.shape[0]
    step = min(rows, 128)
    for r in range(0, rows, step):
        inner = jnp.dot(x_ref[r : r + step], w_ref[...], preferred_element_type=f32)
        active, slope = gelu(inner + bias_ref[...])
        active_ref[r : r + step] = active.astype(active_ref.dtype)
        slope_ref[r : r + step] = slope.astype(slope_ref.dtype)


def up_project(x, weight, bias):
    rows, width = x.shape
    cols, block = weight.shape[1], 512
    out = jax.ShapeDtypeStruct((rows, cols), bf16)
    return pl.pallas_call(
        up_body,
        grid=(cols // block,),
        in_specs=[
            pl.BlockSpec((rows, width), lambda i: (0, 0)),
            pl.BlockSpec((width, block), lambda i: (0, i)),
            pl.BlockSpec((1, block), lambda i: (0, i)),
        ],
        out_specs=[pl.BlockSpec((rows, block), lambda i: (0, i))] * 2,
        out_shape=[out, out],
        compiler_params=params(
            [(x.shape, bf16, 2), ((width, block), bf16, 2), ((rows, block), bf16, 4)]
        ),
        cost_estimate=NO_COST,
    )(x, weight, bias)


def on_device(
    tokens,
    actions,
    sides,
    action_table,
    norm_gains,
    norm_shifts,
    s_qkv,
    s_out,
    t_qkv,
    t_out,
    w_up,
    b_up,
    w_down,
    b_down,
    grad_out,
):
    shape = tokens.shape
    frames_local, _, slots, width = shape
    place = Place()
    total, core, tm_size = place.total, place.core, place.tm_size
    slots_local = slots // tm_size
    row_count = frames_local * slots
    half = width // 2

    def to_slots(value):
        view = value.reshape(frames_local, tm_size, slots_local, value.shape[-1])
        parts = []
        for o in range(tm_size):
            part = lax.dynamic_index_in_dim(view, place.tm ^ o, 1, keepdims=False)
            parts.append(place.tm_flip(part, o) if o else part)
        return parts

    def from_slots(value, offsets=range(tm_size)):
        view = value.reshape(tm_size, frames_local, slots_local, value.shape[-1])
        return [place.tm_flip(view[o], o) if o else view[o] for o in offsets]

    def in_slots(parts):
        return jnp.concatenate(parts, axis=0)

    def in_frames(parts):
        return jnp.stack(unscramble(parts, place.tm), axis=1).reshape(frames_local, slots, -1)

    def own_and_other(value, axis):
        first, second = (lax.index_in_dim(value, i, axis, keepdims=False) for i in (0, 1))
        return jnp.where(core == 0, first, second), jnp.where(core == 0, second, first)

    def in_order(own, other, axis):
        pair = [jnp.where(core == 0, own, other), jnp.where(core == 0, other, own)]
        return jnp.stack(pair, axis=axis)

    def woven(own, other):
        cuts = [slice(i, i + half) for i in range(0, own.shape[1], half)]
        own_first = [x[:, cut] for cut in cuts for x in (own, other)]
        other_first = [x[:, cut] for cut in cuts for x in (other, own)]
        return jnp.where(
            core == 0,
            jnp.concatenate(own_first, axis=1),
            jnp.concatenate(other_first, axis=1),
        )

    thin = width // total
    counts = [ACTIONS, 3, 3, 1]
    ends = [sum(counts[:i]) for i in range(len(counts) + 1)]
    rows = s_qkv.shape[0]
    hidden_half = w_down.shape[0] // 2

    def attention_group(qkv, out):
        qkv = own_and_other(qkv.reshape(rows, 3, 2, half), 2)
        both = [
            jnp.concatenate([a.reshape(rows, 3 * half), b], axis=1)
            for a, b in zip(qkv, own_and_other(out.reshape(rows, 2, half), 1))
        ]
        return Chain(gather(place, *both))

    front = attention_group(s_qkv, s_out)
    tokens = along(tokens, front)
    rows_in = (action_table, norm_gains, norm_shifts, b_down)
    tokens, rows_in, b_up, grad_out = lax.optimization_barrier((tokens, rows_in, b_up, grad_out))
    action_table, norm_gains, norm_shifts, b_down = rows_in
    small = jnp.concatenate([action_table, norm_gains, norm_shifts, b_down[None]], axis=0).T
    small = jnp.pad(small, ((0, 0), (0, LANES - ends[-1])))
    b_up = jnp.pad(b_up[None], ((0, GROUP - 1), (0, LANES - b_up.shape[0])))
    small = jnp.concatenate([small, b_up], axis=0)
    tokens = along(tokens, front)
    tokens, grad_out = lax.optimization_barrier((tokens, grad_out))
    cotangent = to_slots(grad_out.reshape(frames_local, slots, width))
    small = Chain(gather_small(place, small))
    tokens = along(tokens, small)
    tokens = along(tokens, small)
    tokens, t_qkv, t_out = lax.optimization_barrier((tokens, t_qkv, t_out))
    tokens = along(tokens, front)
    middle = attention_group(t_qkv, t_out)
    tokens = along(tokens, middle)
    tokens, w_up = lax.optimization_barrier((tokens, w_up))
    up_pair = own_and_other(w_up.reshape(rows, total, 2, hidden_half), 2)
    rising = Chain(gather(place, *[x.reshape(rows, -1) for x in up_pair], len(place.xy) // 2))
    tokens, cotangent = lax.optimization_barrier((tokens, cotangent))
    tokens = along(tokens, front, middle, rising)
    tokens = along(tokens, small)
    tokens = along(tokens, small)
    tokens, w_down = lax.optimization_barrier((tokens, w_down))
    falling = Chain(gather(place, *own_and_other(w_down.reshape(2, hidden_half, width), 0)))
    tokens = along(tokens, front, middle, rising, falling)
    while not small.done():
        tokens = along(tokens, small)
    small = small.result.astype(f32)
    table = small[:, :thin].reshape(width, LANES).T

    def unpack(i):
        return table[ends[i] : ends[i + 1]]

    action_rows, gains, shifts, down_bias = [unpack(i) for i in range(4)]
    up_bias = small[:, thin, : 2 * hidden_half].reshape(total, 2, hidden_half)
    up_bias = [x.reshape(1, -1) for x in own_and_other(up_bias, 1)]

    onehot = (actions == jnp.arange(ACTIONS)[None, :]).astype(f32)
    embedded = jnp.dot(onehot, action_rows, precision=highest)
    tokens = tokens.reshape(frames_local, slots, width)
    embedded = embedded[:, None, :]
    normed1 = norm(tokens, embedded, gains[0], shifts[0])
    normed1 = land(normed1, front, middle, rising, falling)
    normed1 = launch(normed1, front, middle, falling)
    s_halves = [x.reshape(width, -1) for x in finish(front)]
    here = core.astype(jnp.int32).reshape(1)

    def projected(x, w, outer):
        return project(x, w, 3 * half, here).reshape(*outer, -1)

    spatial = [projected(normed1, w, (frames_local, slots)) for w in s_halves]
    spatial = land(spatial, middle, falling)
    spatial = launch(spatial, middle, rising)

    def frame_index(i):
        return (i, 0, 0)

    def slot_index(i):
        return (0, i, 0)

    spatial_place = (
        jnp.stack([sides[0], core.astype(jnp.int32)]), (1, slots), frames_local, frame_index,
    )
    (s_mixed,) = run_attention(
        partial(attention_forward, spatial_bias), *spatial_place, spatial, [width]
    )
    s_mixed = s_mixed.reshape(row_count, width)
    flat = tokens.reshape(row_count, width)
    hidden1 = add_spatial(s_mixed, s_halves, flat, embedded, here)

    hidden1 = hold(hidden1, middle, rising)
    parts = to_slots(hidden1.reshape(tokens.shape))
    parts[1] = along(parts[1], middle, rising)
    parts = land(parts, middle, rising)
    hidden1 = in_slots(parts)
    frames = hidden1.shape[0]
    slot_at = place.tm * slots_local + jnp.arange(slots_local)
    mask = (slot_at < sides[0] * sides[0])[None, :, None]
    nothing = jnp.zeros((1, 1, width), f32)
    normed2 = norm(hidden1, nothing, gains[1], shifts[1])
    hidden1 = hidden1.reshape(row_count, width)
    normed2 = launch(normed2, rising, falling)
    t_halves = [x.reshape(width, -1) for x in finish(middle)]
    temporal = [projected(normed2, w, (frames, slots_local)) for w in t_halves]
    temporal_place = (
        jnp.stack([place.tm.astype(jnp.int32), core.astype(jnp.int32)]), (frames, GROUP),
        slots_local // GROUP, slot_index,
    )
    make_bias = partial(temporal_bias, frames_local)
    (t_mixed,) = run_attention(
        partial(attention_forward, make_bias), *temporal_place, temporal, [width]
    )
    t_mixed = t_mixed.reshape(row_count, width)
    hidden2, normed3 = add_temporal(t_mixed, t_halves, hidden1, gains[2], shifts[2], here)
    normed3 = along(normed3, rising, falling)
    up_halves = [x.reshape(width, -1) for x in finish(rising)]
    first = up_project(normed3, up_halves[0], up_bias[0])
    first = along(first, falling)
    normed3, first = lax.optimization_barrier((normed3, first))
    second = up_project(normed3, up_halves[1], up_bias[1])
    (active, slope), (active2, slope2) = first, second

    core_pair = (place.core_bit, place.core_bit)

    def exchanged(grad):
        return place.flip(grad, core_pair)

    def sums(*parts):
        return Chain(scatter(place, lambda k, value: weight_split(parts, k, value, core)))

    down_in = jnp.where(mask, in_slots(cotangent), 0).reshape(row_count, width)
    send = weight_grad(active2, down_in, total, here)
    down_in, send = land((down_in, send), falling)
    own_rows = falling.pending[0].reshape(-1, width)
    down_in, send = launch(down_in, falling, also=[send])
    got = exchanged(send)
    inner_grad, b_sum = inner_back(down_in, own_rows, slope, here)
    hidden2, inner_grad = land((hidden2, inner_grad), falling)
    down_halves = [x.reshape(-1, width) for x in finish(falling)]
    inner_grad2, b_sum2 = inner_back(down_in, down_halves[1], slope2, here)
    send = weight_grad(normed3, inner_grad2, total, here)
    down_in, hidden2, send, got = lax.optimization_barrier((down_in, hidden2, send, got))
    got_up = exchanged(send)
    s_down = sums((active, down_in, got, None))
    down_in, hidden2 = launch((down_in, hidden2), s_down)

    mask_rows = jnp.broadcast_to(mask, (frames, slots_local, 1)).reshape(row_count, 1).astype(f32)
    mixed = down_project([active, active2], down_halves, hidden2, down_bias, mask_rows, here)
    mixed, got_up = lax.optimization_barrier((mixed, got_up))
    s_up = sums((normed3, inner_grad, got_up, None))
    hidden2, s_up.pending, mixed = land((hidden2, s_up.pending, mixed), s_down)
    hidden2 = launch(hidden2, s_down, s_up)

    grad2, sums3 = norm_back(
        (inner_grad, inner_grad2), up_halves, hidden2, nothing, gains[2], down_in, bf16, here
    )
    b_sums = [x.reshape(total, -1, thin).swapaxes(0, 1) for x in (b_sum, b_sum2)]
    late_rows = [x.reshape(-1, width) for x in b_sums]
    late_rows = jnp.where(
        core == 0, jnp.concatenate(late_rows, axis=0), jnp.concatenate(late_rows[::-1], axis=0)
    )
    late_rows = jnp.concatenate([jnp.sum(down_in.astype(f32), axis=0)[None], late_rows], axis=0)
    t_mix_grad = mixed_back(grad2, t_halves, here).reshape(frames, slots_local, width)
    send2 = weight_grad(t_mixed, grad2, total, here, 1)

    def back(side, where, make, values, grad):
        (out,) = run_attention(
            partial(attention_backward, make, (side,)), *where, [values[side], grad], [3 * half]
        )
        return out.reshape(row_count, -1)

    t_grad2 = back(1, temporal_place, make_bias, temporal, t_mix_grad)
    t_mix_grad, t_grad2, late_rows = land((t_mix_grad, t_grad2, late_rows), s_down, s_up)
    t_mix_grad, t_grad2 = launch((t_mix_grad, t_grad2), s_down, s_up)
    t_grad = back(0, temporal_place, make_bias, temporal, t_mix_grad)
    send = weight_grad(normed2, t_grad2, total, here)
    t_grads, send = land(((t_grad, t_grad2), send), s_down, s_up)
    t_grads, send, send2 = launch(t_grads, s_down, also=[send, send2])
    gots = [exchanged(send), exchanged(send2)]

    grad1, sums2 = norm_back(t_grads, t_halves, hidden1, nothing, gains[1], grad2, bf16, here)
    grad1 = hold(grad1, s_down)
    grad1, gots = lax.optimization_barrier((grad1, gots))
    parts = from_slots(grad1)
    parts[1] = along(parts[1], s_down, s_up)
    s_time = sums((normed2, t_grads[0], gots[0], None), (t_mixed, grad2, gots[1], 0))
    parts[0], s_time.pending = lax.optimization_barrier((parts[0], s_time.pending))
    parts = land(parts, s_down, s_up)
    grad1 = in_frames(parts).reshape(row_count, width)
    grad1 = launch(grad1, s_down, s_up, s_time)

    send2 = weight_grad(s_mixed, grad1, total, here, 1)
    mix_grad = mixed_back(grad1, s_halves, here).reshape(frames_local, slots, width)
    s_grad2 = back(1, spatial_place, spatial_bias, spatial, mix_grad)
    send = weight_grad(normed1, s_grad2, total, here)
    mix_grad, send, send2 = land((mix_grad, send, send2), s_down, s_up, s_time)
    mix_grad, send, send2 = launch(mix_grad, s_down, s_up, s_time, also=[send, send2])
    gots = [exchanged(send), exchanged(send2)]

    s_grad = back(0, spatial_place, spatial_bias, spatial, mix_grad)
    s_grad, *gots = land(s_grad, s_down, s_up, s_time, also=gots)
    s_space = sums((normed1, s_grad, gots[0], None), (s_mixed, grad1, gots[1], 0))
    s_grads = launch((s_grad, s_grad2), s_time, s_space)

    input_grad, sums1 = norm_back(
        s_grads, s_halves, flat, embedded, gains[0], grad1, f32, here
    )
    sums1, input_grad = land((sums1, input_grad), s_time, s_space)
    sums1, input_grad = launch((sums1, input_grad), s_time, s_space)
    g_actions = jnp.sum(onehot[:, :, None] * sums1[:, 2][:, None, :], axis=0)
    all_sums = [jnp.sum(x[:, :2], axis=0) for x in (sums1, sums2, sums3)]
    both_norms = [jnp.stack([x[i] for x in all_sums]) for i in (0, 1)]
    packed = jnp.concatenate([g_actions, *both_norms, late_rows], axis=0)
    s_small = Chain(scatter_small(place, packed))
    packed = launch(packed, s_small)
    packed = land(packed, s_time, s_space, s_small)
    packed, mixed = launch((packed, mixed), s_time, s_space, s_small)
    near = from_slots(mixed, range(tm_size // 2 + 1))
    packed, down_sums, up_sums = lax.optimization_barrier((packed, finish(s_down), finish(s_up)))
    g_w_down = in_order(*down_sums, 0).reshape(w_down.shape)
    g_w_up = in_order(*[x.reshape(rows, total, -1) for x in up_sums], 2).reshape(w_up.shape)
    packed = along(packed, s_small)
    packed, *near = land(packed, s_time, s_space, s_small, also=near)
    packed, mixed = launch((packed, mixed), s_time, s_space, s_small)
    packed, g_w_down, g_w_up = lax.optimization_barrier((packed, g_w_down, g_w_up))
    far = from_slots(mixed, range(tm_size // 2 + 1, tm_size))
    packed = along(packed, s_small)
    packed, *far = land(packed, s_time, s_space, s_small, also=far)
    packed = launch(packed, s_time, s_space, s_small)
    mixed = in_frames(near + far)
    packed, mixed = lax.optimization_barrier((packed, mixed))
    while not (s_time.done() and s_space.done() and s_small.done()):
        packed = along(packed, s_time, s_space, s_small)
    summed = s_small.result
    (g_t_qkv, g_t_out), (g_s_qkv, g_s_out) = [
        [woven(*[x[:, cut] for x in c.result]) for cut in (slice(3 * half), slice(3 * half, None))]
        for c in (s_time, s_space)
    ]

    return (
        mixed.reshape(shape),
        input_grad.reshape(shape),
        summed[:8],
        summed[8:11],
        summed[11:14],
        g_s_qkv,
        g_s_out,
        g_t_qkv,
        g_t_out,
        g_w_up,
        summed[15:].reshape(-1),
        g_w_down,
        summed[14],
    )


def solution(mesh):
    whole = P(("tm", "clip"), None)
    spread = P(None, ("tm", "clip"))
    frames = P("tm", "clip", None, None)
    vector = P(("tm", "clip"))
    return jax.shard_map(
        on_device,
        mesh=mesh,
        in_specs=(
            frames, P("tm", "clip"), P("clip"), spread, spread, spread, whole, whole, whole,
            whole, whole, vector, whole, vector, frames,
        ),
        out_specs=(
            frames, frames, spread, spread, spread, whole, whole, whole, whole, whole, vector,
            whole, vector,
        ),
        check_vma=False,
    )
```

```python
import math
from functools import partial

import jax
import jax.numpy as jnp
from jax import lax
from jax.experimental import pallas as pl
from jax.experimental.pallas import tpu as pltpu
from jax.sharding import PartitionSpec as P

H = 16
E = 64
ACTIONS = 8
FRAMES = 16
AXES = ("tm", "clip")
LANES = 128
GROUP = 16

negative = -1e30
highest = lax.Precision.HIGHEST
MIB = 1024 * 1024
bf16, f32 = jnp.bfloat16, jnp.float32
NO_COST = pl.CostEstimate(flops=0, bytes_accessed=0, transcendentals=0)


def params(blocks, margin=6):
    size = sum(math.prod(shape) * jnp.dtype(dtype).itemsize * n for shape, dtype, n in blocks)
    return pltpu.CompilerParams(vmem_limit_bytes=(-(-size // MIB) + margin) * MIB)


class Place:
    def __init__(self):
        tm_size, clip_size = lax.axis_size("tm"), lax.axis_size("clip")
        self.tm_size, self.clip_size, self.total = tm_size, clip_size, tm_size * clip_size
        self.tm = lax.axis_index("tm")
        self.me = self.tm * clip_size + lax.axis_index("clip")
        self.core_bit = clip_size
        self.core = self.bit_of(clip_size)
        clip_bits = [1 << i for i in range(clip_size.bit_length() - 1)]
        tm_bits = [clip_size << i for i in range(tm_size.bit_length() - 1)]
        x, z, y = clip_bits[:-2], clip_bits[-2:], tm_bits[1:]
        self.z = [(b, b) for b in z]
        self.xy = list(zip(x + y, y + x))

    def bit_of(self, bit):
        return (self.me // bit) % 2

    def mine(self, pair):
        return jnp.where(self.core == 0, self.bit_of(pair[0]), self.bit_of(pair[1]))

    def choose(self, pair):
        return jnp.where(self.core == 0, pair[0], pair[1])

    def flip(self, value, pair):
        moves = [(i, i ^ pair[(i // self.core_bit) % 2]) for i in range(self.total)]
        return lax.ppermute(value, AXES, moves)

    def tm_flip(self, value, offset):
        moves = [(i, i ^ (offset * self.clip_size)) for i in range(self.total)]
        return lax.ppermute(value, AXES, moves)


def below(have, bit):
    return sum(1 for b in have if b < bit)


def unscramble(parts, me):
    bit = 1
    while bit < len(parts):
        swap = (me & bit) != 0
        parts = [jnp.where(swap, parts[p ^ bit], parts[p]) for p in range(len(parts))]
        bit *= 2
    return parts


def position(m, value, k):
    m = jnp.int32(m)
    high = lax.shift_left(lax.shift_right_logical(m, k), k + 1)
    return high | lax.shift_left(value, k) | (m & (lax.shift_left(jnp.int32(1), k) - 1))


def merge_body(info_ref, mine_ref, other_ref, out_ref):
    k, value = info_ref[0], info_ref[1]
    for m in range(mine_ref.shape[0]):
        out_ref[position(m, value, k)] = mine_ref[m]
        out_ref[position(m, 1 - value, k)] = other_ref[m]


def column_block(shape):
    blocks, rows, cols = shape
    return cols if blocks * rows * cols <= 512 * 1024 else min(cols, 512)


def merge(mine, other, k, value):
    m, r, n = mine.shape
    block = column_block((2 * m, r, n))
    spec = pl.BlockSpec((m, r, block), lambda j: (0, 0, j))
    return pl.pallas_call(
        merge_body,
        grid=(n // block,),
        in_specs=[pl.BlockSpec(memory_space=pltpu.SMEM), spec, spec],
        out_specs=pl.BlockSpec((2 * m, r, block), lambda j: (0, 0, j)),
        out_shape=jax.ShapeDtypeStruct((2 * m, r, n), mine.dtype),
        compiler_params=params([((4 * m, r, block), mine.dtype, 2)], 2),
        cost_estimate=NO_COST,
    )(jnp.stack([jnp.int32(k), value.astype(jnp.int32)]), mine, other)


def part(info_ref, source_ref, send_ref, keep_ref):
    k, value = info_ref[0], info_ref[1]
    for m in range(send_ref.shape[0]):
        for out_ref, at in ((send_ref, 1 - value), (keep_ref, value)):
            out_ref[m] = source_ref[position(m, at, k)].astype(out_ref.dtype)


def split_body(info_ref, a_ref, b_ref, send_ref, keep_ref):
    k, value = info_ref[0], info_ref[1]
    for m in range(send_ref.shape[0]):
        for out_ref, at in ((send_ref, 1 - value), (keep_ref, value)):
            i = position(m, at, k)
            out_ref[m] = (a_ref[i].astype(f32) + b_ref[i].astype(f32)).astype(out_ref.dtype)


def split(a, b, k, value, dtype):
    blocks, r, n = a.shape
    block = column_block(a.shape)
    out = jax.ShapeDtypeStruct((blocks // 2, r, n), dtype)
    return pl.pallas_call(
        split_body,
        grid=(n // block,),
        in_specs=[pl.BlockSpec(memory_space=pltpu.SMEM)]
        + [pl.BlockSpec((blocks, r, block), lambda j: (0, 0, j))] * 2,
        out_specs=[pl.BlockSpec((blocks // 2, r, block), lambda j: (0, 0, j))] * 2,
        out_shape=[out, out],
        compiler_params=params([((3 * blocks, r, block), dtype, 2)], 3),
        cost_estimate=NO_COST,
    )(jnp.stack([jnp.int32(k), value.astype(jnp.int32)]), a, b)


def gather_small(place, value):
    core = (place.core_bit, place.core_bit)
    x_and_y = [(b, b) for b, _ in place.xy]
    count = len(x_and_y) // 2
    blocks, have = value[None], []
    for pair in x_and_y[:count] + [core] + x_and_y[count:] + place.z:
        (send,) = yield [blocks]
        (got,) = yield [place.flip(send, pair)]
        blocks = merge(blocks, got, below(have, pair[0]), place.bit_of(pair[0]))
        have.append(pair[0])
    return blocks


def scatter_small(place, value):
    bit = place.total // 2
    while bit:
        half = value.shape[1] // 2
        low_half, high_half = value[:, :half], value[:, half:]
        mine = (place.me & bit) != 0
        (send,) = yield [jnp.where(mine, low_half, high_half)]
        (got,) = yield [place.flip(send, (bit, bit))]
        value = jnp.where(mine, high_half, low_half) + got
        bit //= 2
    return value


def gather(place, keep, send, ahead=0):
    core = (place.core_bit, place.core_bit)
    have = ([], [])
    blocks, out = keep[None], send[None]
    for pair in [core] + place.xy[:ahead] + place.z[::-1] + place.xy[ahead:]:
        (out,) = yield [out]
        (got,) = yield [place.flip(out, pair)]
        k = [below(h, b) for h, b in zip(have, pair)]
        blocks = out = merge(blocks, got, place.choose(k), place.mine(pair))
        have = (have[0] + [pair[0]], have[1] + [pair[1]])
    (out,) = yield [out]
    (got,) = yield [place.flip(out, core)]
    return blocks, got


def scatter(place, first):
    core = (place.core_bit, place.core_bit)
    bits = [1 << i for i in range(place.total.bit_length() - 1)]
    have, pairs = (bits, bits), None
    for pair in place.xy[::-1] + place.z + [core]:
        have = tuple([b for b in h if b != bit] for h, bit in zip(have, pair))
        k = place.choose([below(h, b) for h, b in zip(have, pair)])
        dtype = f32 if pair == core else bf16
        if pairs is None:
            send, keep = first(k, place.mine(pair))
        else:
            send, keep = split(*pairs, k, place.mine(pair), dtype)
        (send,) = yield [send]
        (got,) = yield [place.flip(send, pair)]
        pairs = (keep, got)
    return keep[0], got[0]


class Chain:
    def __init__(self, steps):
        self.steps, self.flying, self.result, self.started = steps, False, None, 0
        self.pending = next(steps)

    def done(self):
        return self.result is not None

    def move(self):
        try:
            self.pending = self.steps.send(self.pending)
        except StopIteration as stop:
            self.result = stop.value
        self.flying = not self.flying
        self.started += self.flying


def hold(value, *chains):
    chains = [c for c in chains if c.flying]
    value, got = lax.optimization_barrier((value, [c.pending for c in chains]))
    for c, g in zip(chains, got):
        c.pending = g
    return value


def land(value, *chains, also=()):
    chains = [c for c in chains if c.flying]
    value, got, also = lax.optimization_barrier((value, [c.pending for c in chains], list(also)))
    for c, g in zip(chains, got):
        c.pending = g
        c.move()
    return (value, *also) if also else value


def launch(value, *chains, also=()):
    chains = [c for c in chains if not c.done() and not c.flying]
    value, sent, also = lax.optimization_barrier((value, [c.pending for c in chains], list(also)))
    for c, g in zip(chains, sent):
        c.pending = g
        c.move()
    return (value, *also) if also else value


def along(value, *chains):
    return launch(land(value, *chains), *chains)


def up_to(chain, count):
    while chain.started < count or chain.flying:
        chain.move()
    return chain.pending


def finish(chain):
    while not chain.done():
        chain.move()
    return chain.result


def spatial_bias(scalar, rows, keys):
    key = lax.broadcasted_iota(jnp.int32, (1, rows) if keys == 1 else (rows, 1), keys)
    return jnp.where(key < scalar * scalar, 0.0, negative)


def temporal_bias(frames_local, scalar, rows, keys):
    def place(axis):
        index = lax.broadcasted_iota(jnp.int32, (rows, rows), axis)
        slot, at = index % GROUP, index // GROUP
        frame = ((at // frames_local) ^ scalar) * frames_local + at % frames_local
        return slot, frame

    slot_q, frame_q = place(1 - keys)
    slot_k, frame_k = place(keys)
    return jnp.where((slot_q == slot_k) & (frame_q >= frame_k), 0.0, negative)


def dot_t(a, b):
    return lax.dot_general(a, b, (((1,), (1,)), ((), ())), preferred_element_type=f32)


def t_dot(a, b):
    return lax.dot_general(a, b, (((0,), (0,)), ((), ())), preferred_element_type=f32)


def columns(scalar_ref, side, start):
    half = H * E // 2
    return pl.ds(pl.multiple_of((scalar_ref[1] ^ side) * half + start, LANES), LANES)


def two_heads(rows):
    half = lax.broadcasted_iota(jnp.int32, (rows, LANES), 1) < E

    def apart(x):
        return jnp.concatenate([jnp.where(half, x, 0), jnp.where(half, 0, x)], axis=0)

    def together(x):
        return jnp.where(half, x[:rows], x[rows:])

    return apart, together


def head_pairs(sides, refs):
    a, b, width = refs[0].shape
    rows, width = a * b, width // 3
    for i, side in enumerate(sides):
        for c in range(0, width, LANES):
            q, k, v = (
                refs[i][:, :, at : at + LANES].reshape(rows, LANES)
                for at in (c, width + c, 2 * width + c)
            )
            yield i, side, c, q * bf16(E ** (-0.5)), k, v


def in_turn(items, first, last):
    waiting = None
    for item in items:
        ready = first(*item)
        if waiting is not None:
            last(*waiting)
        waiting = ready
    last(*waiting)


def attention_forward(make_bias, scalar_ref, own_ref, other_ref, out_ref):
    a, b, width = own_ref.shape
    rows, width = a * b, width // 3
    bias = make_bias(scalar_ref[0], rows, 1)
    apart, together = two_heads(rows)

    def first(i, side, c, q, k, v):
        scores = dot_t(apart(q), k).reshape(2, rows, rows) + bias[None]
        weights = jnp.exp(scores - jnp.max(scores, axis=2, keepdims=True))
        scale = 1.0 / jnp.sum(weights, axis=2, keepdims=True)
        return side, c, v, weights.astype(bf16).reshape(2 * rows, rows), scale

    def last(side, c, v, weights, scale):
        mixed = jnp.dot(weights, v, preferred_element_type=f32) * scale.reshape(2 * rows, 1)
        mixed = together(mixed).astype(out_ref.dtype)
        out_ref[:, :, columns(scalar_ref, side, c)] = mixed.reshape(a, b, LANES)

    in_turn(head_pairs((0, 1), (own_ref, other_ref)), first, last)


def attention_backward(make_bias, sides, scalar_ref, *refs):
    grad_ref = refs[len(sides)]
    a, b, width = refs[0].shape
    rows, width = a * b, width // 3
    bias = make_bias(scalar_ref[0], rows, 0)
    apart, together = two_heads(rows)

    def first(i, side, c, q, k, v):
        g = grad_ref[:, :, columns(scalar_ref, side, c)].reshape(rows, LANES)
        scores = dot_t(apart(k), q).reshape(2, rows, rows) + bias[None]
        prob_grad = dot_t(apart(v), g).reshape(2, rows, rows)
        weights = jnp.exp(scores - jnp.max(scores, axis=1, keepdims=True))
        probs = weights * (1.0 / jnp.sum(weights, axis=1, keepdims=True))
        delta = jnp.sum(probs * prob_grad, axis=1, keepdims=True)
        return i, c, q, k, g, probs.astype(bf16), (probs * (prob_grad - delta)).astype(bf16)

    def last(i, c, q, k, g, probs, score_grad):
        turned = jnp.concatenate([score_grad[0].T, score_grad[1].T], axis=0)
        dq = jnp.dot(turned, k, preferred_element_type=f32) * E ** (-0.5)
        dk = jnp.dot(score_grad.reshape(2 * rows, rows), q, preferred_element_type=f32)
        dv = jnp.dot(probs.reshape(2 * rows, rows), g, preferred_element_type=f32)
        for index, grad in enumerate((dq, dk, dv)):
            start = index * width + c
            merged = together(grad).astype(bf16).reshape(a, b, LANES)
            refs[len(sides) + 1 + i][:, :, start : start + LANES] = merged

    in_turn(head_pairs(sides, refs), first, last)


def run_attention(body, scalars, block, grid, index, inputs, out_widths):
    a, b = block
    outer = inputs[0].shape[:2]
    return pl.pallas_call(
        body,
        grid=(grid,),
        in_specs=[pl.BlockSpec(memory_space=pltpu.SMEM)]
        + [pl.BlockSpec((a, b, x.shape[-1]), index) for x in inputs],
        out_specs=[pl.BlockSpec((a, b, width), index) for width in out_widths],
        out_shape=[jax.ShapeDtypeStruct((*outer, width), bf16) for width in out_widths],
        compiler_params=params(
            [((a, b, width), bf16, 2) for width in (*(x.shape[-1] for x in inputs), *out_widths)], 8
        ),
        cost_estimate=NO_COST,
    )(scalars, *inputs)


def centre(x):
    average = jnp.mean(x, axis=-1, keepdims=True)
    centered = x - average
    variance = jnp.mean(centered * centered, axis=-1, keepdims=True)
    scale = lax.rsqrt(variance + 1e-05)
    return centered * scale, scale


def norm_body(x_ref, added_ref, gain_ref, shift_ref, out_ref):
    unit, _ = centre(x_ref[0].astype(f32) + added_ref[0])
    out_ref[0] = (unit * gain_ref[...] + shift_ref[...]).astype(out_ref.dtype)


def by_rows(body, arrays, rows, outs):
    blocks = arrays[0].shape[0]
    specs = []
    for x in arrays:
        if x.ndim == 2:
            specs.append(pl.BlockSpec(x.shape, lambda i: (0, 0)))
        else:
            at = (lambda i: (i, 0, 0)) if x.shape[0] == blocks else (lambda i: (0, 0, 0))
            specs.append(pl.BlockSpec((1, *x.shape[1:]), at))
    return pl.pallas_call(
        body,
        grid=(blocks,),
        in_specs=specs,
        out_specs=[pl.BlockSpec((1, *shape[1:]), lambda i: (i, 0, 0)) for shape, _ in outs],
        out_shape=[jax.ShapeDtypeStruct(shape, dtype) for shape, dtype in outs],
        compiler_params=params([(x.shape[1:], f32, 4) for x in arrays]),
        cost_estimate=NO_COST,
    )(*arrays)


def norm(x, added, gain, shift):
    shape = (x.shape[0] * x.shape[1] // 256, 256, x.shape[2])
    arrays = [x.reshape(shape), added, gain[None], shift[None]]
    (out,) = by_rows(norm_body, arrays, 256, [(shape, bf16)])
    return out.reshape(-1, shape[2])


BLOCK = 512


def dense(body, grid, scalars, inputs, outs, scratch=(), margin=6):
    used = [(block, x.dtype, 1 if index is FIXED else 2) for x, block, index in inputs]
    used += [(block, dtype, 2) for _, dtype, block, _ in outs]
    used += [(x.shape, x.dtype, 1) for x in scratch]

    def spec(block, index):
        if index is FIXED:
            zeros = (0,) * len(block)
            return pl.BlockSpec(block, lambda *_: zeros, pipeline_mode=pl.Buffered(1))
        return pl.BlockSpec(block, index)

    return pl.pallas_call(
        body,
        grid_spec=pltpu.PrefetchScalarGridSpec(
            num_scalar_prefetch=1,
            grid=grid,
            in_specs=[spec(block, index) for _, block, index in inputs],
            out_specs=[pl.BlockSpec(block, index) for _, _, block, index in outs],
            scratch_shapes=list(scratch),
        ),
        out_shape=[jax.ShapeDtypeStruct(shape, dtype) for shape, dtype, _, _ in outs],
        compiler_params=params(used, margin),
        cost_estimate=NO_COST,
    )(scalars, *[x for x, _, _ in inputs])


FIXED = None


def at(*index):
    return lambda j, ref: index


def whole(x):
    return (x, x.shape, FIXED)


def rows_of(x, rows=256):
    return (x, (rows, x.shape[1]), lambda i, ref: (i, 0))


def project_body(_, x_ref, w_ref, out_ref):
    out_ref[...] = jnp.dot(x_ref[...], w_ref[...], preferred_element_type=f32).astype(bf16)


def project(x, w, cols, scalars):
    index = lambda j, ref: (0, j)
    rows = x.shape[0]
    (out,) = dense(
        project_body, (cols // BLOCK,), scalars,
        [whole(x), (w, (w.shape[0], BLOCK), index)],
        [((rows, cols), bf16, (rows, BLOCK), index)],
    )
    return out


def sides(core, own_ref, other_ref):
    for side, ref in ((core, own_ref), (1 - core, other_ref)):
        yield pl.ds(pl.multiple_of(side * BLOCK, BLOCK), BLOCK), ref


def hidden1_body(core_ref, mixed_ref, own_ref, other_ref, x_ref, added_ref, out_ref):
    for cols, w_ref in sides(core_ref[0], own_ref, other_ref):
        dot = jnp.dot(mixed_ref[...], w_ref[...], preferred_element_type=f32)
        out_ref[:, cols] = (x_ref[:, cols].astype(f32) + added_ref[0, :, cols] + dot).astype(bf16)


def out_half(w):
    return (w, (w.shape[0], BLOCK), at(0, w.shape[1] // BLOCK - 1))


def add_spatial(mixed, halves, x, added, scalars):
    rows, width = x.shape
    step = rows // added.shape[0]
    (out,) = dense(
        hidden1_body, (rows // step,), scalars,
        [rows_of(mixed, step), *[out_half(w) for w in halves], rows_of(x, step),
         (added, (1, 1, width), lambda i, ref: (i, 0, 0))],
        [((rows, width), bf16, (step, width), lambda i, ref: (i, 0))],
    )
    return out


def hidden2_body(
    core_ref, mixed_ref, own_ref, other_ref, x_ref, gain_ref, shift_ref, out_ref, norm_ref
):
    for cols, w_ref in sides(core_ref[0], own_ref, other_ref):
        dot = jnp.dot(mixed_ref[...], w_ref[...], preferred_element_type=f32)
        out_ref[:, cols] = x_ref[:, cols].astype(f32) + dot
    unit, _ = centre(out_ref[...])
    norm_ref[...] = (unit * gain_ref[...] + shift_ref[...]).astype(bf16)


def add_temporal(mixed, halves, x, gain, shift, scalars):
    rows, width = x.shape
    block = ((256, width), lambda i, ref: (i, 0))
    return dense(
        hidden2_body, (rows // 256,), scalars,
        [rows_of(mixed), *[out_half(w) for w in halves], rows_of(x), whole(gain[None]),
         whole(shift[None])],
        [((rows, width), f32, *block), ((rows, width), bf16, *block)],
    )


def hidden3_body(_, a_ref, b_ref, own_ref, other_ref, x_ref, bias_ref, mask_ref, out_ref):
    out = x_ref[...] + bias_ref[...]
    out += jnp.dot(a_ref[...], own_ref[...], preferred_element_type=f32)
    out += jnp.dot(b_ref[...], other_ref[...], preferred_element_type=f32)
    out_ref[...] = jnp.where(mask_ref[...] > 0, out, 0).astype(bf16)


def down_project(actives, halves, x, bias, mask, scalars):
    rows, width = x.shape
    (out,) = dense(
        hidden3_body, (rows // 256,), scalars,
        [*[rows_of(y) for y in actives], *[whole(w) for w in halves], rows_of(x), whole(bias),
         rows_of(mask)],
        [((rows, width), bf16, (256, width), lambda i, ref: (i, 0))], margin=30,
    )
    return out


def inner_back_body(_, x_ref, w_ref, slope_ref, out_ref, sum_ref):
    grad = dot_t(x_ref[...], w_ref[...]) * slope_ref[...].astype(f32)
    out_ref[...] = grad.astype(bf16)
    sum_ref[...] = jnp.sum(out_ref[...].astype(f32), axis=0, keepdims=True)


def inner_back(x, w, slope, scalars):
    rows, cols = slope.shape
    index = lambda j, ref: (0, j)
    return dense(
        inner_back_body, (cols // BLOCK,), scalars,
        [whole(x), (w, (BLOCK, w.shape[1]), lambda j, ref: (j, 0)), (slope, (rows, BLOCK), index)],
        [((rows, cols), bf16, (rows, BLOCK), index), ((1, cols), f32, (1, BLOCK), index)],
    )


def norm_back_body(
    _, a_ref, b_ref, own_ref, other_ref, x_ref, added_ref, gain_ref, rest_ref, out_ref, sums_ref
):
    grad = dot_t(a_ref[...], own_ref[...]) + dot_t(b_ref[...], other_ref[...])
    unit, scale = centre(x_ref[...].astype(f32) + added_ref[0])
    scaled = grad * gain_ref[...]
    first = jnp.mean(scaled, axis=-1, keepdims=True)
    second = jnp.mean(scaled * unit, axis=-1, keepdims=True)
    out = rest_ref[...].astype(f32) + scale * (scaled - first - unit * second)
    out_ref[...] = out.astype(out_ref.dtype)
    terms = (grad * unit, grad, out)
    sums_ref[0] = jnp.concatenate([jnp.sum(x, axis=0, keepdims=True) for x in terms], axis=0)


def norm_back(grads, halves, x, added, gain, rest, dtype, scalars):
    rows, width = x.shape
    step, cols = 256, grads[0].shape[1]
    added_at = (lambda i, ref: (i, 0, 0)) if added.shape[0] > 1 else at(0, 0, 0)
    return dense(
        norm_back_body, (rows // step,), scalars,
        [*[rows_of(g) for g in grads], *[(w, (w.shape[0], cols), FIXED) for w in halves],
         rows_of(x), (added, (1, 1, width), added_at), whole(gain[None]), rows_of(rest)],
        [((rows, width), dtype, (step, width), lambda i, ref: (i, 0)),
         ((rows // step, 3, width), f32, (1, 3, width), lambda i, ref: (i, 0, 0))],
        margin=30 if dtype == f32 or cols > 3 * BLOCK else 6,
    )


def mixed_back_body(core_ref, x_ref, own_ref, other_ref, out_ref):
    grad = 0
    for cols, w_ref in sides(core_ref[0], own_ref, other_ref):
        grad += dot_t(x_ref[:, cols], w_ref[...])
    out_ref[...] = grad.astype(bf16)


def mixed_back(x, halves, scalars):
    rows, width = x.shape
    last = halves[0].shape[1] // BLOCK - 1
    (out,) = dense(
        mixed_back_body, (width // BLOCK,), scalars,
        [whole(x), *[(w, (BLOCK, BLOCK), lambda j, ref: (j, last)) for w in halves]],
        [((rows, width), bf16, (rows, BLOCK), lambda j, ref: (0, j))],
    )
    return out


def weight_grad_body(_, x_ref, y_ref, out_ref):
    out_ref[...] = t_dot(x_ref[...], y_ref[...]).astype(bf16).reshape(out_ref.shape)


def weight_grad(x, y, total, scalars, half=None):
    rows, count = x.shape
    cols = y.shape[1] if half is None else BLOCK
    shift = (lambda j, ref: (0, j)) if half is None else (lambda j, ref: (0, ref[0] ^ half))
    shape = (total, count // total)
    (out,) = dense(
        weight_grad_body, (cols // BLOCK,), scalars,
        [whole(x), (y, (rows, BLOCK), shift)],
        [((*shape, cols), bf16, (*shape, BLOCK), lambda j, ref: (0, 0, j))],
    )
    return out


def weight_split_body(ends, info_ref, *refs):
    send_ref, keep_ref, sum_ref = refs[-3:]
    step = pl.program_id(0)
    for p in range(len(ends) - 1):

        @pl.when((step >= ends[p]) & (step < ends[p + 1]))
        def _(x_ref=refs[3 * p], y_ref=refs[3 * p + 1], got_ref=refs[3 * p + 2]):
            grad = t_dot(x_ref[...], y_ref[...]).reshape(sum_ref.shape)
            sum_ref[...] = grad + got_ref[...].astype(f32)

    part(info_ref, sum_ref, send_ref, keep_ref)


def weight_split(parts, k, value, core):
    scalars = jnp.stack([jnp.int32(k), value.astype(jnp.int32), core.astype(jnp.int32)])
    total, r, _ = parts[0][2].shape
    widths = [got.shape[2] for _, _, got, _ in parts]
    ends = [sum(widths[:i]) // BLOCK for i in range(len(parts) + 1)]
    inputs = []
    for (x, y, got, half), low, high in zip(parts, ends[:-1], ends[1:]):
        place = lambda j, low=low, high=high: jnp.clip(j - low, 0, high - low - 1)
        if half is None:
            index = lambda j, ref, place=place: (0, place(j))
        else:
            index = lambda j, ref, half=half: (0, ref[2] ^ half)
        inputs += [
            whole(x),
            (y, (y.shape[0], BLOCK), index),
            (got, (total, r, BLOCK), lambda j, ref, place=place: (0, 0, place(j))),
        ]
    shape = (total // 2, r)
    out = ((*shape, sum(widths)), bf16, (*shape, BLOCK), lambda j, ref: (0, 0, j))
    return dense(
        partial(weight_split_body, ends), (ends[-1],), scalars, inputs, [out, out],
        [pltpu.VMEM((total, r, BLOCK), f32)],
    )


TAIL = (
    0.14760860800743103, 0.14761532843112946, 0.127163827419281, 0.09018292278051376,
    0.013407237827777863, 0.06451446563005447, -0.19429759681224823, 0.13513216376304626,
    -0.031326886266469955,
)


def gelu(inner):
    size = 1.0 + 0.37 * jnp.abs(inner)
    t = pl.reciprocal(size, approx=True)
    t = t * (2.0 - size * t)
    bell = jnp.exp2(inner * inner * -0.7213475204444817)
    series = TAIL[-1]
    for term in reversed(TAIL[:-1]):
        series = series * t + term
    tail = series * t * bell
    cdf = jnp.where(inner > 0, 1.0 - tail, tail)
    return inner * cdf, cdf + inner * bell * 0.3989422804014327


def up_body(x_ref, w_ref, bias_ref, active_ref, slope_ref):
    rows = x_ref.shape[0]
    step = min(rows, 128)
    for r in range(0, rows, step):
        inner = jnp.dot(x_ref[r : r + step], w_ref[...], preferred_element_type=f32)
        active, slope = gelu(inner + bias_ref[...])
        active_ref[r : r + step] = active.astype(active_ref.dtype)
        slope_ref[r : r + step] = slope.astype(slope_ref.dtype)


def up_project(x, weight, bias):
    rows, width = x.shape
    cols, block = weight.shape[1], 512
    out = jax.ShapeDtypeStruct((rows, cols), bf16)
    return pl.pallas_call(
        up_body,
        grid=(cols // block,),
        in_specs=[
            pl.BlockSpec((rows, width), lambda i: (0, 0)),
            pl.BlockSpec((width, block), lambda i: (0, i)),
            pl.BlockSpec((1, block), lambda i: (0, i)),
        ],
        out_specs=[pl.BlockSpec((rows, block), lambda i: (0, i))] * 2,
        out_shape=[out, out],
        compiler_params=params(
            [(x.shape, bf16, 2), ((width, block), bf16, 2), ((rows, block), bf16, 4)]
        ),
        cost_estimate=NO_COST,
    )(x, weight, bias)


def on_device(
    tokens,
    actions,
    sides,
    action_table,
    norm_gains,
    norm_shifts,
    s_qkv,
    s_out,
    t_qkv,
    t_out,
    w_up,
    b_up,
    w_down,
    b_down,
    grad_out,
):
    shape = tokens.shape
    frames_local, _, slots, width = shape
    place = Place()
    total, core, tm_size = place.total, place.core, place.tm_size
    slots_local = slots // tm_size
    row_count = frames_local * slots
    half = width // 2

    def to_slots(value):
        view = value.reshape(frames_local, tm_size, slots_local, value.shape[-1])
        parts = []
        for o in range(tm_size):
            part = lax.dynamic_index_in_dim(view, place.tm ^ o, 1, keepdims=False)
            parts.append(place.tm_flip(part, o) if o else part)
        return parts

    def from_slots(value, offsets=range(tm_size)):
        view = value.reshape(tm_size, frames_local, slots_local, value.shape[-1])
        return [place.tm_flip(view[o], o) if o else view[o] for o in offsets]

    def in_slots(parts):
        return jnp.concatenate(parts, axis=0)

    def in_frames(parts):
        return jnp.stack(unscramble(parts, place.tm), axis=1).reshape(frames_local, slots, -1)

    def own_and_other(value, axis):
        first, second = (lax.index_in_dim(value, i, axis, keepdims=False) for i in (0, 1))
        return jnp.where(core == 0, first, second), jnp.where(core == 0, second, first)

    def in_order(own, other, axis):
        pair = [jnp.where(core == 0, own, other), jnp.where(core == 0, other, own)]
        return jnp.stack(pair, axis=axis)

    def woven(own, other):
        cuts = [slice(i, i + half) for i in range(0, own.shape[1], half)]
        own_first = [x[:, cut] for cut in cuts for x in (own, other)]
        other_first = [x[:, cut] for cut in cuts for x in (other, own)]
        return jnp.where(
            core == 0,
            jnp.concatenate(own_first, axis=1),
            jnp.concatenate(other_first, axis=1),
        )

    thin = width // total
    counts = [ACTIONS, 3, 3, 1]
    ends = [sum(counts[:i]) for i in range(len(counts) + 1)]
    rows = s_qkv.shape[0]
    hidden_half = w_down.shape[0] // 2

    def attention_group(qkv, out):
        qkv = own_and_other(qkv.reshape(rows, 3, 2, half), 2)
        both = [
            jnp.concatenate([a.reshape(rows, 3 * half), b], axis=1)
            for a, b in zip(qkv, own_and_other(out.reshape(rows, 2, half), 1))
        ]
        return Chain(gather(place, *both))

    front = attention_group(s_qkv, s_out)
    tokens = along(tokens, front)
    rows_in = (action_table, norm_gains, norm_shifts, b_down)
    tokens, rows_in, b_up, grad_out = lax.optimization_barrier((tokens, rows_in, b_up, grad_out))
    action_table, norm_gains, norm_shifts, b_down = rows_in
    small = jnp.concatenate([action_table, norm_gains, norm_shifts, b_down[None]], axis=0).T
    small = jnp.pad(small, ((0, 0), (0, LANES - ends[-1])))
    b_up = jnp.pad(b_up[None], ((0, GROUP - 1), (0, LANES - b_up.shape[0])))
    small = jnp.concatenate([small, b_up], axis=0)
    tokens = along(tokens, front)
    tokens, grad_out = lax.optimization_barrier((tokens, grad_out))
    cotangent = to_slots(grad_out.reshape(frames_local, slots, width))
    small = Chain(gather_small(place, small))
    tokens = along(tokens, small)
    tokens = along(tokens, small)
    tokens, t_qkv, t_out = lax.optimization_barrier((tokens, t_qkv, t_out))
    tokens = along(tokens, front)
    middle = attention_group(t_qkv, t_out)
    tokens = along(tokens, middle)
    tokens, w_up = lax.optimization_barrier((tokens, w_up))
    up_pair = own_and_other(w_up.reshape(rows, total, 2, hidden_half), 2)
    rising = Chain(gather(place, *[x.reshape(rows, -1) for x in up_pair], len(place.xy) // 2))
    tokens, cotangent = lax.optimization_barrier((tokens, cotangent))
    tokens = along(tokens, front, middle, rising)
    tokens = along(tokens, small)
    tokens = along(tokens, small)
    tokens, w_down = lax.optimization_barrier((tokens, w_down))
    falling = Chain(gather(place, *own_and_other(w_down.reshape(2, hidden_half, width), 0)))
    tokens = along(tokens, front, middle, rising, falling)
    while not small.done():
        tokens = along(tokens, small)
    small = small.result.astype(f32)
    table = small[:, :thin].reshape(width, LANES).T

    def unpack(i):
        return table[ends[i] : ends[i + 1]]

    action_rows, gains, shifts, down_bias = [unpack(i) for i in range(4)]
    up_bias = small[:, thin, : 2 * hidden_half].reshape(total, 2, hidden_half)
    up_bias = [x.reshape(1, -1) for x in own_and_other(up_bias, 1)]

    onehot = (actions == jnp.arange(ACTIONS)[None, :]).astype(f32)
    embedded = jnp.dot(onehot, action_rows, precision=highest)
    tokens = tokens.reshape(frames_local, slots, width)
    embedded = embedded[:, None, :]
    normed1 = norm(tokens, embedded, gains[0], shifts[0])
    normed1 = land(normed1, front, middle, rising, falling)
    normed1 = launch(normed1, front, middle, falling)
    s_halves = [x.reshape(width, -1) for x in finish(front)]
    here = core.astype(jnp.int32).reshape(1)

    def projected(x, w, outer):
        return project(x, w, 3 * half, here).reshape(*outer, -1)

    spatial = [projected(normed1, w, (frames_local, slots)) for w in s_halves]
    spatial = land(spatial, middle, falling)
    spatial = launch(spatial, middle, rising)

    def frame_index(i):
        return (i, 0, 0)

    def slot_index(i):
        return (0, i, 0)

    spatial_place = (
        jnp.stack([sides[0], core.astype(jnp.int32)]), (1, slots), frames_local, frame_index,
    )
    (s_mixed,) = run_attention(
        partial(attention_forward, spatial_bias), *spatial_place, spatial, [width]
    )
    s_mixed = s_mixed.reshape(row_count, width)
    flat = tokens.reshape(row_count, width)
    hidden1 = add_spatial(s_mixed, s_halves, flat, embedded, here)

    hidden1 = hold(hidden1, middle, rising)
    parts = to_slots(hidden1.reshape(tokens.shape))
    parts[1] = along(parts[1], middle, rising)
    parts = land(parts, middle, rising)
    hidden1 = in_slots(parts)
    frames = hidden1.shape[0]
    slot_at = place.tm * slots_local + jnp.arange(slots_local)
    mask = (slot_at < sides[0] * sides[0])[None, :, None]
    nothing = jnp.zeros((1, 1, width), f32)
    normed2 = norm(hidden1, nothing, gains[1], shifts[1])
    hidden1 = hidden1.reshape(row_count, width)
    normed2 = launch(normed2, rising, falling)
    t_halves = [x.reshape(width, -1) for x in finish(middle)]
    temporal = [projected(normed2, w, (frames, slots_local)) for w in t_halves]
    temporal_place = (
        jnp.stack([place.tm.astype(jnp.int32), core.astype(jnp.int32)]), (frames, GROUP),
        slots_local // GROUP, slot_index,
    )
    make_bias = partial(temporal_bias, frames_local)
    (t_mixed,) = run_attention(
        partial(attention_forward, make_bias), *temporal_place, temporal, [width]
    )
    t_mixed = t_mixed.reshape(row_count, width)
    hidden2, normed3 = add_temporal(t_mixed, t_halves, hidden1, gains[2], shifts[2], here)
    normed3 = along(normed3, rising, falling)
    up_halves = [x.reshape(width, -1) for x in finish(rising)]
    first = up_project(normed3, up_halves[0], up_bias[0])
    first = along(first, falling)
    normed3, first = lax.optimization_barrier((normed3, first))
    second = up_project(normed3, up_halves[1], up_bias[1])
    (active, slope), (active2, slope2) = first, second

    core_pair = (place.core_bit, place.core_bit)

    def exchanged(grad):
        return place.flip(grad, core_pair)

    def sums(*parts):
        return Chain(scatter(place, lambda k, value: weight_split(parts, k, value, core)))

    down_in = jnp.where(mask, in_slots(cotangent), 0).reshape(row_count, width)
    send = weight_grad(active2, down_in, total, here)
    down_in, send = land((down_in, send), falling)
    (own_rows,) = up_to(falling, total.bit_length() - 1)
    own_rows = own_rows.reshape(-1, width)
    down_in, send = launch(down_in, falling, also=[send])
    got = exchanged(send)
    inner_grad, b_sum = inner_back(down_in, own_rows, slope, here)
    hidden2, inner_grad = land((hidden2, inner_grad), falling)
    down_halves = [x.reshape(-1, width) for x in finish(falling)]
    inner_grad2, b_sum2 = inner_back(down_in, down_halves[1], slope2, here)
    send = weight_grad(normed3, inner_grad2, total, here)
    down_in, hidden2, send, got = lax.optimization_barrier((down_in, hidden2, send, got))
    got_up = exchanged(send)
    s_down = sums((active, down_in, got, None))
    down_in, hidden2 = launch((down_in, hidden2), s_down)

    mask_rows = jnp.broadcast_to(mask, (frames, slots_local, 1)).reshape(row_count, 1).astype(f32)
    mixed = down_project([active, active2], down_halves, hidden2, down_bias, mask_rows, here)
    mixed, got_up = lax.optimization_barrier((mixed, got_up))
    s_up = sums((normed3, inner_grad, got_up, None))
    hidden2, s_up.pending, mixed = land((hidden2, s_up.pending, mixed), s_down)
    hidden2 = launch(hidden2, s_down, s_up)

    grad2, sums3 = norm_back(
        (inner_grad, inner_grad2), up_halves, hidden2, nothing, gains[2], down_in, bf16, here
    )
    b_sums = [x.reshape(total, -1, thin).swapaxes(0, 1) for x in (b_sum, b_sum2)]
    late_rows = [x.reshape(-1, width) for x in b_sums]
    late_rows = jnp.where(
        core == 0, jnp.concatenate(late_rows, axis=0), jnp.concatenate(late_rows[::-1], axis=0)
    )
    late_rows = jnp.concatenate([jnp.sum(down_in.astype(f32), axis=0)[None], late_rows], axis=0)
    t_mix_grad = mixed_back(grad2, t_halves, here).reshape(frames, slots_local, width)
    send2 = weight_grad(t_mixed, grad2, total, here, 1)

    def back(side, where, make, values, grad):
        (out,) = run_attention(
            partial(attention_backward, make, (side,)), *where, [values[side], grad], [3 * half]
        )
        return out.reshape(row_count, -1)

    t_grad2 = back(1, temporal_place, make_bias, temporal, t_mix_grad)
    t_mix_grad, t_grad2, late_rows = land((t_mix_grad, t_grad2, late_rows), s_down, s_up)
    t_mix_grad, t_grad2 = launch((t_mix_grad, t_grad2), s_down, s_up)
    t_grad = back(0, temporal_place, make_bias, temporal, t_mix_grad)
    send = weight_grad(normed2, t_grad2, total, here)
    t_grads, send = land(((t_grad, t_grad2), send), s_down, s_up)
    t_grads, send, send2 = launch(t_grads, s_down, also=[send, send2])
    gots = [exchanged(send), exchanged(send2)]

    grad1, sums2 = norm_back(t_grads, t_halves, hidden1, nothing, gains[1], grad2, bf16, here)
    grad1 = hold(grad1, s_down)
    grad1, gots = lax.optimization_barrier((grad1, gots))
    parts = from_slots(grad1)
    parts[1] = along(parts[1], s_down, s_up)
    s_time = sums((normed2, t_grads[0], gots[0], None), (t_mixed, grad2, gots[1], 0))
    parts[0], s_time.pending = lax.optimization_barrier((parts[0], s_time.pending))
    parts = land(parts, s_down, s_up)
    grad1 = in_frames(parts).reshape(row_count, width)
    grad1 = launch(grad1, s_down, s_up, s_time)

    send2 = weight_grad(s_mixed, grad1, total, here, 1)
    mix_grad = mixed_back(grad1, s_halves, here).reshape(frames_local, slots, width)
    s_grad2 = back(1, spatial_place, spatial_bias, spatial, mix_grad)
    send = weight_grad(normed1, s_grad2, total, here)
    mix_grad, send, send2 = land((mix_grad, send, send2), s_down, s_up, s_time)
    mix_grad, send, send2 = launch(mix_grad, s_down, s_up, s_time, also=[send, send2])
    gots = [exchanged(send), exchanged(send2)]

    s_grad = back(0, spatial_place, spatial_bias, spatial, mix_grad)
    s_grad, *gots = land(s_grad, s_down, s_up, s_time, also=gots)
    s_space = sums((normed1, s_grad, gots[0], None), (s_mixed, grad1, gots[1], 0))
    s_grads = launch((s_grad, s_grad2), s_time, s_space)

    input_grad, sums1 = norm_back(
        s_grads, s_halves, flat, embedded, gains[0], grad1, f32, here
    )
    sums1, input_grad = land((sums1, input_grad), s_time, s_space)
    sums1, input_grad = launch((sums1, input_grad), s_time, s_space)
    g_actions = jnp.sum(onehot[:, :, None] * sums1[:, 2][:, None, :], axis=0)
    all_sums = [jnp.sum(x[:, :2], axis=0) for x in (sums1, sums2, sums3)]
    both_norms = [jnp.stack([x[i] for x in all_sums]) for i in (0, 1)]
    packed = jnp.concatenate([g_actions, *both_norms, late_rows], axis=0)
    s_small = Chain(scatter_small(place, packed))
    packed = launch(packed, s_small)
    packed = land(packed, s_time, s_space, s_small)
    packed, mixed = launch((packed, mixed), s_time, s_space, s_small)
    near = from_slots(mixed, range(tm_size // 2 + 1))
    packed, down_sums, up_sums = lax.optimization_barrier((packed, finish(s_down), finish(s_up)))
    g_w_down = in_order(*down_sums, 0).reshape(w_down.shape)
    g_w_up = in_order(*[x.reshape(rows, total, -1) for x in up_sums], 2).reshape(w_up.shape)
    packed = along(packed, s_small)
    packed, *near = land(packed, s_time, s_space, s_small, also=near)
    packed, mixed = launch((packed, mixed), s_time, s_space, s_small)
    packed, g_w_down, g_w_up = lax.optimization_barrier((packed, g_w_down, g_w_up))
    far = from_slots(mixed, range(tm_size // 2 + 1, tm_size))
    packed = along(packed, s_small)
    packed, *far = land(packed, s_time, s_space, s_small, also=far)
    packed = launch(packed, s_time, s_space, s_small)
    mixed = in_frames(near + far)
    packed, mixed = lax.optimization_barrier((packed, mixed))
    while not (s_time.done() and s_space.done() and s_small.done()):
        packed = along(packed, s_time, s_space, s_small)
    summed = s_small.result
    (g_t_qkv, g_t_out), (g_s_qkv, g_s_out) = [
        [woven(*[x[:, cut] for x in c.result]) for cut in (slice(3 * half), slice(3 * half, None))]
        for c in (s_time, s_space)
    ]

    return (
        mixed.reshape(shape),
        input_grad.reshape(shape),
        summed[:8],
        summed[8:11],
        summed[11:14],
        g_s_qkv,
        g_s_out,
        g_t_qkv,
        g_t_out,
        g_w_up,
        summed[15:].reshape(-1),
        g_w_down,
        summed[14],
    )


def solution(mesh):
    whole = P(("tm", "clip"), None)
    spread = P(None, ("tm", "clip"))
    frames = P("tm", "clip", None, None)
    vector = P(("tm", "clip"))
    return jax.shard_map(
        on_device,
        mesh=mesh,
        in_specs=(
            frames, P("tm", "clip"), P("clip"), spread, spread, spread, whole, whole, whole,
            whole, whole, vector, whole, vector, frames,
        ),
        out_specs=(
            frames, frames, spread, spread, spread, whole, whole, whole, whole, whole, vector,
            whole, vector,
        ),
        check_vma=False,
    )
```

```python
import math
from functools import partial

import jax
import jax.numpy as jnp
from jax import lax
from jax.experimental import pallas as pl
from jax.experimental.pallas import tpu as pltpu
from jax.sharding import PartitionSpec as P

H = 16
E = 64
ACTIONS = 8
FRAMES = 16
AXES = ("tm", "clip")
LANES = 128
GROUP = 16

negative = -1e30
highest = lax.Precision.HIGHEST
MIB = 1024 * 1024
bf16, f32 = jnp.bfloat16, jnp.float32
NO_COST = pl.CostEstimate(flops=0, bytes_accessed=0, transcendentals=0)


def params(blocks, margin=6):
    size = sum(math.prod(shape) * jnp.dtype(dtype).itemsize * n for shape, dtype, n in blocks)
    return pltpu.CompilerParams(vmem_limit_bytes=(-(-size // MIB) + margin) * MIB)


class Place:
    def __init__(self):
        tm_size, clip_size = lax.axis_size("tm"), lax.axis_size("clip")
        self.tm_size, self.clip_size, self.total = tm_size, clip_size, tm_size * clip_size
        self.tm = lax.axis_index("tm")
        self.me = self.tm * clip_size + lax.axis_index("clip")
        self.core_bit = clip_size
        self.core = self.bit_of(clip_size)
        clip_bits = [1 << i for i in range(clip_size.bit_length() - 1)]
        tm_bits = [clip_size << i for i in range(tm_size.bit_length() - 1)]
        x, z, y = clip_bits[:-2], clip_bits[-2:], tm_bits[1:]
        self.z = [(b, b) for b in z]
        self.xy = list(zip(x + y, y + x))

    def bit_of(self, bit):
        return (self.me // bit) % 2

    def mine(self, pair):
        return jnp.where(self.core == 0, self.bit_of(pair[0]), self.bit_of(pair[1]))

    def choose(self, pair):
        return jnp.where(self.core == 0, pair[0], pair[1])

    def flip(self, value, pair):
        moves = [(i, i ^ pair[(i // self.core_bit) % 2]) for i in range(self.total)]
        return lax.ppermute(value, AXES, moves)

    def tm_flip(self, value, offset):
        moves = [(i, i ^ (offset * self.clip_size)) for i in range(self.total)]
        return lax.ppermute(value, AXES, moves)


def below(have, bit):
    return sum(1 for b in have if b < bit)


def unscramble(parts, me):
    bit = 1
    while bit < len(parts):
        swap = (me & bit) != 0
        parts = [jnp.where(swap, parts[p ^ bit], parts[p]) for p in range(len(parts))]
        bit *= 2
    return parts


def position(m, value, k):
    m = jnp.int32(m)
    high = lax.shift_left(lax.shift_right_logical(m, k), k + 1)
    return high | lax.shift_left(value, k) | (m & (lax.shift_left(jnp.int32(1), k) - 1))


def merge_body(info_ref, mine_ref, other_ref, out_ref):
    k, value = info_ref[0], info_ref[1]
    for m in range(mine_ref.shape[0]):
        out_ref[position(m, value, k)] = mine_ref[m]
        out_ref[position(m, 1 - value, k)] = other_ref[m]


def column_block(shape):
    blocks, rows, cols = shape
    return cols if blocks * rows * cols <= 512 * 1024 else min(cols, 512)


def merge(mine, other, k, value):
    m, r, n = mine.shape
    block = column_block((2 * m, r, n))
    spec = pl.BlockSpec((m, r, block), lambda j: (0, 0, j))
    return pl.pallas_call(
        merge_body,
        grid=(n // block,),
        in_specs=[pl.BlockSpec(memory_space=pltpu.SMEM), spec, spec],
        out_specs=pl.BlockSpec((2 * m, r, block), lambda j: (0, 0, j)),
        out_shape=jax.ShapeDtypeStruct((2 * m, r, n), mine.dtype),
        compiler_params=params([((4 * m, r, block), mine.dtype, 2)], 2),
        cost_estimate=NO_COST,
    )(jnp.stack([jnp.int32(k), value.astype(jnp.int32)]), mine, other)


def part(info_ref, source_ref, send_ref, keep_ref):
    k, value = info_ref[0], info_ref[1]
    for m in range(send_ref.shape[0]):
        for out_ref, at in ((send_ref, 1 - value), (keep_ref, value)):
            out_ref[m] = source_ref[position(m, at, k)].astype(out_ref.dtype)


def split_body(info_ref, a_ref, b_ref, send_ref, keep_ref):
    k, value = info_ref[0], info_ref[1]
    for m in range(send_ref.shape[0]):
        for out_ref, at in ((send_ref, 1 - value), (keep_ref, value)):
            i = position(m, at, k)
            out_ref[m] = (a_ref[i].astype(f32) + b_ref[i].astype(f32)).astype(out_ref.dtype)


def split(a, b, k, value, dtype):
    blocks, r, n = a.shape
    block = column_block(a.shape)
    out = jax.ShapeDtypeStruct((blocks // 2, r, n), dtype)
    return pl.pallas_call(
        split_body,
        grid=(n // block,),
        in_specs=[pl.BlockSpec(memory_space=pltpu.SMEM)]
        + [pl.BlockSpec((blocks, r, block), lambda j: (0, 0, j))] * 2,
        out_specs=[pl.BlockSpec((blocks // 2, r, block), lambda j: (0, 0, j))] * 2,
        out_shape=[out, out],
        compiler_params=params([((3 * blocks, r, block), dtype, 2)], 3),
        cost_estimate=NO_COST,
    )(jnp.stack([jnp.int32(k), value.astype(jnp.int32)]), a, b)


def gather_small(place, value):
    core = (place.core_bit, place.core_bit)
    x_and_y = [(b, b) for b, _ in place.xy]
    count = len(x_and_y) // 2
    blocks, have = value[None], []
    for pair in x_and_y[:count] + [core] + x_and_y[count:] + place.z:
        (send,) = yield [blocks]
        (got,) = yield [place.flip(send, pair)]
        blocks = merge(blocks, got, below(have, pair[0]), place.bit_of(pair[0]))
        have.append(pair[0])
    return blocks


def scatter_small(place, value):
    bit = place.total // 2
    while bit:
        half = value.shape[1] // 2
        low_half, high_half = value[:, :half], value[:, half:]
        mine = (place.me & bit) != 0
        (send,) = yield [jnp.where(mine, low_half, high_half)]
        (got,) = yield [place.flip(send, (bit, bit))]
        value = jnp.where(mine, high_half, low_half) + got
        bit //= 2
    return value


def gather(place, keep, send, ahead=0):
    core = (place.core_bit, place.core_bit)
    have = ([], [])
    blocks, out = keep[None], send[None]
    for pair in [core] + place.xy[:ahead] + place.z[::-1] + place.xy[ahead:]:
        (out,) = yield [out]
        (got,) = yield [place.flip(out, pair)]
        k = [below(h, b) for h, b in zip(have, pair)]
        blocks = out = merge(blocks, got, place.choose(k), place.mine(pair))
        have = (have[0] + [pair[0]], have[1] + [pair[1]])
    (out,) = yield [out]
    (got,) = yield [place.flip(out, core)]
    return blocks, got


def scatter(place, first):
    core = (place.core_bit, place.core_bit)
    bits = [1 << i for i in range(place.total.bit_length() - 1)]
    have, pairs = (bits, bits), None
    for pair in place.xy[::-1] + place.z + [core]:
        have = tuple([b for b in h if b != bit] for h, bit in zip(have, pair))
        k = place.choose([below(h, b) for h, b in zip(have, pair)])
        dtype = f32 if pair == core else bf16
        if pairs is None:
            send, keep = first(k, place.mine(pair))
        else:
            send, keep = split(*pairs, k, place.mine(pair), dtype)
        (send,) = yield [send]
        (got,) = yield [place.flip(send, pair)]
        pairs = (keep, got)
    return keep[0], got[0]


class Chain:
    def __init__(self, steps):
        self.steps, self.flying, self.result, self.started = steps, False, None, 0
        self.pending = next(steps)

    def done(self):
        return self.result is not None

    def move(self):
        try:
            self.pending = self.steps.send(self.pending)
        except StopIteration as stop:
            self.result = stop.value
        self.flying = not self.flying
        self.started += self.flying


def hold(value, *chains):
    chains = [c for c in chains if c.flying]
    value, got = lax.optimization_barrier((value, [c.pending for c in chains]))
    for c, g in zip(chains, got):
        c.pending = g
    return value


def land(value, *chains, also=()):
    chains = [c for c in chains if c.flying]
    value, got, also = lax.optimization_barrier((value, [c.pending for c in chains], list(also)))
    for c, g in zip(chains, got):
        c.pending = g
        c.move()
    return (value, *also) if also else value


def launch(value, *chains, also=()):
    chains = [c for c in chains if not c.done() and not c.flying]
    value, sent, also = lax.optimization_barrier((value, [c.pending for c in chains], list(also)))
    for c, g in zip(chains, sent):
        c.pending = g
        c.move()
    return (value, *also) if also else value


def along(value, *chains):
    return launch(land(value, *chains), *chains)


def up_to(chain, count):
    while chain.started < count or chain.flying:
        chain.move()
    return chain.pending


def finish(chain):
    while not chain.done():
        chain.move()
    return chain.result


def spatial_bias(scalar, rows, keys):
    key = lax.broadcasted_iota(jnp.int32, (1, rows) if keys == 1 else (rows, 1), keys)
    return jnp.where(key < scalar * scalar, 0.0, negative)


def temporal_bias(frames_local, scalar, rows, keys):
    def place(axis):
        index = lax.broadcasted_iota(jnp.int32, (rows, rows), axis)
        slot, at = index % GROUP, index // GROUP
        frame = ((at // frames_local) ^ scalar) * frames_local + at % frames_local
        return slot, frame

    slot_q, frame_q = place(1 - keys)
    slot_k, frame_k = place(keys)
    return jnp.where((slot_q == slot_k) & (frame_q >= frame_k), 0.0, negative)


def dot_t(a, b):
    return lax.dot_general(a, b, (((1,), (1,)), ((), ())), preferred_element_type=f32)


def t_dot(a, b):
    return lax.dot_general(a, b, (((0,), (0,)), ((), ())), preferred_element_type=f32)


def columns(scalar_ref, side, start):
    half = H * E // 2
    return pl.ds(pl.multiple_of((scalar_ref[1] ^ side) * half + start, LANES), LANES)


def two_heads(rows):
    half = lax.broadcasted_iota(jnp.int32, (rows, LANES), 1) < E

    def apart(x):
        return jnp.concatenate([jnp.where(half, x, 0), jnp.where(half, 0, x)], axis=0)

    def together(x):
        return jnp.where(half, x[:rows], x[rows:])

    return apart, together


def head_pairs(sides, refs):
    a, b, width = refs[0].shape
    rows, width = a * b, width // 3
    for i, side in enumerate(sides):
        for c in range(0, width, LANES):
            q, k, v = (
                refs[i][:, :, at : at + LANES].reshape(rows, LANES)
                for at in (c, width + c, 2 * width + c)
            )
            yield i, side, c, q * bf16(E ** (-0.5)), k, v


def in_turn(items, first, last):
    waiting = None
    for item in items:
        ready = first(*item)
        if waiting is not None:
            last(*waiting)
        waiting = ready
    last(*waiting)


def attention_forward(make_bias, scalar_ref, own_ref, other_ref, out_ref):
    a, b, width = own_ref.shape
    rows, width = a * b, width // 3
    bias = make_bias(scalar_ref[0], rows, 1)
    apart, together = two_heads(rows)

    def first(i, side, c, q, k, v):
        scores = dot_t(apart(q), k).reshape(2, rows, rows) + bias[None]
        weights = jnp.exp(scores - jnp.max(scores, axis=2, keepdims=True))
        scale = 1.0 / jnp.sum(weights, axis=2, keepdims=True)
        return side, c, v, weights.astype(bf16).reshape(2 * rows, rows), scale

    def last(side, c, v, weights, scale):
        mixed = jnp.dot(weights, v, preferred_element_type=f32) * scale.reshape(2 * rows, 1)
        mixed = together(mixed).astype(out_ref.dtype)
        out_ref[:, :, columns(scalar_ref, side, c)] = mixed.reshape(a, b, LANES)

    in_turn(head_pairs((0, 1), (own_ref, other_ref)), first, last)


def attention_backward(make_bias, sides, scalar_ref, *refs):
    grad_ref = refs[len(sides)]
    a, b, width = refs[0].shape
    rows, width = a * b, width // 3
    bias = make_bias(scalar_ref[0], rows, 0)
    apart, together = two_heads(rows)

    def first(i, side, c, q, k, v):
        g = grad_ref[:, :, columns(scalar_ref, side, c)].reshape(rows, LANES)
        scores = dot_t(apart(k), q).reshape(2, rows, rows) + bias[None]
        prob_grad = dot_t(apart(v), g).reshape(2, rows, rows)
        weights = jnp.exp(scores - jnp.max(scores, axis=1, keepdims=True))
        probs = weights * (1.0 / jnp.sum(weights, axis=1, keepdims=True))
        delta = jnp.sum(probs * prob_grad, axis=1, keepdims=True)
        return i, c, q, k, g, probs.astype(bf16), (probs * (prob_grad - delta)).astype(bf16)

    def last(i, c, q, k, g, probs, score_grad):
        turned = jnp.concatenate([score_grad[0].T, score_grad[1].T], axis=0)
        dq = jnp.dot(turned, k, preferred_element_type=f32) * E ** (-0.5)
        dk = jnp.dot(score_grad.reshape(2 * rows, rows), q, preferred_element_type=f32)
        dv = jnp.dot(probs.reshape(2 * rows, rows), g, preferred_element_type=f32)
        for index, grad in enumerate((dq, dk, dv)):
            start = index * width + c
            merged = together(grad).astype(bf16).reshape(a, b, LANES)
            refs[len(sides) + 1 + i][:, :, start : start + LANES] = merged

    in_turn(head_pairs(sides, refs), first, last)


def run_attention(body, scalars, block, grid, index, inputs, out_widths):
    a, b = block
    outer = inputs[0].shape[:2]
    return pl.pallas_call(
        body,
        grid=(grid,),
        in_specs=[pl.BlockSpec(memory_space=pltpu.SMEM)]
        + [pl.BlockSpec((a, b, x.shape[-1]), index) for x in inputs],
        out_specs=[pl.BlockSpec((a, b, width), index) for width in out_widths],
        out_shape=[jax.ShapeDtypeStruct((*outer, width), bf16) for width in out_widths],
        compiler_params=params(
            [((a, b, width), bf16, 2) for width in (*(x.shape[-1] for x in inputs), *out_widths)], 8
        ),
        cost_estimate=NO_COST,
    )(scalars, *inputs)


def centre(x):
    average = jnp.mean(x, axis=-1, keepdims=True)
    centered = x - average
    variance = jnp.mean(centered * centered, axis=-1, keepdims=True)
    scale = lax.rsqrt(variance + 1e-05)
    return centered * scale, scale


def norm_body(x_ref, added_ref, gain_ref, shift_ref, out_ref):
    unit, _ = centre(x_ref[0].astype(f32) + added_ref[0])
    out_ref[0] = (unit * gain_ref[...] + shift_ref[...]).astype(out_ref.dtype)


def by_rows(body, arrays, rows, outs):
    blocks = arrays[0].shape[0]
    specs = []
    for x in arrays:
        if x.ndim == 2:
            specs.append(pl.BlockSpec(x.shape, lambda i: (0, 0)))
        else:
            at = (lambda i: (i, 0, 0)) if x.shape[0] == blocks else (lambda i: (0, 0, 0))
            specs.append(pl.BlockSpec((1, *x.shape[1:]), at))
    return pl.pallas_call(
        body,
        grid=(blocks,),
        in_specs=specs,
        out_specs=[pl.BlockSpec((1, *shape[1:]), lambda i: (i, 0, 0)) for shape, _ in outs],
        out_shape=[jax.ShapeDtypeStruct(shape, dtype) for shape, dtype in outs],
        compiler_params=params([(x.shape[1:], f32, 4) for x in arrays]),
        cost_estimate=NO_COST,
    )(*arrays)


def norm(x, added, gain, shift):
    shape = (x.shape[0] * x.shape[1] // 256, 256, x.shape[2])
    arrays = [x.reshape(shape), added, gain[None], shift[None]]
    (out,) = by_rows(norm_body, arrays, 256, [(shape, bf16)])
    return out.reshape(-1, shape[2])


BLOCK = 512


def dense(body, grid, scalars, inputs, outs, scratch=(), margin=6):
    used = [(block, x.dtype, 1 if index is FIXED else 2) for x, block, index in inputs]
    used += [(block, dtype, 2) for _, dtype, block, _ in outs]
    used += [(x.shape, x.dtype, 1) for x in scratch]

    def spec(block, index):
        if index is FIXED:
            zeros = (0,) * len(block)
            return pl.BlockSpec(block, lambda *_: zeros, pipeline_mode=pl.Buffered(1))
        return pl.BlockSpec(block, index)

    return pl.pallas_call(
        body,
        grid_spec=pltpu.PrefetchScalarGridSpec(
            num_scalar_prefetch=1,
            grid=grid,
            in_specs=[spec(block, index) for _, block, index in inputs],
            out_specs=[pl.BlockSpec(block, index) for _, _, block, index in outs],
            scratch_shapes=list(scratch),
        ),
        out_shape=[jax.ShapeDtypeStruct(shape, dtype) for shape, dtype, _, _ in outs],
        compiler_params=params(used, margin),
        cost_estimate=NO_COST,
    )(scalars, *[x for x, _, _ in inputs])


FIXED = None


def at(*index):
    return lambda j, ref: index


def whole(x):
    return (x, x.shape, FIXED)


def rows_of(x, rows=256):
    return (x, (rows, x.shape[1]), lambda i, ref: (i, 0))


def project_body(_, x_ref, w_ref, out_ref):
    out_ref[...] = jnp.dot(x_ref[...], w_ref[...], preferred_element_type=f32).astype(bf16)


def project(x, w, cols, scalars):
    index = lambda j, ref: (0, j)
    rows = x.shape[0]
    (out,) = dense(
        project_body, (cols // BLOCK,), scalars,
        [whole(x), (w, (w.shape[0], BLOCK), index)],
        [((rows, cols), bf16, (rows, BLOCK), index)],
    )
    return out


def sides(core, own_ref, other_ref):
    for side, ref in ((core, own_ref), (1 - core, other_ref)):
        yield pl.ds(pl.multiple_of(side * BLOCK, BLOCK), BLOCK), ref


def hidden1_body(core_ref, mixed_ref, own_ref, other_ref, x_ref, added_ref, out_ref):
    for cols, w_ref in sides(core_ref[0], own_ref, other_ref):
        dot = jnp.dot(mixed_ref[...], w_ref[...], preferred_element_type=f32)
        out_ref[:, cols] = (x_ref[:, cols].astype(f32) + added_ref[0, :, cols] + dot).astype(bf16)


def out_half(w):
    return (w, (w.shape[0], BLOCK), at(0, w.shape[1] // BLOCK - 1))


def add_spatial(mixed, halves, x, added, scalars):
    rows, width = x.shape
    step = rows // added.shape[0]
    (out,) = dense(
        hidden1_body, (rows // step,), scalars,
        [rows_of(mixed, step), *[out_half(w) for w in halves], rows_of(x, step),
         (added, (1, 1, width), lambda i, ref: (i, 0, 0))],
        [((rows, width), bf16, (step, width), lambda i, ref: (i, 0))],
    )
    return out


def hidden2_body(
    core_ref, mixed_ref, own_ref, other_ref, x_ref, gain_ref, shift_ref, out_ref, norm_ref
):
    for cols, w_ref in sides(core_ref[0], own_ref, other_ref):
        dot = jnp.dot(mixed_ref[...], w_ref[...], preferred_element_type=f32)
        out_ref[:, cols] = x_ref[:, cols].astype(f32) + dot
    unit, _ = centre(out_ref[...])
    norm_ref[...] = (unit * gain_ref[...] + shift_ref[...]).astype(bf16)


def add_temporal(mixed, halves, x, gain, shift, scalars):
    rows, width = x.shape
    block = ((256, width), lambda i, ref: (i, 0))
    return dense(
        hidden2_body, (rows // 256,), scalars,
        [rows_of(mixed), *[out_half(w) for w in halves], rows_of(x), whole(gain[None]),
         whole(shift[None])],
        [((rows, width), f32, *block), ((rows, width), bf16, *block)],
    )


def hidden3_body(_, a_ref, b_ref, own_ref, other_ref, x_ref, bias_ref, mask_ref, out_ref):
    out = x_ref[...] + bias_ref[...]
    out += jnp.dot(a_ref[...], own_ref[...], preferred_element_type=f32)
    out += jnp.dot(b_ref[...], other_ref[...], preferred_element_type=f32)
    out_ref[...] = jnp.where(mask_ref[...] > 0, out, 0).astype(bf16)


def down_project(actives, halves, x, bias, mask, scalars):
    rows, width = x.shape
    (out,) = dense(
        hidden3_body, (rows // 256,), scalars,
        [*[rows_of(y) for y in actives], *[whole(w) for w in halves], rows_of(x), whole(bias),
         rows_of(mask)],
        [((rows, width), bf16, (256, width), lambda i, ref: (i, 0))], margin=30,
    )
    return out


def inner_back_body(_, x_ref, w_ref, slope_ref, out_ref, sum_ref):
    grad = dot_t(x_ref[...], w_ref[...]) * slope_ref[...].astype(f32)
    out_ref[...] = grad.astype(bf16)
    sum_ref[...] = jnp.sum(out_ref[...].astype(f32), axis=0, keepdims=True)


def inner_back(x, w, slope, scalars):
    rows, cols = slope.shape
    index = lambda j, ref: (0, j)
    return dense(
        inner_back_body, (cols // BLOCK,), scalars,
        [whole(x), (w, (BLOCK, w.shape[1]), lambda j, ref: (j, 0)), (slope, (rows, BLOCK), index)],
        [((rows, cols), bf16, (rows, BLOCK), index), ((1, cols), f32, (1, BLOCK), index)],
    )


def norm_back_body(
    _, a_ref, b_ref, own_ref, other_ref, x_ref, added_ref, gain_ref, rest_ref, out_ref, sums_ref
):
    grad = dot_t(a_ref[...], own_ref[...]) + dot_t(b_ref[...], other_ref[...])
    unit, scale = centre(x_ref[...].astype(f32) + added_ref[0])
    scaled = grad * gain_ref[...]
    first = jnp.mean(scaled, axis=-1, keepdims=True)
    second = jnp.mean(scaled * unit, axis=-1, keepdims=True)
    out = rest_ref[...].astype(f32) + scale * (scaled - first - unit * second)
    out_ref[...] = out.astype(out_ref.dtype)
    terms = (grad * unit, grad, out)
    sums_ref[0] = jnp.concatenate([jnp.sum(x, axis=0, keepdims=True) for x in terms], axis=0)


def norm_back(grads, halves, x, added, gain, rest, dtype, scalars):
    rows, width = x.shape
    step, cols = 256, grads[0].shape[1]
    added_at = (lambda i, ref: (i, 0, 0)) if added.shape[0] > 1 else at(0, 0, 0)
    return dense(
        norm_back_body, (rows // step,), scalars,
        [*[rows_of(g) for g in grads], *[(w, (w.shape[0], cols), FIXED) for w in halves],
         rows_of(x), (added, (1, 1, width), added_at), whole(gain[None]), rows_of(rest)],
        [((rows, width), dtype, (step, width), lambda i, ref: (i, 0)),
         ((rows // step, 3, width), f32, (1, 3, width), lambda i, ref: (i, 0, 0))],
        margin=30 if dtype == f32 or cols > 3 * BLOCK else 6,
    )


def mixed_back_body(core_ref, x_ref, own_ref, other_ref, out_ref):
    grad = 0
    for cols, w_ref in sides(core_ref[0], own_ref, other_ref):
        grad += dot_t(x_ref[:, cols], w_ref[...])
    out_ref[...] = grad.astype(bf16)


def mixed_back(x, halves, scalars):
    rows, width = x.shape
    last = halves[0].shape[1] // BLOCK - 1
    (out,) = dense(
        mixed_back_body, (width // BLOCK,), scalars,
        [whole(x), *[(w, (BLOCK, BLOCK), lambda j, ref: (j, last)) for w in halves]],
        [((rows, width), bf16, (rows, BLOCK), lambda j, ref: (0, j))],
    )
    return out


def weight_grad_body(_, x_ref, y_ref, out_ref):
    out_ref[...] = t_dot(x_ref[...], y_ref[...]).astype(bf16).reshape(out_ref.shape)


def weight_grad(x, y, total, scalars, half=None):
    rows, count = x.shape
    cols = y.shape[1] if half is None else BLOCK
    shift = (lambda j, ref: (0, j)) if half is None else (lambda j, ref: (0, ref[0] ^ half))
    shape = (total, count // total)
    (out,) = dense(
        weight_grad_body, (cols // BLOCK,), scalars,
        [whole(x), (y, (rows, BLOCK), shift)],
        [((*shape, cols), bf16, (*shape, BLOCK), lambda j, ref: (0, 0, j))],
    )
    return out


def weight_split_body(ends, info_ref, *refs):
    send_ref, keep_ref, sum_ref = refs[-3:]
    step = pl.program_id(0)
    for p in range(len(ends) - 1):

        @pl.when((step >= ends[p]) & (step < ends[p + 1]))
        def _(x_ref=refs[3 * p], y_ref=refs[3 * p + 1], got_ref=refs[3 * p + 2]):
            grad = t_dot(x_ref[...], y_ref[...]).reshape(sum_ref.shape)
            sum_ref[...] = grad + got_ref[...].astype(f32)

    part(info_ref, sum_ref, send_ref, keep_ref)


def weight_split(parts, k, value, core):
    scalars = jnp.stack([jnp.int32(k), value.astype(jnp.int32), core.astype(jnp.int32)])
    total, r, _ = parts[0][2].shape
    widths = [got.shape[2] for _, _, got, _ in parts]
    ends = [sum(widths[:i]) // BLOCK for i in range(len(parts) + 1)]
    inputs = []
    for (x, y, got, half), low, high in zip(parts, ends[:-1], ends[1:]):
        place = lambda j, low=low, high=high: jnp.clip(j - low, 0, high - low - 1)
        if half is None:
            index = lambda j, ref, place=place: (0, place(j))
        else:
            index = lambda j, ref, half=half: (0, ref[2] ^ half)
        inputs += [
            whole(x),
            (y, (y.shape[0], BLOCK), index),
            (got, (total, r, BLOCK), lambda j, ref, place=place: (0, 0, place(j))),
        ]
    shape = (total // 2, r)
    out = ((*shape, sum(widths)), bf16, (*shape, BLOCK), lambda j, ref: (0, 0, j))
    return dense(
        partial(weight_split_body, ends), (ends[-1],), scalars, inputs, [out, out],
        [pltpu.VMEM((total, r, BLOCK), f32)],
    )


TAIL = (
    0.14760860800743103, 0.14761532843112946, 0.127163827419281, 0.09018292278051376,
    0.013407237827777863, 0.06451446563005447, -0.19429759681224823, 0.13513216376304626,
    -0.031326886266469955,
)


def gelu(inner):
    size = 1.0 + 0.37 * jnp.abs(inner)
    t = pl.reciprocal(size, approx=True)
    t = t * (2.0 - size * t)
    bell = jnp.exp2(inner * inner * -0.7213475204444817)
    series = TAIL[-1]
    for term in reversed(TAIL[:-1]):
        series = series * t + term
    tail = series * t * bell
    cdf = jnp.where(inner > 0, 1.0 - tail, tail)
    return inner * cdf, cdf + inner * bell * 0.3989422804014327


def up_body(x_ref, w_ref, bias_ref, active_ref, slope_ref):
    rows = x_ref.shape[0]
    step = min(rows, 128)
    for r in range(0, rows, step):
        inner = jnp.dot(x_ref[r : r + step], w_ref[...], preferred_element_type=f32)
        active, slope = gelu(inner + bias_ref[...])
        active_ref[r : r + step] = active.astype(active_ref.dtype)
        slope_ref[r : r + step] = slope.astype(slope_ref.dtype)


def up_project(x, weight, bias):
    rows, width = x.shape
    cols, block = weight.shape[1], 512
    out = jax.ShapeDtypeStruct((rows, cols), bf16)
    return pl.pallas_call(
        up_body,
        grid=(cols // block,),
        in_specs=[
            pl.BlockSpec((rows, width), lambda i: (0, 0)),
            pl.BlockSpec((width, block), lambda i: (0, i)),
            pl.BlockSpec((1, block), lambda i: (0, i)),
        ],
        out_specs=[pl.BlockSpec((rows, block), lambda i: (0, i))] * 2,
        out_shape=[out, out],
        compiler_params=params(
            [(x.shape, bf16, 2), ((width, block), bf16, 2), ((rows, block), bf16, 4)], 30
        ),
        cost_estimate=NO_COST,
    )(x, weight, bias)


def on_device(
    tokens,
    actions,
    sides,
    action_table,
    norm_gains,
    norm_shifts,
    s_qkv,
    s_out,
    t_qkv,
    t_out,
    w_up,
    b_up,
    w_down,
    b_down,
    grad_out,
):
    shape = tokens.shape
    frames_local, _, slots, width = shape
    place = Place()
    total, core, tm_size = place.total, place.core, place.tm_size
    slots_local = slots // tm_size
    row_count = frames_local * slots
    half = width // 2

    def to_slots(value):
        view = value.reshape(frames_local, tm_size, slots_local, value.shape[-1])
        parts = []
        for o in range(tm_size):
            part = lax.dynamic_index_in_dim(view, place.tm ^ o, 1, keepdims=False)
            parts.append(place.tm_flip(part, o) if o else part)
        return parts

    def from_slots(value, offsets=range(tm_size)):
        view = value.reshape(tm_size, frames_local, slots_local, value.shape[-1])
        return [place.tm_flip(view[o], o) if o else view[o] for o in offsets]

    def in_slots(parts):
        return jnp.concatenate(parts, axis=0)

    def in_frames(parts):
        return jnp.stack(unscramble(parts, place.tm), axis=1).reshape(frames_local, slots, -1)

    def own_and_other(value, axis):
        first, second = (lax.index_in_dim(value, i, axis, keepdims=False) for i in (0, 1))
        return jnp.where(core == 0, first, second), jnp.where(core == 0, second, first)

    def in_order(own, other, axis):
        pair = [jnp.where(core == 0, own, other), jnp.where(core == 0, other, own)]
        return jnp.stack(pair, axis=axis)

    def woven(own, other):
        cuts = [slice(i, i + half) for i in range(0, own.shape[1], half)]
        own_first = [x[:, cut] for cut in cuts for x in (own, other)]
        other_first = [x[:, cut] for cut in cuts for x in (other, own)]
        return jnp.where(
            core == 0,
            jnp.concatenate(own_first, axis=1),
            jnp.concatenate(other_first, axis=1),
        )

    thin = width // total
    counts = [ACTIONS, 3, 3, 1]
    ends = [sum(counts[:i]) for i in range(len(counts) + 1)]
    rows = s_qkv.shape[0]
    hidden_half = w_down.shape[0] // 2

    def attention_group(qkv, out):
        qkv = own_and_other(qkv.reshape(rows, 3, 2, half), 2)
        both = [
            jnp.concatenate([a.reshape(rows, 3 * half), b], axis=1)
            for a, b in zip(qkv, own_and_other(out.reshape(rows, 2, half), 1))
        ]
        return Chain(gather(place, *both))

    front = attention_group(s_qkv, s_out)
    tokens = along(tokens, front)
    rows_in = (action_table, norm_gains, norm_shifts, b_down)
    tokens, rows_in, b_up, grad_out = lax.optimization_barrier((tokens, rows_in, b_up, grad_out))
    action_table, norm_gains, norm_shifts, b_down = rows_in
    small = jnp.concatenate([action_table, norm_gains, norm_shifts, b_down[None]], axis=0).T
    small = jnp.pad(small, ((0, 0), (0, LANES - ends[-1])))
    b_up = jnp.pad(b_up[None], ((0, GROUP - 1), (0, LANES - b_up.shape[0])))
    small = jnp.concatenate([small, b_up], axis=0)
    tokens = along(tokens, front)
    tokens, grad_out = lax.optimization_barrier((tokens, grad_out))
    cotangent = to_slots(grad_out.reshape(frames_local, slots, width))
    small = Chain(gather_small(place, small))
    tokens = along(tokens, small)
    tokens = along(tokens, small)
    tokens, t_qkv, t_out = lax.optimization_barrier((tokens, t_qkv, t_out))
    tokens = along(tokens, front)
    middle = attention_group(t_qkv, t_out)
    tokens = along(tokens, middle)
    tokens, w_up = lax.optimization_barrier((tokens, w_up))
    up_pair = own_and_other(w_up.reshape(rows, total, 2, hidden_half), 2)
    rising = Chain(gather(place, *[x.reshape(rows, -1) for x in up_pair], len(place.xy) // 2))
    tokens, cotangent = lax.optimization_barrier((tokens, cotangent))
    tokens = along(tokens, front, middle, rising)
    tokens = along(tokens, small)
    tokens = along(tokens, small)
    tokens, w_down = lax.optimization_barrier((tokens, w_down))
    falling = Chain(gather(place, *own_and_other(w_down.reshape(2, hidden_half, width), 0)))
    tokens = along(tokens, front, middle, rising, falling)
    while not small.done():
        tokens = along(tokens, small)
    small = small.result.astype(f32)
    table = small[:, :thin].reshape(width, LANES).T

    def unpack(i):
        return table[ends[i] : ends[i + 1]]

    action_rows, gains, shifts, down_bias = [unpack(i) for i in range(4)]
    up_bias = small[:, thin, : 2 * hidden_half].reshape(total, 2, hidden_half)
    up_bias = [x.reshape(1, -1) for x in own_and_other(up_bias, 1)]

    onehot = (actions == jnp.arange(ACTIONS)[None, :]).astype(f32)
    embedded = jnp.dot(onehot, action_rows, precision=highest)
    tokens = tokens.reshape(frames_local, slots, width)
    embedded = embedded[:, None, :]
    normed1 = norm(tokens, embedded, gains[0], shifts[0])
    normed1 = land(normed1, front, middle, rising, falling)
    normed1 = launch(normed1, front, middle, falling)
    s_halves = [x.reshape(width, -1) for x in finish(front)]
    here = core.astype(jnp.int32).reshape(1)

    def projected(x, w, outer):
        return project(x, w, 3 * half, here).reshape(*outer, -1)

    spatial = [projected(normed1, w, (frames_local, slots)) for w in s_halves]
    spatial = land(spatial, middle, falling)
    spatial = launch(spatial, middle, rising)

    def frame_index(i):
        return (i, 0, 0)

    def slot_index(i):
        return (0, i, 0)

    spatial_place = (
        jnp.stack([sides[0], core.astype(jnp.int32)]), (1, slots), frames_local, frame_index,
    )
    (s_mixed,) = run_attention(
        partial(attention_forward, spatial_bias), *spatial_place, spatial, [width]
    )
    s_mixed = s_mixed.reshape(row_count, width)
    flat = tokens.reshape(row_count, width)
    hidden1 = add_spatial(s_mixed, s_halves, flat, embedded, here)

    hidden1 = hold(hidden1, middle, rising)
    parts = to_slots(hidden1.reshape(tokens.shape))
    parts[1] = along(parts[1], middle, rising)
    parts = land(parts, middle, rising)
    hidden1 = in_slots(parts)
    frames = hidden1.shape[0]
    slot_at = place.tm * slots_local + jnp.arange(slots_local)
    mask = (slot_at < sides[0] * sides[0])[None, :, None]
    nothing = jnp.zeros((1, 1, width), f32)
    normed2 = norm(hidden1, nothing, gains[1], shifts[1])
    hidden1 = hidden1.reshape(row_count, width)
    normed2 = launch(normed2, rising, falling)
    t_halves = [x.reshape(width, -1) for x in finish(middle)]
    temporal = [projected(normed2, w, (frames, slots_local)) for w in t_halves]
    temporal_place = (
        jnp.stack([place.tm.astype(jnp.int32), core.astype(jnp.int32)]), (frames, GROUP),
        slots_local // GROUP, slot_index,
    )
    make_bias = partial(temporal_bias, frames_local)
    (t_mixed,) = run_attention(
        partial(attention_forward, make_bias), *temporal_place, temporal, [width]
    )
    t_mixed = t_mixed.reshape(row_count, width)
    hidden2, normed3 = add_temporal(t_mixed, t_halves, hidden1, gains[2], shifts[2], here)
    normed3 = along(normed3, rising, falling)
    up_halves = [x.reshape(width, -1) for x in finish(rising)]
    first = up_project(normed3, up_halves[0], up_bias[0])
    first = along(first, falling)
    normed3, first = lax.optimization_barrier((normed3, first))
    second = up_project(normed3, up_halves[1], up_bias[1])
    (active, slope), (active2, slope2) = first, second

    core_pair = (place.core_bit, place.core_bit)

    def exchanged(grad):
        return place.flip(grad, core_pair)

    def sums(*parts):
        return Chain(scatter(place, lambda k, value: weight_split(parts, k, value, core)))

    down_in = jnp.where(mask, in_slots(cotangent), 0).reshape(row_count, width)
    send = weight_grad(active2, down_in, total, here)
    down_in, send = land((down_in, send), falling)
    (own_rows,) = up_to(falling, total.bit_length() - 1)
    own_rows = own_rows.reshape(-1, width)
    down_in, send = launch(down_in, falling, also=[send])
    got = exchanged(send)
    inner_grad, b_sum = inner_back(down_in, own_rows, slope, here)
    hidden2, inner_grad = land((hidden2, inner_grad), falling)
    down_halves = [x.reshape(-1, width) for x in finish(falling)]
    inner_grad2, b_sum2 = inner_back(down_in, down_halves[1], slope2, here)
    send = weight_grad(normed3, inner_grad2, total, here)
    down_in, hidden2, send, got = lax.optimization_barrier((down_in, hidden2, send, got))
    got_up = exchanged(send)
    s_down = sums((active, down_in, got, None))
    down_in, hidden2 = launch((down_in, hidden2), s_down)

    mask_rows = jnp.broadcast_to(mask, (frames, slots_local, 1)).reshape(row_count, 1).astype(f32)
    mixed = down_project([active, active2], down_halves, hidden2, down_bias, mask_rows, here)
    mixed, got_up = lax.optimization_barrier((mixed, got_up))
    s_up = sums((normed3, inner_grad, got_up, None))
    hidden2, s_up.pending, mixed = land((hidden2, s_up.pending, mixed), s_down)
    hidden2 = launch(hidden2, s_down, s_up)

    grad2, sums3 = norm_back(
        (inner_grad, inner_grad2), up_halves, hidden2, nothing, gains[2], down_in, bf16, here
    )
    b_sums = [x.reshape(total, -1, thin).swapaxes(0, 1) for x in (b_sum, b_sum2)]
    late_rows = [x.reshape(-1, width) for x in b_sums]
    late_rows = jnp.where(
        core == 0, jnp.concatenate(late_rows, axis=0), jnp.concatenate(late_rows[::-1], axis=0)
    )
    late_rows = jnp.concatenate([jnp.sum(down_in.astype(f32), axis=0)[None], late_rows], axis=0)
    t_mix_grad = mixed_back(grad2, t_halves, here).reshape(frames, slots_local, width)
    send2 = weight_grad(t_mixed, grad2, total, here, 1)

    def back(side, where, make, values, grad):
        (out,) = run_attention(
            partial(attention_backward, make, (side,)), *where, [values[side], grad], [3 * half]
        )
        return out.reshape(row_count, -1)

    t_grad2 = back(1, temporal_place, make_bias, temporal, t_mix_grad)
    t_mix_grad, t_grad2, late_rows = land((t_mix_grad, t_grad2, late_rows), s_down, s_up)
    t_mix_grad, t_grad2 = launch((t_mix_grad, t_grad2), s_down, s_up)
    t_grad = back(0, temporal_place, make_bias, temporal, t_mix_grad)
    send = weight_grad(normed2, t_grad2, total, here)
    t_grads, send = land(((t_grad, t_grad2), send), s_down, s_up)
    t_grads, send, send2 = launch(t_grads, s_down, also=[send, send2])
    gots = [exchanged(send), exchanged(send2)]

    grad1, sums2 = norm_back(t_grads, t_halves, hidden1, nothing, gains[1], grad2, bf16, here)
    grad1 = hold(grad1, s_down)
    grad1, gots = lax.optimization_barrier((grad1, gots))
    parts = from_slots(grad1)
    parts[1] = along(parts[1], s_down, s_up)
    s_time = sums((normed2, t_grads[0], gots[0], None), (t_mixed, grad2, gots[1], 0))
    parts[0], s_time.pending = lax.optimization_barrier((parts[0], s_time.pending))
    parts = land(parts, s_down, s_up)
    grad1 = in_frames(parts).reshape(row_count, width)
    grad1 = launch(grad1, s_down, s_up, s_time)

    send2 = weight_grad(s_mixed, grad1, total, here, 1)
    mix_grad = mixed_back(grad1, s_halves, here).reshape(frames_local, slots, width)
    s_grad2 = back(1, spatial_place, spatial_bias, spatial, mix_grad)
    send = weight_grad(normed1, s_grad2, total, here)
    mix_grad, send, send2 = land((mix_grad, send, send2), s_down, s_up, s_time)
    mix_grad, send, send2 = launch(mix_grad, s_down, s_up, s_time, also=[send, send2])
    gots = [exchanged(send), exchanged(send2)]

    s_grad = back(0, spatial_place, spatial_bias, spatial, mix_grad)
    s_grad, *gots = land(s_grad, s_down, s_up, s_time, also=gots)
    s_space = sums((normed1, s_grad, gots[0], None), (s_mixed, grad1, gots[1], 0))
    s_grads = launch((s_grad, s_grad2), s_time, s_space)

    input_grad, sums1 = norm_back(
        s_grads, s_halves, flat, embedded, gains[0], grad1, f32, here
    )
    sums1, input_grad = land((sums1, input_grad), s_time, s_space)
    sums1, input_grad = launch((sums1, input_grad), s_time, s_space)
    g_actions = jnp.sum(onehot[:, :, None] * sums1[:, 2][:, None, :], axis=0)
    all_sums = [jnp.sum(x[:, :2], axis=0) for x in (sums1, sums2, sums3)]
    both_norms = [jnp.stack([x[i] for x in all_sums]) for i in (0, 1)]
    packed = jnp.concatenate([g_actions, *both_norms, late_rows], axis=0)
    s_small = Chain(scatter_small(place, packed))
    packed = launch(packed, s_small)
    packed = land(packed, s_time, s_space, s_small)
    packed, mixed = launch((packed, mixed), s_time, s_space, s_small)
    near = from_slots(mixed, range(tm_size // 2 + 1))
    packed, down_sums, up_sums = lax.optimization_barrier((packed, finish(s_down), finish(s_up)))
    g_w_down = in_order(*down_sums, 0).reshape(w_down.shape)
    g_w_up = in_order(*[x.reshape(rows, total, -1) for x in up_sums], 2).reshape(w_up.shape)
    packed = along(packed, s_small)
    packed, *near = land(packed, s_time, s_space, s_small, also=near)
    packed, mixed = launch((packed, mixed), s_time, s_space, s_small)
    packed, g_w_down, g_w_up = lax.optimization_barrier((packed, g_w_down, g_w_up))
    far = from_slots(mixed, range(tm_size // 2 + 1, tm_size))
    packed = along(packed, s_small)
    packed, *far = land(packed, s_time, s_space, s_small, also=far)
    packed = launch(packed, s_time, s_space, s_small)
    mixed = in_frames(near + far)
    packed, mixed = lax.optimization_barrier((packed, mixed))
    while not (s_time.done() and s_space.done() and s_small.done()):
        packed = along(packed, s_time, s_space, s_small)
    summed = s_small.result
    (g_t_qkv, g_t_out), (g_s_qkv, g_s_out) = [
        [woven(*[x[:, cut] for x in c.result]) for cut in (slice(3 * half), slice(3 * half, None))]
        for c in (s_time, s_space)
    ]

    return (
        mixed.reshape(shape),
        input_grad.reshape(shape),
        summed[:8],
        summed[8:11],
        summed[11:14],
        g_s_qkv,
        g_s_out,
        g_t_qkv,
        g_t_out,
        g_w_up,
        summed[15:].reshape(-1),
        g_w_down,
        summed[14],
    )


def solution(mesh):
    whole = P(("tm", "clip"), None)
    spread = P(None, ("tm", "clip"))
    frames = P("tm", "clip", None, None)
    vector = P(("tm", "clip"))
    return jax.shard_map(
        on_device,
        mesh=mesh,
        in_specs=(
            frames, P("tm", "clip"), P("clip"), spread, spread, spread, whole, whole, whole,
            whole, whole, vector, whole, vector, frames,
        ),
        out_specs=(
            frames, frames, spread, spread, spread, whole, whole, whole, whole, whole, vector,
            whole, vector,
        ),
        check_vma=False,
    )
```

```python
import math
from functools import partial

import jax
import jax.numpy as jnp
from jax import lax
from jax.experimental import pallas as pl
from jax.experimental.pallas import tpu as pltpu
from jax.sharding import PartitionSpec as P

H = 16
E = 64
ACTIONS = 8
FRAMES = 16
AXES = ("tm", "clip")
LANES = 128
GROUP = 16

negative = -1e30
highest = lax.Precision.HIGHEST
MIB = 1024 * 1024
bf16, f32 = jnp.bfloat16, jnp.float32
NO_COST = pl.CostEstimate(flops=0, bytes_accessed=0, transcendentals=0)


def params(blocks, margin=6):
    size = sum(math.prod(shape) * jnp.dtype(dtype).itemsize * n for shape, dtype, n in blocks)
    return pltpu.CompilerParams(vmem_limit_bytes=(-(-size // MIB) + margin) * MIB)


class Place:
    def __init__(self):
        tm_size, clip_size = lax.axis_size("tm"), lax.axis_size("clip")
        self.tm_size, self.clip_size, self.total = tm_size, clip_size, tm_size * clip_size
        self.tm = lax.axis_index("tm")
        self.me = self.tm * clip_size + lax.axis_index("clip")
        self.core_bit = clip_size
        self.core = self.bit_of(clip_size)
        clip_bits = [1 << i for i in range(clip_size.bit_length() - 1)]
        tm_bits = [clip_size << i for i in range(tm_size.bit_length() - 1)]
        x, z, y = clip_bits[:-2], clip_bits[-2:], tm_bits[1:]
        self.z = [(b, b) for b in z]
        self.xy = list(zip(x + y, y + x))

    def bit_of(self, bit):
        return (self.me // bit) % 2

    def mine(self, pair):
        return jnp.where(self.core == 0, self.bit_of(pair[0]), self.bit_of(pair[1]))

    def choose(self, pair):
        return jnp.where(self.core == 0, pair[0], pair[1])

    def flip(self, value, pair):
        moves = [(i, i ^ pair[(i // self.core_bit) % 2]) for i in range(self.total)]
        return lax.ppermute(value, AXES, moves)

    def tm_flip(self, value, offset):
        moves = [(i, i ^ (offset * self.clip_size)) for i in range(self.total)]
        return lax.ppermute(value, AXES, moves)


def below(have, bit):
    return sum(1 for b in have if b < bit)


def unscramble(parts, me):
    bit = 1
    while bit < len(parts):
        swap = (me & bit) != 0
        parts = [jnp.where(swap, parts[p ^ bit], parts[p]) for p in range(len(parts))]
        bit *= 2
    return parts


def position(m, value, k):
    m = jnp.int32(m)
    high = lax.shift_left(lax.shift_right_logical(m, k), k + 1)
    return high | lax.shift_left(value, k) | (m & (lax.shift_left(jnp.int32(1), k) - 1))


def merge_body(info_ref, mine_ref, other_ref, out_ref):
    k, value = info_ref[0], info_ref[1]
    for m in range(mine_ref.shape[0]):
        out_ref[position(m, value, k)] = mine_ref[m]
        out_ref[position(m, 1 - value, k)] = other_ref[m]


def column_block(shape):
    blocks, rows, cols = shape
    return cols if blocks * rows * cols <= 512 * 1024 else min(cols, 512)


def merge(mine, other, k, value):
    m, r, n = mine.shape
    block = column_block((2 * m, r, n))
    spec = pl.BlockSpec((m, r, block), lambda j: (0, 0, j))
    return pl.pallas_call(
        merge_body,
        grid=(n // block,),
        in_specs=[pl.BlockSpec(memory_space=pltpu.SMEM), spec, spec],
        out_specs=pl.BlockSpec((2 * m, r, block), lambda j: (0, 0, j)),
        out_shape=jax.ShapeDtypeStruct((2 * m, r, n), mine.dtype),
        compiler_params=params([((4 * m, r, block), mine.dtype, 2)], 2),
        cost_estimate=NO_COST,
    )(jnp.stack([jnp.int32(k), value.astype(jnp.int32)]), mine, other)


def part(info_ref, source_ref, send_ref, keep_ref):
    k, value = info_ref[0], info_ref[1]
    for m in range(send_ref.shape[0]):
        for out_ref, at in ((send_ref, 1 - value), (keep_ref, value)):
            out_ref[m] = source_ref[position(m, at, k)].astype(out_ref.dtype)


def split_body(info_ref, a_ref, b_ref, send_ref, keep_ref):
    k, value = info_ref[0], info_ref[1]
    for m in range(send_ref.shape[0]):
        for out_ref, at in ((send_ref, 1 - value), (keep_ref, value)):
            i = position(m, at, k)
            out_ref[m] = (a_ref[i].astype(f32) + b_ref[i].astype(f32)).astype(out_ref.dtype)


def split(a, b, k, value, dtype):
    blocks, r, n = a.shape
    block = column_block(a.shape)
    out = jax.ShapeDtypeStruct((blocks // 2, r, n), dtype)
    return pl.pallas_call(
        split_body,
        grid=(n // block,),
        in_specs=[pl.BlockSpec(memory_space=pltpu.SMEM)]
        + [pl.BlockSpec((blocks, r, block), lambda j: (0, 0, j))] * 2,
        out_specs=[pl.BlockSpec((blocks // 2, r, block), lambda j: (0, 0, j))] * 2,
        out_shape=[out, out],
        compiler_params=params([((3 * blocks, r, block), dtype, 2)], 3),
        cost_estimate=NO_COST,
    )(jnp.stack([jnp.int32(k), value.astype(jnp.int32)]), a, b)


def gather_small(place, value):
    core = (place.core_bit, place.core_bit)
    x_and_y = [(b, b) for b, _ in place.xy]
    count = len(x_and_y) // 2
    blocks, have = value[None], []
    for pair in x_and_y[:count] + [core] + x_and_y[count:] + place.z:
        (send,) = yield [blocks]
        (got,) = yield [place.flip(send, pair)]
        blocks = merge(blocks, got, below(have, pair[0]), place.bit_of(pair[0]))
        have.append(pair[0])
    return blocks


def scatter_small(place, value):
    bit = place.total // 2
    while bit:
        half = value.shape[1] // 2
        low_half, high_half = value[:, :half], value[:, half:]
        mine = (place.me & bit) != 0
        (send,) = yield [jnp.where(mine, low_half, high_half)]
        (got,) = yield [place.flip(send, (bit, bit))]
        value = jnp.where(mine, high_half, low_half) + got
        bit //= 2
    return value


def gather(place, keep, send, ahead=0):
    core = (place.core_bit, place.core_bit)
    have = ([], [])
    blocks, out = keep[None], send[None]
    for pair in [core] + place.xy[:ahead] + place.z[::-1] + place.xy[ahead:]:
        (out,) = yield [out]
        (got,) = yield [place.flip(out, pair)]
        k = [below(h, b) for h, b in zip(have, pair)]
        blocks = out = merge(blocks, got, place.choose(k), place.mine(pair))
        have = (have[0] + [pair[0]], have[1] + [pair[1]])
    (out,) = yield [out]
    (got,) = yield [place.flip(out, core)]
    return blocks, got


def scatter(place, first):
    core = (place.core_bit, place.core_bit)
    bits = [1 << i for i in range(place.total.bit_length() - 1)]
    have, pairs = (bits, bits), None
    for pair in place.xy[::-1] + place.z + [core]:
        have = tuple([b for b in h if b != bit] for h, bit in zip(have, pair))
        k = place.choose([below(h, b) for h, b in zip(have, pair)])
        dtype = f32 if pair == core else bf16
        if pairs is None:
            send, keep = first(k, place.mine(pair))
        else:
            send, keep = split(*pairs, k, place.mine(pair), dtype)
        (send,) = yield [send]
        (got,) = yield [place.flip(send, pair)]
        pairs = (keep, got)
    return keep[0], got[0]


class Chain:
    def __init__(self, steps):
        self.steps, self.flying, self.result, self.started = steps, False, None, 0
        self.pending = next(steps)

    def done(self):
        return self.result is not None

    def move(self):
        try:
            self.pending = self.steps.send(self.pending)
        except StopIteration as stop:
            self.result = stop.value
        self.flying = not self.flying
        self.started += self.flying


def hold(value, *chains):
    chains = [c for c in chains if c.flying]
    value, got = lax.optimization_barrier((value, [c.pending for c in chains]))
    for c, g in zip(chains, got):
        c.pending = g
    return value


def land(value, *chains, also=()):
    chains = [c for c in chains if c.flying]
    value, got, also = lax.optimization_barrier((value, [c.pending for c in chains], list(also)))
    for c, g in zip(chains, got):
        c.pending = g
        c.move()
    return (value, *also) if also else value


def launch(value, *chains, also=()):
    chains = [c for c in chains if not c.done() and not c.flying]
    value, sent, also = lax.optimization_barrier((value, [c.pending for c in chains], list(also)))
    for c, g in zip(chains, sent):
        c.pending = g
        c.move()
    return (value, *also) if also else value


def along(value, *chains):
    return launch(land(value, *chains), *chains)


def up_to(chain, count):
    while chain.started < count or chain.flying:
        chain.move()
    return chain.pending


def finish(chain):
    while not chain.done():
        chain.move()
    return chain.result


def spatial_bias(scalar, rows, keys):
    key = lax.broadcasted_iota(jnp.int32, (1, rows) if keys == 1 else (rows, 1), keys)
    return jnp.where(key < scalar * scalar, 0.0, negative)


def temporal_bias(frames_local, scalar, rows, keys):
    def place(axis):
        index = lax.broadcasted_iota(jnp.int32, (rows, rows), axis)
        slot, at = index % GROUP, index // GROUP
        frame = ((at // frames_local) ^ scalar) * frames_local + at % frames_local
        return slot, frame

    slot_q, frame_q = place(1 - keys)
    slot_k, frame_k = place(keys)
    return jnp.where((slot_q == slot_k) & (frame_q >= frame_k), 0.0, negative)


def dot_t(a, b):
    return lax.dot_general(a, b, (((1,), (1,)), ((), ())), preferred_element_type=f32)


def t_dot(a, b):
    return lax.dot_general(a, b, (((0,), (0,)), ((), ())), preferred_element_type=f32)


def columns(scalar_ref, side, start):
    half = H * E // 2
    return pl.ds(pl.multiple_of((scalar_ref[1] ^ side) * half + start, LANES), LANES)


def two_heads(rows):
    half = lax.broadcasted_iota(jnp.int32, (rows, LANES), 1) < E

    def apart(x):
        return jnp.concatenate([jnp.where(half, x, 0), jnp.where(half, 0, x)], axis=0)

    def together(x):
        return jnp.where(half, x[:rows], x[rows:])

    return apart, together


def head_pairs(sides, refs):
    a, b, width = refs[0].shape
    rows, width = a * b, width // 3
    for i, side in enumerate(sides):
        for c in range(0, width, LANES):
            q, k, v = (
                refs[i][:, :, at : at + LANES].reshape(rows, LANES)
                for at in (c, width + c, 2 * width + c)
            )
            yield i, side, c, q * bf16(E ** (-0.5)), k, v


def in_turn(items, first, last):
    waiting = None
    for item in items:
        ready = first(*item)
        if waiting is not None:
            last(*waiting)
        waiting = ready
    last(*waiting)


def attention_forward(make_bias, scalar_ref, own_ref, other_ref, out_ref):
    a, b, width = own_ref.shape
    rows, width = a * b, width // 3
    bias = make_bias(scalar_ref[0], rows, 1)
    apart, together = two_heads(rows)

    def first(i, side, c, q, k, v):
        scores = dot_t(apart(q), k).reshape(2, rows, rows) + bias[None]
        weights = jnp.exp(scores - jnp.max(scores, axis=2, keepdims=True))
        scale = 1.0 / jnp.sum(weights, axis=2, keepdims=True)
        return side, c, v, weights.astype(bf16).reshape(2 * rows, rows), scale

    def last(side, c, v, weights, scale):
        mixed = jnp.dot(weights, v, preferred_element_type=f32) * scale.reshape(2 * rows, 1)
        mixed = together(mixed).astype(out_ref.dtype)
        out_ref[:, :, columns(scalar_ref, side, c)] = mixed.reshape(a, b, LANES)

    in_turn(head_pairs((0, 1), (own_ref, other_ref)), first, last)


def attention_backward(make_bias, sides, scalar_ref, *refs):
    grad_ref = refs[len(sides)]
    a, b, width = refs[0].shape
    rows, width = a * b, width // 3
    bias = make_bias(scalar_ref[0], rows, 0)
    apart, together = two_heads(rows)

    def first(i, side, c, q, k, v):
        g = grad_ref[:, :, columns(scalar_ref, side, c)].reshape(rows, LANES)
        scores = dot_t(apart(k), q).reshape(2, rows, rows) + bias[None]
        prob_grad = dot_t(apart(v), g).reshape(2, rows, rows)
        weights = jnp.exp(scores - jnp.max(scores, axis=1, keepdims=True))
        probs = weights * (1.0 / jnp.sum(weights, axis=1, keepdims=True))
        delta = jnp.sum(probs * prob_grad, axis=1, keepdims=True)
        return i, c, q, k, g, probs.astype(bf16), (probs * (prob_grad - delta)).astype(bf16)

    def last(i, c, q, k, g, probs, score_grad):
        turned = jnp.concatenate([score_grad[0].T, score_grad[1].T], axis=0)
        dq = jnp.dot(turned, k, preferred_element_type=f32) * E ** (-0.5)
        dk = jnp.dot(score_grad.reshape(2 * rows, rows), q, preferred_element_type=f32)
        dv = jnp.dot(probs.reshape(2 * rows, rows), g, preferred_element_type=f32)
        for index, grad in enumerate((dq, dk, dv)):
            start = index * width + c
            merged = together(grad).astype(bf16).reshape(a, b, LANES)
            refs[len(sides) + 1 + i][:, :, start : start + LANES] = merged

    in_turn(head_pairs(sides, refs), first, last)


def run_attention(body, scalars, block, grid, index, inputs, out_widths):
    a, b = block
    outer = inputs[0].shape[:2]
    return pl.pallas_call(
        body,
        grid=(grid,),
        in_specs=[pl.BlockSpec(memory_space=pltpu.SMEM)]
        + [pl.BlockSpec((a, b, x.shape[-1]), index) for x in inputs],
        out_specs=[pl.BlockSpec((a, b, width), index) for width in out_widths],
        out_shape=[jax.ShapeDtypeStruct((*outer, width), bf16) for width in out_widths],
        compiler_params=params(
            [((a, b, width), bf16, 2) for width in (*(x.shape[-1] for x in inputs), *out_widths)], 8
        ),
        cost_estimate=NO_COST,
    )(scalars, *inputs)


def centre(x):
    average = jnp.mean(x, axis=-1, keepdims=True)
    centered = x - average
    variance = jnp.mean(centered * centered, axis=-1, keepdims=True)
    scale = lax.rsqrt(variance + 1e-05)
    return centered * scale, scale


def norm_body(x_ref, added_ref, gain_ref, shift_ref, out_ref):
    unit, _ = centre(x_ref[0].astype(f32) + added_ref[0])
    out_ref[0] = (unit * gain_ref[...] + shift_ref[...]).astype(out_ref.dtype)


def by_rows(body, arrays, rows, outs):
    blocks = arrays[0].shape[0]
    specs = []
    for x in arrays:
        if x.ndim == 2:
            specs.append(pl.BlockSpec(x.shape, lambda i: (0, 0)))
        else:
            at = (lambda i: (i, 0, 0)) if x.shape[0] == blocks else (lambda i: (0, 0, 0))
            specs.append(pl.BlockSpec((1, *x.shape[1:]), at))
    return pl.pallas_call(
        body,
        grid=(blocks,),
        in_specs=specs,
        out_specs=[pl.BlockSpec((1, *shape[1:]), lambda i: (i, 0, 0)) for shape, _ in outs],
        out_shape=[jax.ShapeDtypeStruct(shape, dtype) for shape, dtype in outs],
        compiler_params=params([(x.shape[1:], f32, 4) for x in arrays]),
        cost_estimate=NO_COST,
    )(*arrays)


def norm(x, added, gain, shift):
    shape = (x.shape[0] * x.shape[1] // 256, 256, x.shape[2])
    arrays = [x.reshape(shape), added, gain[None], shift[None]]
    (out,) = by_rows(norm_body, arrays, 256, [(shape, bf16)])
    return out.reshape(-1, shape[2])


BLOCK = 512


def dense(body, grid, scalars, inputs, outs, scratch=(), margin=6):
    used = [(block, x.dtype, 1 if index is FIXED else 2) for x, block, index in inputs]
    used += [(block, dtype, 2) for _, dtype, block, _ in outs]
    used += [(x.shape, x.dtype, 1) for x in scratch]

    def spec(block, index):
        if index is FIXED:
            zeros = (0,) * len(block)
            return pl.BlockSpec(block, lambda *_: zeros, pipeline_mode=pl.Buffered(1))
        return pl.BlockSpec(block, index)

    return pl.pallas_call(
        body,
        grid_spec=pltpu.PrefetchScalarGridSpec(
            num_scalar_prefetch=1,
            grid=grid,
            in_specs=[spec(block, index) for _, block, index in inputs],
            out_specs=[pl.BlockSpec(block, index) for _, _, block, index in outs],
            scratch_shapes=list(scratch),
        ),
        out_shape=[jax.ShapeDtypeStruct(shape, dtype) for shape, dtype, _, _ in outs],
        compiler_params=params(used, margin),
        cost_estimate=NO_COST,
    )(scalars, *[x for x, _, _ in inputs])


FIXED = None


def at(*index):
    return lambda j, ref: index


def whole(x):
    return (x, x.shape, FIXED)


def rows_of(x, rows=256):
    return (x, (rows, x.shape[1]), lambda i, ref: (i, 0))


def project_body(_, x_ref, w_ref, out_ref):
    out_ref[...] = jnp.dot(x_ref[...], w_ref[...], preferred_element_type=f32).astype(bf16)


def project(x, w, cols, scalars):
    index = lambda j, ref: (0, j)
    rows = x.shape[0]
    (out,) = dense(
        project_body, (cols // BLOCK,), scalars,
        [whole(x), (w, (w.shape[0], BLOCK), index)],
        [((rows, cols), bf16, (rows, BLOCK), index)],
    )
    return out


def sides(core, own_ref, other_ref):
    for side, ref in ((core, own_ref), (1 - core, other_ref)):
        yield pl.ds(pl.multiple_of(side * BLOCK, BLOCK), BLOCK), ref


def hidden1_body(core_ref, mixed_ref, own_ref, other_ref, x_ref, added_ref, out_ref):
    for cols, w_ref in sides(core_ref[0], own_ref, other_ref):
        dot = jnp.dot(mixed_ref[...], w_ref[...], preferred_element_type=f32)
        out_ref[:, cols] = (x_ref[:, cols].astype(f32) + added_ref[0, :, cols] + dot).astype(bf16)


def out_half(w):
    return (w, (w.shape[0], BLOCK), at(0, w.shape[1] // BLOCK - 1))


def add_spatial(mixed, halves, x, added, scalars):
    rows, width = x.shape
    step = rows // added.shape[0]
    (out,) = dense(
        hidden1_body, (rows // step,), scalars,
        [rows_of(mixed, step), *[out_half(w) for w in halves], rows_of(x, step),
         (added, (1, 1, width), lambda i, ref: (i, 0, 0))],
        [((rows, width), bf16, (step, width), lambda i, ref: (i, 0))],
    )
    return out


def hidden2_body(
    core_ref, mixed_ref, own_ref, other_ref, x_ref, gain_ref, shift_ref, out_ref, norm_ref
):
    for cols, w_ref in sides(core_ref[0], own_ref, other_ref):
        dot = jnp.dot(mixed_ref[...], w_ref[...], preferred_element_type=f32)
        out_ref[:, cols] = x_ref[:, cols].astype(f32) + dot
    unit, _ = centre(out_ref[...])
    norm_ref[...] = (unit * gain_ref[...] + shift_ref[...]).astype(bf16)


def add_temporal(mixed, halves, x, gain, shift, scalars):
    rows, width = x.shape
    block = ((256, width), lambda i, ref: (i, 0))
    return dense(
        hidden2_body, (rows // 256,), scalars,
        [rows_of(mixed), *[out_half(w) for w in halves], rows_of(x), whole(gain[None]),
         whole(shift[None])],
        [((rows, width), f32, *block), ((rows, width), bf16, *block)],
    )


def hidden3_body(_, a_ref, b_ref, own_ref, other_ref, x_ref, bias_ref, mask_ref, out_ref):
    out = x_ref[...] + bias_ref[...]
    out += jnp.dot(a_ref[...], own_ref[...], preferred_element_type=f32)
    out += jnp.dot(b_ref[...], other_ref[...], preferred_element_type=f32)
    out_ref[...] = jnp.where(mask_ref[...] > 0, out, 0).astype(bf16)


def down_project(actives, halves, x, bias, mask, scalars):
    rows, width = x.shape
    (out,) = dense(
        hidden3_body, (rows // 256,), scalars,
        [*[rows_of(y) for y in actives], *[whole(w) for w in halves], rows_of(x), whole(bias),
         rows_of(mask)],
        [((rows, width), bf16, (256, width), lambda i, ref: (i, 0))], margin=40,
    )
    return out


def inner_back_body(_, x_ref, w_ref, slope_ref, out_ref, sum_ref):
    grad = dot_t(x_ref[...], w_ref[...]) * slope_ref[...].astype(f32)
    out_ref[...] = grad.astype(bf16)
    sum_ref[...] = jnp.sum(out_ref[...].astype(f32), axis=0, keepdims=True)


def inner_back(x, w, slope, scalars):
    rows, cols = slope.shape
    index = lambda j, ref: (0, j)
    return dense(
        inner_back_body, (cols // BLOCK,), scalars,
        [whole(x), (w, (BLOCK, w.shape[1]), lambda j, ref: (j, 0)), (slope, (rows, BLOCK), index)],
        [((rows, cols), bf16, (rows, BLOCK), index), ((1, cols), f32, (1, BLOCK), index)],
    )


def norm_back_body(
    _, a_ref, b_ref, own_ref, other_ref, x_ref, added_ref, gain_ref, rest_ref, out_ref, sums_ref
):
    grad = dot_t(a_ref[...], own_ref[...]) + dot_t(b_ref[...], other_ref[...])
    unit, scale = centre(x_ref[...].astype(f32) + added_ref[0])
    scaled = grad * gain_ref[...]
    first = jnp.mean(scaled, axis=-1, keepdims=True)
    second = jnp.mean(scaled * unit, axis=-1, keepdims=True)
    out = rest_ref[...].astype(f32) + scale * (scaled - first - unit * second)
    out_ref[...] = out.astype(out_ref.dtype)
    terms = (grad * unit, grad, out)
    sums_ref[0] = jnp.concatenate([jnp.sum(x, axis=0, keepdims=True) for x in terms], axis=0)


def norm_back(grads, halves, x, added, gain, rest, dtype, scalars):
    rows, width = x.shape
    step, cols = 256, grads[0].shape[1]
    added_at = (lambda i, ref: (i, 0, 0)) if added.shape[0] > 1 else at(0, 0, 0)
    return dense(
        norm_back_body, (rows // step,), scalars,
        [*[rows_of(g) for g in grads], *[(w, (w.shape[0], cols), FIXED) for w in halves],
         rows_of(x), (added, (1, 1, width), added_at), whole(gain[None]), rows_of(rest)],
        [((rows, width), dtype, (step, width), lambda i, ref: (i, 0)),
         ((rows // step, 3, width), f32, (1, 3, width), lambda i, ref: (i, 0, 0))],
        margin=42 if dtype == f32 else 30 if cols > 3 * BLOCK else 6,
    )


def mixed_back_body(core_ref, x_ref, own_ref, other_ref, out_ref):
    grad = 0
    for cols, w_ref in sides(core_ref[0], own_ref, other_ref):
        grad += dot_t(x_ref[:, cols], w_ref[...])
    out_ref[...] = grad.astype(bf16)


def mixed_back(x, halves, scalars):
    rows, width = x.shape
    last = halves[0].shape[1] // BLOCK - 1
    (out,) = dense(
        mixed_back_body, (width // BLOCK,), scalars,
        [whole(x), *[(w, (BLOCK, BLOCK), lambda j, ref: (j, last)) for w in halves]],
        [((rows, width), bf16, (rows, BLOCK), lambda j, ref: (0, j))],
    )
    return out


def weight_grad_body(_, x_ref, y_ref, out_ref):
    out_ref[...] = t_dot(x_ref[...], y_ref[...]).astype(bf16).reshape(out_ref.shape)


def weight_grad(x, y, total, scalars, half=None):
    rows, count = x.shape
    cols = y.shape[1] if half is None else BLOCK
    shift = (lambda j, ref: (0, j)) if half is None else (lambda j, ref: (0, ref[0] ^ half))
    shape = (total, count // total)
    (out,) = dense(
        weight_grad_body, (cols // BLOCK,), scalars,
        [whole(x), (y, (rows, BLOCK), shift)],
        [((*shape, cols), bf16, (*shape, BLOCK), lambda j, ref: (0, 0, j))],
    )
    return out


def weight_split_body(ends, info_ref, *refs):
    send_ref, keep_ref, sum_ref = refs[-3:]
    step = pl.program_id(0)
    for p in range(len(ends) - 1):

        @pl.when((step >= ends[p]) & (step < ends[p + 1]))
        def _(x_ref=refs[3 * p], y_ref=refs[3 * p + 1], got_ref=refs[3 * p + 2]):
            grad = t_dot(x_ref[...], y_ref[...]).reshape(sum_ref.shape)
            sum_ref[...] = grad + got_ref[...].astype(f32)

    part(info_ref, sum_ref, send_ref, keep_ref)


def weight_split(parts, k, value, core):
    scalars = jnp.stack([jnp.int32(k), value.astype(jnp.int32), core.astype(jnp.int32)])
    total, r, _ = parts[0][2].shape
    widths = [got.shape[2] for _, _, got, _ in parts]
    ends = [sum(widths[:i]) // BLOCK for i in range(len(parts) + 1)]
    inputs = []
    for (x, y, got, half), low, high in zip(parts, ends[:-1], ends[1:]):
        place = lambda j, low=low, high=high: jnp.clip(j - low, 0, high - low - 1)
        if half is None:
            index = lambda j, ref, place=place: (0, place(j))
        else:
            index = lambda j, ref, half=half: (0, ref[2] ^ half)
        inputs += [
            whole(x),
            (y, (y.shape[0], BLOCK), index),
            (got, (total, r, BLOCK), lambda j, ref, place=place: (0, 0, place(j))),
        ]
    shape = (total // 2, r)
    out = ((*shape, sum(widths)), bf16, (*shape, BLOCK), lambda j, ref: (0, 0, j))
    return dense(
        partial(weight_split_body, ends), (ends[-1],), scalars, inputs, [out, out],
        [pltpu.VMEM((total, r, BLOCK), f32)],
    )


TAIL = (
    0.14760860800743103, 0.14761532843112946, 0.127163827419281, 0.09018292278051376,
    0.013407237827777863, 0.06451446563005447, -0.19429759681224823, 0.13513216376304626,
    -0.031326886266469955,
)


def gelu(inner):
    size = 1.0 + 0.37 * jnp.abs(inner)
    t = pl.reciprocal(size, approx=True)
    t = t * (2.0 - size * t)
    bell = jnp.exp2(inner * inner * -0.7213475204444817)
    series = TAIL[-1]
    for term in reversed(TAIL[:-1]):
        series = series * t + term
    tail = series * t * bell
    cdf = jnp.where(inner > 0, 1.0 - tail, tail)
    return inner * cdf, cdf + inner * bell * 0.3989422804014327


def up_body(x_ref, w_ref, bias_ref, active_ref, slope_ref):
    rows = x_ref.shape[0]
    step = min(rows, 128)
    for r in range(0, rows, step):
        inner = jnp.dot(x_ref[r : r + step], w_ref[...], preferred_element_type=f32)
        active, slope = gelu(inner + bias_ref[...])
        active_ref[r : r + step] = active.astype(active_ref.dtype)
        slope_ref[r : r + step] = slope.astype(slope_ref.dtype)


def up_project(x, weight, bias):
    rows, width = x.shape
    cols, block = weight.shape[1], 512
    out = jax.ShapeDtypeStruct((rows, cols), bf16)
    return pl.pallas_call(
        up_body,
        grid=(cols // block,),
        in_specs=[
            pl.BlockSpec((rows, width), lambda i: (0, 0)),
            pl.BlockSpec((width, block), lambda i: (0, i)),
            pl.BlockSpec((1, block), lambda i: (0, i)),
        ],
        out_specs=[pl.BlockSpec((rows, block), lambda i: (0, i))] * 2,
        out_shape=[out, out],
        compiler_params=params(
            [(x.shape, bf16, 2), ((width, block), bf16, 2), ((rows, block), bf16, 4)], 30
        ),
        cost_estimate=NO_COST,
    )(x, weight, bias)


def on_device(
    tokens,
    actions,
    sides,
    action_table,
    norm_gains,
    norm_shifts,
    s_qkv,
    s_out,
    t_qkv,
    t_out,
    w_up,
    b_up,
    w_down,
    b_down,
    grad_out,
):
    shape = tokens.shape
    frames_local, _, slots, width = shape
    place = Place()
    total, core, tm_size = place.total, place.core, place.tm_size
    slots_local = slots // tm_size
    row_count = frames_local * slots
    half = width // 2

    def to_slots(value):
        view = value.reshape(frames_local, tm_size, slots_local, value.shape[-1])
        parts = []
        for o in range(tm_size):
            part = lax.dynamic_index_in_dim(view, place.tm ^ o, 1, keepdims=False)
            parts.append(place.tm_flip(part, o) if o else part)
        return parts

    def from_slots(value, offsets=range(tm_size)):
        view = value.reshape(tm_size, frames_local, slots_local, value.shape[-1])
        return [place.tm_flip(view[o], o) if o else view[o] for o in offsets]

    def in_slots(parts):
        return jnp.concatenate(parts, axis=0)

    def in_frames(parts):
        return jnp.stack(unscramble(parts, place.tm), axis=1).reshape(frames_local, slots, -1)

    def own_and_other(value, axis):
        first, second = (lax.index_in_dim(value, i, axis, keepdims=False) for i in (0, 1))
        return jnp.where(core == 0, first, second), jnp.where(core == 0, second, first)

    def in_order(own, other, axis):
        pair = [jnp.where(core == 0, own, other), jnp.where(core == 0, other, own)]
        return jnp.stack(pair, axis=axis)

    def woven(own, other):
        cuts = [slice(i, i + half) for i in range(0, own.shape[1], half)]
        own_first = [x[:, cut] for cut in cuts for x in (own, other)]
        other_first = [x[:, cut] for cut in cuts for x in (other, own)]
        return jnp.where(
            core == 0,
            jnp.concatenate(own_first, axis=1),
            jnp.concatenate(other_first, axis=1),
        )

    thin = width // total
    counts = [ACTIONS, 3, 3, 1]
    ends = [sum(counts[:i]) for i in range(len(counts) + 1)]
    rows = s_qkv.shape[0]
    hidden_half = w_down.shape[0] // 2

    def attention_group(qkv, out):
        qkv = own_and_other(qkv.reshape(rows, 3, 2, half), 2)
        both = [
            jnp.concatenate([a.reshape(rows, 3 * half), b], axis=1)
            for a, b in zip(qkv, own_and_other(out.reshape(rows, 2, half), 1))
        ]
        return Chain(gather(place, *both))

    front = attention_group(s_qkv, s_out)
    tokens = along(tokens, front)
    rows_in = (action_table, norm_gains, norm_shifts, b_down)
    tokens, rows_in, b_up, grad_out = lax.optimization_barrier((tokens, rows_in, b_up, grad_out))
    action_table, norm_gains, norm_shifts, b_down = rows_in
    small = jnp.concatenate([action_table, norm_gains, norm_shifts, b_down[None]], axis=0).T
    small = jnp.pad(small, ((0, 0), (0, LANES - ends[-1])))
    b_up = jnp.pad(b_up[None], ((0, GROUP - 1), (0, LANES - b_up.shape[0])))
    small = jnp.concatenate([small, b_up], axis=0)
    tokens = along(tokens, front)
    tokens, grad_out = lax.optimization_barrier((tokens, grad_out))
    cotangent = to_slots(grad_out.reshape(frames_local, slots, width))
    small = Chain(gather_small(place, small))
    tokens = along(tokens, small)
    tokens = along(tokens, small)
    tokens, t_qkv, t_out = lax.optimization_barrier((tokens, t_qkv, t_out))
    tokens = along(tokens, front)
    middle = attention_group(t_qkv, t_out)
    tokens = along(tokens, middle)
    tokens, w_up = lax.optimization_barrier((tokens, w_up))
    up_pair = own_and_other(w_up.reshape(rows, total, 2, hidden_half), 2)
    rising = Chain(gather(place, *[x.reshape(rows, -1) for x in up_pair], len(place.xy) // 2))
    tokens, cotangent = lax.optimization_barrier((tokens, cotangent))
    tokens = along(tokens, front, middle, rising)
    tokens = along(tokens, small)
    tokens = along(tokens, small)
    tokens, w_down = lax.optimization_barrier((tokens, w_down))
    falling = Chain(gather(place, *own_and_other(w_down.reshape(2, hidden_half, width), 0)))
    tokens = along(tokens, front, middle, rising, falling)
    while not small.done():
        tokens = along(tokens, small)
    small = small.result.astype(f32)
    table = small[:, :thin].reshape(width, LANES).T

    def unpack(i):
        return table[ends[i] : ends[i + 1]]

    action_rows, gains, shifts, down_bias = [unpack(i) for i in range(4)]
    up_bias = small[:, thin, : 2 * hidden_half].reshape(total, 2, hidden_half)
    up_bias = [x.reshape(1, -1) for x in own_and_other(up_bias, 1)]

    onehot = (actions == jnp.arange(ACTIONS)[None, :]).astype(f32)
    embedded = jnp.dot(onehot, action_rows, precision=highest)
    tokens = tokens.reshape(frames_local, slots, width)
    embedded = embedded[:, None, :]
    normed1 = norm(tokens, embedded, gains[0], shifts[0])
    normed1 = land(normed1, front, middle, rising, falling)
    normed1 = launch(normed1, front, middle, falling)
    s_halves = [x.reshape(width, -1) for x in finish(front)]
    here = core.astype(jnp.int32).reshape(1)

    def projected(x, w, outer):
        return project(x, w, 3 * half, here).reshape(*outer, -1)

    spatial = [projected(normed1, w, (frames_local, slots)) for w in s_halves]
    spatial = land(spatial, middle, falling)
    spatial = launch(spatial, middle, rising)

    def frame_index(i):
        return (i, 0, 0)

    def slot_index(i):
        return (0, i, 0)

    spatial_place = (
        jnp.stack([sides[0], core.astype(jnp.int32)]), (1, slots), frames_local, frame_index,
    )
    (s_mixed,) = run_attention(
        partial(attention_forward, spatial_bias), *spatial_place, spatial, [width]
    )
    s_mixed = s_mixed.reshape(row_count, width)
    flat = tokens.reshape(row_count, width)
    hidden1 = add_spatial(s_mixed, s_halves, flat, embedded, here)

    hidden1 = hold(hidden1, middle, rising)
    parts = to_slots(hidden1.reshape(tokens.shape))
    parts[1] = along(parts[1], middle, rising)
    parts = land(parts, middle, rising)
    hidden1 = in_slots(parts)
    frames = hidden1.shape[0]
    slot_at = place.tm * slots_local + jnp.arange(slots_local)
    mask = (slot_at < sides[0] * sides[0])[None, :, None]
    nothing = jnp.zeros((1, 1, width), f32)
    normed2 = norm(hidden1, nothing, gains[1], shifts[1])
    hidden1 = hidden1.reshape(row_count, width)
    normed2 = launch(normed2, rising, falling)
    t_halves = [x.reshape(width, -1) for x in finish(middle)]
    temporal = [projected(normed2, w, (frames, slots_local)) for w in t_halves]
    temporal_place = (
        jnp.stack([place.tm.astype(jnp.int32), core.astype(jnp.int32)]), (frames, GROUP),
        slots_local // GROUP, slot_index,
    )
    make_bias = partial(temporal_bias, frames_local)
    (t_mixed,) = run_attention(
        partial(attention_forward, make_bias), *temporal_place, temporal, [width]
    )
    t_mixed = t_mixed.reshape(row_count, width)
    hidden2, normed3 = add_temporal(t_mixed, t_halves, hidden1, gains[2], shifts[2], here)
    normed3 = along(normed3, rising, falling)
    up_halves = [x.reshape(width, -1) for x in finish(rising)]
    first = up_project(normed3, up_halves[0], up_bias[0])
    first = along(first, falling)
    normed3, first = lax.optimization_barrier((normed3, first))
    second = up_project(normed3, up_halves[1], up_bias[1])
    (active, slope), (active2, slope2) = first, second

    core_pair = (place.core_bit, place.core_bit)

    def exchanged(grad):
        return place.flip(grad, core_pair)

    def sums(*parts):
        return Chain(scatter(place, lambda k, value: weight_split(parts, k, value, core)))

    down_in = jnp.where(mask, in_slots(cotangent), 0).reshape(row_count, width)
    send = weight_grad(active2, down_in, total, here)
    down_in, send = land((down_in, send), falling)
    (own_rows,) = up_to(falling, total.bit_length() - 1)
    own_rows = own_rows.reshape(-1, width)
    down_in, send = launch(down_in, falling, also=[send])
    got = exchanged(send)
    inner_grad, b_sum = inner_back(down_in, own_rows, slope, here)
    hidden2, inner_grad = land((hidden2, inner_grad), falling)
    down_halves = [x.reshape(-1, width) for x in finish(falling)]
    inner_grad2, b_sum2 = inner_back(down_in, down_halves[1], slope2, here)
    send = weight_grad(normed3, inner_grad2, total, here)
    down_in, hidden2, send, got = lax.optimization_barrier((down_in, hidden2, send, got))
    got_up = exchanged(send)
    s_down = sums((active, down_in, got, None))
    down_in, hidden2 = launch((down_in, hidden2), s_down)

    mask_rows = jnp.broadcast_to(mask, (frames, slots_local, 1)).reshape(row_count, 1).astype(f32)
    mixed = down_project([active, active2], down_halves, hidden2, down_bias, mask_rows, here)
    mixed, got_up = lax.optimization_barrier((mixed, got_up))
    s_up = sums((normed3, inner_grad, got_up, None))
    hidden2, s_up.pending, mixed = land((hidden2, s_up.pending, mixed), s_down)
    hidden2 = launch(hidden2, s_down, s_up)

    grad2, sums3 = norm_back(
        (inner_grad, inner_grad2), up_halves, hidden2, nothing, gains[2], down_in, bf16, here
    )
    b_sums = [x.reshape(total, -1, thin).swapaxes(0, 1) for x in (b_sum, b_sum2)]
    late_rows = [x.reshape(-1, width) for x in b_sums]
    late_rows = jnp.where(
        core == 0, jnp.concatenate(late_rows, axis=0), jnp.concatenate(late_rows[::-1], axis=0)
    )
    late_rows = jnp.concatenate([jnp.sum(down_in.astype(f32), axis=0)[None], late_rows], axis=0)
    t_mix_grad = mixed_back(grad2, t_halves, here).reshape(frames, slots_local, width)
    send2 = weight_grad(t_mixed, grad2, total, here, 1)

    def back(side, where, make, values, grad):
        (out,) = run_attention(
            partial(attention_backward, make, (side,)), *where, [values[side], grad], [3 * half]
        )
        return out.reshape(row_count, -1)

    t_grad2 = back(1, temporal_place, make_bias, temporal, t_mix_grad)
    t_mix_grad, t_grad2, late_rows = land((t_mix_grad, t_grad2, late_rows), s_down, s_up)
    t_mix_grad, t_grad2 = launch((t_mix_grad, t_grad2), s_down, s_up)
    t_grad = back(0, temporal_place, make_bias, temporal, t_mix_grad)
    send = weight_grad(normed2, t_grad2, total, here)
    t_grads, send = land(((t_grad, t_grad2), send), s_down, s_up)
    t_grads, send, send2 = launch(t_grads, s_down, also=[send, send2])
    gots = [exchanged(send), exchanged(send2)]

    grad1, sums2 = norm_back(t_grads, t_halves, hidden1, nothing, gains[1], grad2, bf16, here)
    grad1 = hold(grad1, s_down)
    grad1, gots = lax.optimization_barrier((grad1, gots))
    parts = from_slots(grad1)
    parts[1] = along(parts[1], s_down, s_up)
    s_time = sums((normed2, t_grads[0], gots[0], None), (t_mixed, grad2, gots[1], 0))
    parts[0], s_time.pending = lax.optimization_barrier((parts[0], s_time.pending))
    parts = land(parts, s_down, s_up)
    grad1 = in_frames(parts).reshape(row_count, width)
    grad1 = launch(grad1, s_down, s_up, s_time)

    send2 = weight_grad(s_mixed, grad1, total, here, 1)
    mix_grad = mixed_back(grad1, s_halves, here).reshape(frames_local, slots, width)
    s_grad2 = back(1, spatial_place, spatial_bias, spatial, mix_grad)
    send = weight_grad(normed1, s_grad2, total, here)
    mix_grad, send, send2 = land((mix_grad, send, send2), s_down, s_up, s_time)
    mix_grad, send, send2 = launch(mix_grad, s_down, s_up, s_time, also=[send, send2])
    gots = [exchanged(send), exchanged(send2)]

    s_grad = back(0, spatial_place, spatial_bias, spatial, mix_grad)
    s_grad, *gots = land(s_grad, s_down, s_up, s_time, also=gots)
    s_space = sums((normed1, s_grad, gots[0], None), (s_mixed, grad1, gots[1], 0))
    s_grads = launch((s_grad, s_grad2), s_time, s_space)

    input_grad, sums1 = norm_back(
        s_grads, s_halves, flat, embedded, gains[0], grad1, f32, here
    )
    sums1, input_grad = land((sums1, input_grad), s_time, s_space)
    sums1, input_grad = launch((sums1, input_grad), s_time, s_space)
    g_actions = jnp.sum(onehot[:, :, None] * sums1[:, 2][:, None, :], axis=0)
    all_sums = [jnp.sum(x[:, :2], axis=0) for x in (sums1, sums2, sums3)]
    both_norms = [jnp.stack([x[i] for x in all_sums]) for i in (0, 1)]
    packed = jnp.concatenate([g_actions, *both_norms, late_rows], axis=0)
    s_small = Chain(scatter_small(place, packed))
    packed = launch(packed, s_small)
    packed = land(packed, s_time, s_space, s_small)
    packed, mixed = launch((packed, mixed), s_time, s_space, s_small)
    near = from_slots(mixed, range(tm_size // 2 + 1))
    packed, down_sums, up_sums = lax.optimization_barrier((packed, finish(s_down), finish(s_up)))
    g_w_down = in_order(*down_sums, 0).reshape(w_down.shape)
    g_w_up = in_order(*[x.reshape(rows, total, -1) for x in up_sums], 2).reshape(w_up.shape)
    packed = along(packed, s_small)
    packed, *near = land(packed, s_time, s_space, s_small, also=near)
    packed, mixed = launch((packed, mixed), s_time, s_space, s_small)
    packed, g_w_down, g_w_up = lax.optimization_barrier((packed, g_w_down, g_w_up))
    far = from_slots(mixed, range(tm_size // 2 + 1, tm_size))
    packed = along(packed, s_small)
    packed, *far = land(packed, s_time, s_space, s_small, also=far)
    packed = launch(packed, s_time, s_space, s_small)
    mixed = in_frames(near + far)
    packed, mixed = lax.optimization_barrier((packed, mixed))
    while not (s_time.done() and s_space.done() and s_small.done()):
        packed = along(packed, s_time, s_space, s_small)
    summed = s_small.result
    (g_t_qkv, g_t_out), (g_s_qkv, g_s_out) = [
        [woven(*[x[:, cut] for x in c.result]) for cut in (slice(3 * half), slice(3 * half, None))]
        for c in (s_time, s_space)
    ]

    return (
        mixed.reshape(shape),
        input_grad.reshape(shape),
        summed[:8],
        summed[8:11],
        summed[11:14],
        g_s_qkv,
        g_s_out,
        g_t_qkv,
        g_t_out,
        g_w_up,
        summed[15:].reshape(-1),
        g_w_down,
        summed[14],
    )


def solution(mesh):
    whole = P(("tm", "clip"), None)
    spread = P(None, ("tm", "clip"))
    frames = P("tm", "clip", None, None)
    vector = P(("tm", "clip"))
    return jax.shard_map(
        on_device,
        mesh=mesh,
        in_specs=(
            frames, P("tm", "clip"), P("clip"), spread, spread, spread, whole, whole, whole,
            whole, whole, vector, whole, vector, frames,
        ),
        out_specs=(
            frames, frames, spread, spread, spread, whole, whole, whole, whole, whole, vector,
            whole, vector,
        ),
        check_vma=False,
    )
```
